128 devices in a mesh: section: 2 (over core), dp: 64 (over y, z, x).
Axes of the slice: x: 4, y: 4, z: 4, core: 2. Of those that a mesh axis runs over, the one named last changes fastest.
Arguments:
- tokens: bfloat16 [128, 112, 768], P('dp'), may hold values from -6 to 6
- frames: int32 [128], P('dp'), may hold values from 8 to 16, as said below
- visible: int32 [128, 14], P('dp'), may hold values from 0 to 143, as said below
- out_grad: bfloat16 [128, 1152, 384], P('dp'), may hold values from -6 to 6
- enc_vectors: bfloat16 [8, 768], replicated, may hold values from -3 to 3
- enc_qkv: bfloat16 [768, 2304], replicated, may hold values from -0.21875 to 0.21875
- enc_out: bfloat16 [768, 768], replicated, may hold values from -2.5 to 2.5
- enc_up: bfloat16 [768, 3072], replicated, may hold values from -0.21875 to 0.21875
- enc_up_bias: bfloat16 [3072], replicated, may hold values from -3 to 3
- enc_down: bfloat16 [3072, 768], replicated, may hold values from -0.109375 to 0.109375
- proj_weight: bfloat16 [768, 384], replicated, may hold values from -0.21875 to 0.21875
- dec_vectors: bfloat16 [9, 384], replicated, may hold values from -3 to 3
- dec_qkv: bfloat16 [384, 1152], replicated, may hold values from -0.3125 to 0.3125
- dec_out: bfloat16 [384, 384], replicated, may hold values from -6 to 6
- dec_up: bfloat16 [384, 1536], replicated, may hold values from -0.3125 to 0.3125
- dec_up_bias: bfloat16 [1536], replicated, may hold values from -3 to 3
- dec_down: bfloat16 [1536, 384], replicated, may hold values from -0.15625 to 0.15625
- time_pos: bfloat16 [8, 384], replicated, may hold values from -3 to 3
- space_pos: bfloat16 [144, 384], replicated, may hold values from -3 to 3
Outputs:
- decoded: bfloat16 [128, 1152, 384], P('dp', None, 'section')
- token_grad: bfloat16 [128, 112, 768], P('dp', None, 'section')
- grad_enc_vectors: float32 [8, 768], P(None, 'section')
- grad_enc_qkv: float32 [768, 2304], P(None, 'section')
- grad_enc_out: float32 [768, 768], P(None, 'section')
- grad_enc_up: float32 [768, 3072], P(None, 'section')
- grad_enc_up_bias: float32 [3072], P('section')
- grad_enc_down: float32 [3072, 768], P(None, 'section')
- grad_proj_weight: float32 [768, 384], P(None, 'section')
- grad_dec_vectors: float32 [9, 384], P(None, 'section')
- grad_dec_qkv: float32 [384, 1152], P(None, 'section')
- grad_dec_out: float32 [384, 384], P(None, 'section')
- grad_dec_up: float32 [384, 1536], P(None, 'section')
- grad_dec_up_bias: float32 [1536], P('section')
- grad_dec_down: float32 [1536, 384], P(None, 'section')
- grad_time_pos: float32 [8, 384], P(None, 'section')
- grad_space_pos: float32 [144, 384], P(None, 'section')
- grad_norms: float32 [2], P('section')
The draws below stay inside these ranges and needn't reach their ends.
Inputs may be any that keep to these rules, and one draw needn't show every extreme that they name: `frames`: each entry is 8 or 16; at least one clip has 16. `visible`: the 14 entries of a row are distinct.
All inputs are finite; a program needn't handle non-finite values.
Results may differ from the reference program's by a relative error of at most 0.017.
Values may be sent and summed in bfloat16 or wider, within the bound.
No kernel may reach another device: no remote copies, remote signals or barrier semaphores. Data moves between devices by JAX's collectives and lax.ppermute only.
A program may use at most 384 MiB of HBM per device.

```python
import jax
import jax.numpy as jnp
from jax import lax

D_ENC = 768
HEADS_ENC = 12
FF_ENC = 3072
D_DEC = 384
HEADS_DEC = 6
FF_DEC = 1536
SLOTS = 8
PATCHES = 144
VIS = 14
CLIPS = 128
LCAP = 1152
VCAP = 112


def shape_rows(noise, gain_mask, scales):
    return jnp.where(gain_mask[:, None], 1.0 + 0.2 * noise, scales[:, None] * noise)


def draw_frames(key, part):
    key = jax.random.fold_in(key, 1)
    pick = jax.random.randint(key, (CLIPS,), 0, 4)
    pick = pick.at[0].set(0)
    return jnp.where(pick == 0, 2 * SLOTS, SLOTS).astype(jnp.int32)


def draw_visible(key, part):
    key = jax.random.fold_in(key, 2)
    scores = jax.random.randint(key, (CLIPS, PATCHES), 0, 2 ** 20) * PATCHES + jnp.arange(PATCHES, dtype=jnp.int32)[None, :]
    return jnp.argsort(scores, axis=1)[:, :VIS].astype(jnp.int32)


def draw_enc_vectors(key, part):
    key = jax.random.fold_in(key, 3)
    noise = jnp.clip(jax.random.normal(key, (8, D_ENC), jnp.float32), -3.0, 3.0)
    gain_mask = jnp.array([True, False, False, False, False, True, False, False])
    scales = jnp.array([0.0, 0.4, 0.4, 0.4, 0.4, 0.0, 0.4, 0.4], jnp.float32)
    return shape_rows(noise, gain_mask, scales).astype(jnp.bfloat16)


def draw_dec_vectors(key, part):
    key = jax.random.fold_in(key, 4)
    noise = jnp.clip(jax.random.normal(key, (9, D_DEC), jnp.float32), -3.0, 3.0)
    gain_mask = jnp.array([True, False, False, False, False, True, False, False, False])
    scales = jnp.array([0.0, 0.4, 0.4, 0.4, 0.4, 0.0, 0.4, 0.4, 1.0], jnp.float32)
    return shape_rows(noise, gain_mask, scales).astype(jnp.bfloat16)


def steps_of(stream_key, extent, shards, least, largest):
    loudness, own = 1.0, jax.random.fold_in(stream_key, 6)
    for position, blocks in shards:
        heights = jnp.exp(jax.random.uniform(jax.random.fold_in(own, position), (blocks,), jnp.float32, least / len(shards), largest / len(shards)))
        loudness = loudness * jnp.repeat(heights, extent[position] // blocks).reshape([-1 if axis == position else 1 for axis in range(len(extent))])
    return loudness


def bell_draw(key, shape, scale, reach, pieces=(), kind=jnp.bfloat16):
    entries = scale * jax.random.normal(key, shape, jnp.float32)
    if pieces:
        entries = entries * steps_of(key, shape, pieces, -0.22, 0.18)
    return jnp.clip(entries, -reach, reach).astype(kind)


def setup_inputs(seed: int = 0) -> dict:
    splits = jax.random.split(jax.random.key(seed), 20)
    tokens = bell_draw(splits[0], (CLIPS, VCAP, D_ENC), 1.0, 6.0, ((0, 64),))
    frames = draw_frames(jax.random.fold_in(splits[19], 71), 0)
    visible = draw_visible(jax.random.fold_in(splits[19], 71), 0)
    out_grad = bell_draw(splits[3], (CLIPS, LCAP, D_DEC), 1.0, 6.0, ((0, 64),))
    enc_vectors = draw_enc_vectors(jax.random.fold_in(splits[19], 71), 0)
    enc_qkv = bell_draw(splits[5], (D_ENC, 3 * D_ENC), D_ENC ** -0.5, 0.21875)
    enc_out = bell_draw(splits[6], (D_ENC, D_ENC), (max(1, D_ENC // VCAP)) ** -0.5, 2.5)
    enc_up = bell_draw(splits[7], (D_ENC, FF_ENC), D_ENC ** -0.5, 0.21875)
    enc_up_bias = bell_draw(splits[8], (FF_ENC,), 0.5, 3.0)
    enc_down = bell_draw(splits[9], (FF_ENC, D_ENC), FF_ENC ** -0.5, 0.109375)
    proj_weight = bell_draw(splits[10], (D_ENC, D_DEC), D_ENC ** -0.5, 0.21875)
    dec_vectors = draw_dec_vectors(jax.random.fold_in(splits[19], 71), 0)
    dec_qkv = bell_draw(splits[12], (D_DEC, 3 * D_DEC), D_DEC ** -0.5, 0.3125)
    dec_out = bell_draw(splits[13], (D_DEC, D_DEC), (max(1, D_DEC // LCAP)) ** -0.5, 6.0)
    dec_up = bell_draw(splits[14], (D_DEC, FF_DEC), D_DEC ** -0.5, 0.3125)
    dec_up_bias = bell_draw(splits[15], (FF_DEC,), 0.5, 3.0)
    dec_down = bell_draw(splits[16], (FF_DEC, D_DEC), FF_DEC ** -0.5, 0.15625)
    time_pos = bell_draw(splits[17], (SLOTS, D_DEC), 0.5, 3.0)
    space_pos = bell_draw(splits[18], (PATCHES, D_DEC), 0.5, 3.0)
    return {"tokens": tokens, "frames": frames, "visible": visible, "out_grad": out_grad, "enc_vectors": enc_vectors, "enc_qkv": enc_qkv, "enc_out": enc_out, "enc_up": enc_up, "enc_up_bias": enc_up_bias, "enc_down": enc_down, "proj_weight": proj_weight, "dec_vectors": dec_vectors, "dec_qkv": dec_qkv, "dec_out": dec_out, "dec_up": dec_up, "dec_up_bias": dec_up_bias, "dec_down": dec_down, "time_pos": time_pos, "space_pos": space_pos}


@jax.custom_vjp
def low(v):
    return lax.optimization_barrier(v.astype(jnp.bfloat16)).astype(jnp.float32)

@jax.custom_vjp
def low_back(v):
    return v

def low_keep(v):
    return (low(v), None)

def low_pass(kept, grad):
    return (grad,)

def back_keep(v):
    return (v, None)

def back_low(kept, grad):
    return (low(grad),)
low.defvjp(low_keep, low_pass)
low_back.defvjp(back_keep, back_low)
EPSILON = 1e-06
NEGATIVE = -1000000000.0

def layer_norm(value, gain, shift):
    center = value - lax.optimization_barrier(jnp.mean(value, axis=-1, keepdims=True))
    spread = lax.optimization_barrier(jnp.mean(center * center, axis=-1, keepdims=True))
    return center * lax.rsqrt(spread + EPSILON) * gain + shift

def highest(left, right):
    return jnp.dot(left, right, precision=lax.Precision.HIGHEST)

def both_ways(value):
    return low_back(low(value))

def block(inputs, weights, heads, key_valid):
    vectors, qkv_weight, out_weight, up_weight, up_bias, down_weight = weights
    count, width = inputs.shape
    size = width // heads
    scale = size ** (-0.5)
    normed = low(layer_norm(inputs, vectors[0], vectors[1]))
    joined = highest(normed, qkv_weight)
    queries = both_ways(joined[:, :width] + vectors[2]).reshape(count, heads, size)
    keys = both_ways(joined[:, width:2 * width]).reshape(count, heads, size)
    values = both_ways(joined[:, 2 * width:] + vectors[3]).reshape(count, heads, size)
    scores = jnp.einsum('qhd,khd->hqk', queries, keys, precision=lax.Precision.HIGHEST) * scale
    scores = low_back(jnp.where(key_valid[None, None, :], scores, NEGATIVE))
    probs = low(jax.nn.softmax(scores, axis=-1))
    mixed = jnp.einsum('hqk,khd->qhd', probs, values, precision=lax.Precision.HIGHEST)
    mixed = both_ways(mixed.reshape(count, width))
    middle = inputs + low_back(highest(mixed, out_weight) + vectors[4])
    normed_two = low(layer_norm(middle, vectors[5], vectors[6]))
    hidden = low_back(highest(normed_two, up_weight) + up_bias)
    activated = low(jax.nn.gelu(hidden, approximate=False))
    return middle + low_back(highest(activated, down_weight) + vectors[7])

def gather_plan(visible_row, slot_count, patch_count):
    seen_count = visible_row.shape[0]
    patch = jnp.arange(patch_count, dtype=jnp.int32)
    match = visible_row[None, :] == patch[:, None]
    seen = jnp.any(match, axis=1)
    rank = lax.optimization_barrier(jnp.sum(jnp.where(match, jnp.arange(seen_count, dtype=jnp.int32)[None, :], 0), axis=1)).astype(jnp.int32)
    slot = jnp.arange(slot_count, dtype=jnp.int32)
    source = (slot[:, None] * seen_count + rank[None, :]).reshape(-1).astype(jnp.int32)
    seen_row = jnp.broadcast_to(seen[None, :], (slot_count, patch_count)).reshape(-1)
    return (source, seen_row)

def slot_table(slots_used, slot_count):
    slot = jnp.arange(slot_count, dtype=jnp.int32)
    divisor = slots_used - 1
    numerator = slot * (slot_count - 1)
    lower = numerator // divisor
    fraction = (numerator - lower * divisor).astype(jnp.float32) / divisor.astype(jnp.float32)
    upper = jnp.minimum(lower + 1, slot_count - 1)
    column = slot[None, :]
    first = (column == lower[:, None]).astype(jnp.float32)
    second = (column == upper[:, None]).astype(jnp.float32)
    return (1.0 - fraction)[:, None] * first + fraction[:, None] * second

def clip_forward(clip_tokens, enc_weights, dec_weights, slots_used, visible_row):
    proj_weight, dec_vectors, dec_qkv, dec_out, dec_up, dec_up_bias, dec_down, time_pos, space_pos = dec_weights
    seen_count = visible_row.shape[0]
    vis_cap = clip_tokens.shape[0]
    slot_count, width = time_pos.shape
    patch_count = space_pos.shape[0]
    enc_valid = jnp.arange(vis_cap) < slots_used * seen_count
    encoded = block(clip_tokens, enc_weights, HEADS_ENC, enc_valid)
    sent = low(low_back(encoded))
    projected = low_back(highest(sent, proj_weight))
    source, seen_row = gather_plan(visible_row, slot_count, patch_count)
    base = jnp.where(seen_row[:, None], jnp.take(projected, source, axis=0), dec_vectors[8])
    slot_pos = highest(slot_table(slots_used, slot_count), time_pos)
    start = base.reshape(slot_count, patch_count, width) + slot_pos[:, None, :] + space_pos[None]
    start = start.reshape(slot_count * patch_count, width)
    row_valid = jnp.arange(start.shape[0]) < slots_used * patch_count
    dec_block = (dec_vectors[:8], dec_qkv, dec_out, dec_up, dec_up_bias, dec_down)
    output = block(start, dec_block, HEADS_DEC, row_valid)
    return jnp.where(row_valid[:, None], output, 0.0)

def reference(tokens, frames, visible, out_grad, enc_vectors, enc_qkv, enc_out, enc_up, enc_up_bias, enc_down, proj_weight, dec_vectors, dec_qkv, dec_out, dec_up, dec_up_bias, dec_down, time_pos, space_pos):
    enc_weights = tuple((item.astype(jnp.float32) for item in (enc_vectors, enc_qkv, enc_out, enc_up, enc_up_bias, enc_down)))
    dec_weights = tuple((item.astype(jnp.float32) for item in (proj_weight, dec_vectors, dec_qkv, dec_out, dec_up, dec_up_bias, dec_down, time_pos, space_pos)))

    def one_clip(carry, item):
        clip_tokens, frame, visible_row, cotangent = item
        used = frame // 2

        def forward(inputs, enc_params, dec_params):
            return clip_forward(inputs, enc_params, dec_params, used, visible_row)
        decoded, pull = jax.vjp(forward, clip_tokens.astype(jnp.float32), enc_weights, dec_weights)
        grad_in, grad_enc, grad_dec = pull(cotangent.astype(jnp.float32))
        carry = jax.tree.map(lambda total, term: total + term, carry, (grad_enc, grad_dec))
        return (carry, (decoded.astype(jnp.bfloat16), grad_in.astype(jnp.bfloat16)))
    initial = jax.tree.map(jnp.zeros_like, (enc_weights, dec_weights))
    (grad_enc, grad_dec), (decoded, token_grad) = lax.scan(one_clip, initial, (tokens, frames, visible, out_grad))
    enc_square = sum((jnp.sum(item * item) for item in grad_enc))
    dec_square = sum((jnp.sum(item * item) for item in grad_dec))
    grad_norms = jnp.stack([enc_square, dec_square]).astype(jnp.float32)
    return (decoded, token_grad, grad_enc[0], grad_enc[1], grad_enc[2], grad_enc[3], grad_enc[4], grad_enc[5], grad_dec[0], grad_dec[1], grad_dec[2], grad_dec[3], grad_dec[4], grad_dec[5], grad_dec[6], grad_dec[7], grad_dec[8], grad_norms)
```

```python
import jax
import jax.numpy as jnp
from jax import lax
from jax.sharding import PartitionSpec as P

HEAD_SIZE = 64


EPSILON = 1e-06
NEGATIVE = -1000000000.0


def from_partner(value, axis, apart):
    mask = 2**apart
    pairs = [(source, source ^ mask) for source in range(lax.axis_size(axis))]
    return lax.ppermute(value, axis, pairs)


def layer_norm(value, gain, shift):
    center = value - jnp.mean(value, axis=-1, keepdims=True)
    spread = jnp.mean(center * center, axis=-1, keepdims=True)
    return center * lax.rsqrt(spread + EPSILON) * gain + shift


def exact_gelu(value):
    return jax.nn.gelu(value, approximate=False)


def multiply(left, right):
    return jnp.dot(left, right, preferred_element_type=jnp.float32)


def left_transposed(left, right):
    return lax.dot_general(
        left, right, (((0,), (0,)), ((), ())), preferred_element_type=jnp.float32
    )


def right_transposed(left, right):
    return lax.dot_general(
        left, right, (((1,), (1,)), ((), ())), preferred_element_type=jnp.float32
    )


def attention_scores(queries, keys, key_valid, scale):
    scores = jnp.einsum("qhd,khd->hqk", queries, keys, preferred_element_type=jnp.float32) * scale
    return jnp.where(key_valid[None, None, :], scores, NEGATIVE)


def block_forward(inputs, weights, heads, key_valid):
    vectors, qkv_weight, out_weight, up_weight, up_bias, down_weight = weights
    rows = vectors.astype(jnp.float32)
    count, width = inputs.shape
    size = width // heads
    scale = size ** (-0.5)
    normed = layer_norm(inputs, rows[0], rows[1]).astype(jnp.bfloat16)
    joined = multiply(normed, qkv_weight)
    queries = (joined[:, :width] + rows[2]).astype(jnp.bfloat16).reshape(count, heads, size)
    keys = joined[:, width : 2 * width].astype(jnp.bfloat16).reshape(count, heads, size)
    values = (joined[:, 2 * width :] + rows[3]).astype(jnp.bfloat16).reshape(count, heads, size)
    scores = attention_scores(queries, keys, key_valid, scale)
    peak = jnp.max(scores, axis=-1, keepdims=True)
    expo = jnp.exp(scores - peak)
    total = jnp.sum(expo, axis=-1, keepdims=True)
    probs = expo / total
    log_total = peak + jnp.log(total)
    mixed = jnp.einsum(
        "hqk,khd->qhd", probs.astype(jnp.bfloat16), values, preferred_element_type=jnp.float32
    )
    mixed = mixed.reshape(count, width).astype(jnp.bfloat16)
    middle = inputs + (multiply(mixed, out_weight) + rows[4])
    normed_two = layer_norm(middle, rows[5], rows[6]).astype(jnp.bfloat16)
    hidden_pre = multiply(normed_two, up_weight) + up_bias.astype(jnp.float32)
    activated = exact_gelu(hidden_pre).astype(jnp.bfloat16)
    output = middle + (multiply(activated, down_weight) + rows[7])
    saved = (
        inputs,
        normed,
        queries,
        keys,
        values,
        log_total,
        mixed,
        middle,
        normed_two,
        hidden_pre,
        activated,
    )
    return (output, saved)


def block_backward(grad_out, weights, heads, key_valid, saved):
    vectors, qkv_weight, out_weight, up_weight, up_bias, down_weight = weights
    rows = vectors.astype(jnp.float32)
    (
        inputs,
        normed,
        queries,
        keys,
        values,
        log_total,
        mixed,
        middle,
        normed_two,
        hidden_pre,
        activated,
    ) = saved
    count, width = inputs.shape
    size = width // heads
    scale = size ** (-0.5)
    grad_low = grad_out.astype(jnp.bfloat16)
    grad_down = left_transposed(activated, grad_low)
    grad_act = right_transposed(grad_low, down_weight)
    grad_hidden = jax.vjp(exact_gelu, hidden_pre)[1](grad_act)[0].astype(jnp.bfloat16)
    grad_up_bias = jnp.sum(grad_hidden.astype(jnp.float32), axis=0)
    grad_up = left_transposed(normed_two, grad_hidden)
    grad_normed_two = right_transposed(grad_hidden, up_weight)
    norm_pull = jax.vjp(layer_norm, middle, rows[5], rows[6])[1]
    grad_mid_norm, grad_gain_two, grad_shift_two = norm_pull(grad_normed_two)
    grad_middle = grad_out + grad_mid_norm
    grad_branch = grad_middle.astype(jnp.bfloat16)
    grad_out_weight = left_transposed(mixed, grad_branch)
    grad_mixed = (
        right_transposed(grad_branch, out_weight).astype(jnp.bfloat16).reshape(count, heads, size)
    )
    scores = attention_scores(queries, keys, key_valid, scale)
    probs = jnp.exp(scores - log_total)
    grad_values = jnp.einsum(
        "hqk,qhd->khd", probs.astype(jnp.bfloat16), grad_mixed, preferred_element_type=jnp.float32
    ).astype(jnp.bfloat16)
    grad_probs = jnp.einsum("qhd,khd->hqk", grad_mixed, values, preferred_element_type=jnp.float32)
    grad_scores = (
        probs * (grad_probs - jnp.sum(grad_probs * probs, axis=-1, keepdims=True))
    ).astype(jnp.bfloat16)
    grad_queries = (
        jnp.einsum("hqk,khd->qhd", grad_scores, keys, preferred_element_type=jnp.float32) * scale
    ).astype(jnp.bfloat16)
    grad_keys = (
        jnp.einsum("hqk,qhd->khd", grad_scores, queries, preferred_element_type=jnp.float32) * scale
    ).astype(jnp.bfloat16)
    grad_queries = grad_queries.reshape(count, width)
    grad_keys = grad_keys.reshape(count, width)
    grad_values = grad_values.reshape(count, width)
    grad_joined = jnp.concatenate([grad_queries, grad_keys, grad_values], axis=1)
    grad_qkv = left_transposed(normed, grad_joined)
    grad_normed = right_transposed(grad_joined, qkv_weight)
    grad_in_norm, grad_gain, grad_shift = jax.vjp(layer_norm, inputs, rows[0], rows[1])[1](
        grad_normed
    )
    grad_rows = jnp.stack(
        [
            grad_gain,
            grad_shift,
            jnp.sum(grad_queries.astype(jnp.float32), axis=0),
            jnp.sum(grad_values.astype(jnp.float32), axis=0),
            jnp.sum(grad_branch.astype(jnp.float32), axis=0),
            grad_gain_two,
            grad_shift_two,
            jnp.sum(grad_low.astype(jnp.float32), axis=0),
        ]
    )
    return (
        grad_middle + grad_in_norm,
        (grad_rows, grad_qkv, grad_out_weight, grad_up, grad_up_bias, grad_down),
    )


def gather_plan(visible_row, slot_count, patch_count):
    seen_count = visible_row.shape[0]
    patch = jnp.arange(patch_count, dtype=jnp.int32)
    match = visible_row[None, :] == patch[:, None]
    seen = jnp.any(match, axis=1)
    rank = jnp.sum(jnp.where(match, jnp.arange(seen_count, dtype=jnp.int32)[None, :], 0), axis=1)
    slot = jnp.arange(slot_count, dtype=jnp.int32)
    source = (slot[:, None] * seen_count + rank[None, :]).reshape(-1)
    seen_row = jnp.broadcast_to(seen[None, :], (slot_count, patch_count)).reshape(-1)
    return (source, seen_row)


def slot_table(slots_used, slot_count):
    slot = jnp.arange(slot_count, dtype=jnp.int32)
    divisor = slots_used - 1
    numerator = slot * (slot_count - 1)
    lower = numerator // divisor
    fraction = (numerator - lower * divisor).astype(jnp.float32) / divisor.astype(jnp.float32)
    upper = jnp.minimum(lower + 1, slot_count - 1)
    column = slot[None, :]
    first = (column == lower[:, None]).astype(jnp.float32)
    second = (column == upper[:, None]).astype(jnp.float32)
    return (1.0 - fraction)[:, None] * first + fraction[:, None] * second


def square_sum(arrays):
    return sum((jnp.sum(item * item) for item in arrays))


def shards(
    tokens,
    frames,
    visible,
    out_grad,
    enc_vectors,
    enc_qkv,
    enc_out,
    enc_up,
    enc_up_bias,
    enc_down,
    proj_weight,
    dec_vectors,
    dec_qkv,
    dec_out,
    dec_up,
    dec_up_bias,
    dec_down,
    time_pos,
    space_pos,
):
    enc_weights = (enc_vectors, enc_qkv, enc_out, enc_up, enc_up_bias, enc_down)
    dec_block = (dec_vectors[:8], dec_qkv, dec_out, dec_up, dec_up_bias, dec_down)
    dec_params = (
        proj_weight,
        dec_vectors,
        dec_qkv,
        dec_out,
        dec_up,
        dec_up_bias,
        dec_down,
        time_pos,
        space_pos,
    )
    batch, vis_cap, enc_width = tokens.shape
    long_cap, dec_width = (out_grad.shape[1], out_grad.shape[2])
    slot_count = time_pos.shape[0]
    patch_count = space_pos.shape[0]
    seen_count = visible.shape[1]
    enc_heads = enc_width // HEAD_SIZE
    dec_heads = dec_width // HEAD_SIZE
    section = lax.axis_index("section")

    def mine(array):
        return lax.dynamic_index_in_dim(array, section, 0, keepdims=False)

    used = mine(frames) // 2
    seen_row = mine(visible)
    cotangent = mine(out_grad).astype(jnp.float32)
    enc_valid = jnp.arange(vis_cap) < used * seen_count
    enc_output, enc_saved = block_forward(
        mine(tokens).astype(jnp.float32), enc_weights, enc_heads, enc_valid
    )
    sent = enc_output.astype(jnp.bfloat16)
    source, seen_mask = gather_plan(seen_row, slot_count, patch_count)
    target = (
        jnp.arange(slot_count, dtype=jnp.int32)[:, None] * patch_count + seen_row[None, :]
    ).reshape(-1)
    projected = multiply(sent, proj_weight)
    base = jnp.where(
        seen_mask[:, None],
        jnp.take(projected, source, axis=0),
        dec_vectors[8].astype(jnp.float32),
    )
    table = slot_table(used, slot_count)
    slot_pos = jnp.dot(table, time_pos.astype(jnp.float32), precision=lax.Precision.HIGHEST)
    start = (
        base.reshape(slot_count, patch_count, dec_width)
        + slot_pos[:, None, :]
        + space_pos.astype(jnp.float32)[None]
    )
    start = start.reshape(long_cap, dec_width)
    row_valid = jnp.arange(long_cap) < used * patch_count
    output, saved = block_forward(start, dec_block, dec_heads, row_valid)
    decoded_row = jnp.where(row_valid[:, None], output, 0.0).astype(jnp.bfloat16)
    grad_start, block_grads = block_backward(
        jnp.where(row_valid[:, None], cotangent, 0.0), dec_block, dec_heads, row_valid, saved
    )
    grad_grid = grad_start.reshape(slot_count, patch_count, dec_width)
    grad_space = jnp.sum(grad_grid, axis=0)
    grad_time = jnp.dot(table.T, jnp.sum(grad_grid, axis=1), precision=lax.Precision.HIGHEST)
    grad_mask = jnp.sum(jnp.where(seen_mask[:, None], 0.0, grad_start), axis=0)
    grad_projected = jnp.take(grad_start, target, axis=0).astype(jnp.bfloat16)
    grad_proj = left_transposed(sent, grad_projected)
    grad_sent = right_transposed(grad_projected, proj_weight).astype(jnp.bfloat16)
    grad_rows = jnp.concatenate([block_grads[0], grad_mask[None, :]], axis=0)
    grad_in, enc_grads = block_backward(
        grad_sent.astype(jnp.float32), enc_weights, enc_heads, enc_valid, enc_saved
    )
    grads = (
        *enc_grads,
        grad_proj,
        grad_rows,
        *block_grads[1:],
        grad_time,
        grad_space,
    )

    def halves(array):
        axis = array.ndim - 1
        half = array.shape[axis] // 2
        keep = lax.dynamic_slice_in_dim(array, section * half, half, axis)
        give = lax.dynamic_slice_in_dim(array, (1 - section) * half, half, axis)
        return (keep, from_partner(give.astype(jnp.bfloat16), "section", 0))

    def both_clips(array):
        keep, came = halves(array)
        pair = jnp.stack([keep, came])
        return jnp.where(section == 0, pair, pair[::-1])

    decoded_half = both_clips(decoded_row)
    token_half = both_clips(grad_in.astype(jnp.bfloat16))
    local = []
    for item in grads:
        keep, came = halves(item)
        local.append((keep + came.astype(jnp.float32)).astype(jnp.bfloat16))
    summed = [item.astype(jnp.float32) for item in lax.psum(tuple(local), "dp")]
    squares = lax.psum(jnp.stack([square_sum(summed[:6]), square_sum(summed[6:])]), "section")
    norms = lax.dynamic_slice_in_dim(squares, section, 1, 0)
    return (decoded_half, token_half, *summed, norms)


def solution(mesh):
    placed = (
        P("dp", None, None),
        P("dp"),
        P("dp", None),
        P("dp", None, None),
        P(),
        P(),
        P(),
        P(),
        P(),
        P(),
        P(),
        P(),
        P(),
        P(),
        P(),
        P(),
        P(),
        P(),
        P(),
    )
    return jax.shard_map(
        shards,
        mesh=mesh,
        in_specs=placed,
        out_specs=(
            P("dp", None, "section"),
            P("dp", None, "section"),
            P(None, "section"),
            P(None, "section"),
            P(None, "section"),
            P(None, "section"),
            P("section"),
            P(None, "section"),
            P(None, "section"),
            P(None, "section"),
            P(None, "section"),
            P(None, "section"),
            P(None, "section"),
            P("section"),
            P(None, "section"),
            P(None, "section"),
            P(None, "section"),
            P("section"),
        ),
        check_vma=False,
    )
```

```python
import functools
import jax, jax.numpy as jnp, numpy as np
from jax import lax
from jax.experimental import pallas as pl
from jax.experimental.pallas import tpu as pltpu

EPS = 1e-6
NEG = -1e9
LOG2E = 1.4426950408889634
LN2 = 0.6931471805599453
F32, BF = jnp.float32, jnp.bfloat16


def dot(a, b, ca=1, cb=0):
    return lax.dot_general(a, b, (((ca,), (cb,)), ((), ())), preferred_element_type=F32)


def tiles_of(total, size):
    return [(s, min(size, total - s)) for s in range(0, total, size)]


def over(total, size, body, carry):
    full = total // size
    if full:
        carry = lax.fori_loop(0, full, lambda i, k: body(pl.ds(pl.multiple_of(i * size, 128), size), size, k), carry)
    if total % size:
        carry = body(pl.ds(full * size, total % size), total % size, carry)
    return carry


def norm_c(x):
    mean = jnp.mean(x, axis=0, keepdims=True)
    c = x - mean
    r = lax.rsqrt(jnp.mean(c * c, axis=0, keepdims=True) + EPS)
    return c * r, r


def gelu_pair(u):
    a = jnp.abs(u)
    t = 1.0 / (1.0 + (0.3275911 * 0.7071067811865476) * a)
    e = jnp.exp2((-0.5 * LOG2E) * (u * u))
    poly = t * (0.5 * 0.254829592 + t * (0.5 * -0.284496736 + t * (0.5 * 1.421413741 + t * (0.5 * -1.453152027 + t * (0.5 * 1.061405429)))))
    tail = poly * e
    phi = jnp.where(u >= 0, 1.0 - tail, tail)
    return u * phi, phi + u * (e * 0.3989422804014327)


def dec_kernel(used_ref, tgt_ref, proj_ref, posm_ref, space_ref, vec_ref, wqkv_ref, wo_ref, w1_ref, b1_ref, w2_ref, dy_ref,
               decoded_ref, dz_ref, gpos_ref, gvec_ref, gqkv_ref, go_ref, g1_ref, gb1_ref, g2_ref,
               x_s, a1_s, qkv_s, e_s, l_s, o_s, m_s, a2_s, g_s, gp_s, dy_s, db_s, sel_s, doa_s, do_s, o32_s, *, W, L, H, FF, patches, TQ, TA):
    dqkv_s, ds_s = g_s, gp_s
    valid = used_ref[0] * patches
    col = lambda i: vec_ref[:, i:i + 1]
    HS = 64
    lane = lax.broadcasted_iota(jnp.int32, (1, L), 1)
    V = tgt_ref.shape[0]
    onehot = (tgt_ref[...] == lax.broadcasted_iota(jnp.int32, (V, L), 1)).astype(F32)
    slot = lane // patches
    patch_oh = (lax.broadcasted_iota(jnp.int32, (patches, L), 0) == lane - slot * patches).astype(BF)
    seen = jnp.sum(onehot, axis=0, keepdims=True)
    srow = lax.broadcasted_iota(jnp.int32, (32, L), 0)
    slot_oh = jnp.where(srow < 16, ((srow & 7) == slot).astype(F32), jnp.where(srow == 16, 1.0 - seen, 0.0)).astype(BF)
    sel_s[:V, :] = onehot.astype(BF)
    sel_s[V:V + patches, :] = patch_oh
    sel_s[V + patches:, :] = slot_oh
    proj = proj_ref[...]
    hi = proj.astype(BF)
    lo = (proj - hi.astype(F32)).astype(BF)
    src = jnp.concatenate([hi, space_ref[...], posm_ref[...]], axis=0)

    def first(c, n, k):
        x = dot(src, sel_s[:, c], 0, 0) + dot(lo, sel_s[:V, c], 0, 0)
        x_s[:, c] = x
        xh, _ = norm_c(x)
        a1 = (xh * col(0) + col(1)).astype(BF)
        a1_s[:, c] = a1
        j = dot(wqkv_ref[...], a1, 0, 0)
        qkv_s[:W, c] = ((j[:W] + col(2)) * (0.125 * LOG2E)).astype(BF)
        qkv_s[W:2 * W, c] = j[W:2 * W].astype(BF)
        qkv_s[2 * W:, c] = (j[2 * W:] + col(3)).astype(BF)
        return k

    over(L, TQ, first, 0)
    arow = lax.broadcasted_iota(jnp.int32, (16, L), 0)
    kbias = jnp.where((arow == 0) & (lane >= valid), NEG, 0.0).astype(BF)
    one0 = (arow == 0).astype(BF)
    one01 = (arow < 2).astype(BF)

    def fwd_head(h, carry):
        hs = pl.ds(pl.multiple_of(h * HS, HS), HS)
        ks = pl.ds(pl.multiple_of(W + h * HS, HS), HS)
        vs = pl.ds(pl.multiple_of(2 * W + h * HS, HS), HS)
        kr = jnp.concatenate([qkv_s[ks, :], kbias], axis=0).T
        vc = jnp.concatenate([qkv_s[vs, :], one0], axis=0)

        def tile(c, n, exact):
            qc = jnp.concatenate([qkv_s[hs, c], one0[:, :n]], axis=0)
            st = dot(kr, qc)
            if exact:
                st = st - jnp.max(st, axis=0, keepdims=True)
            e = jnp.exp2(st).astype(BF)
            e_s[h, :, c] = e
            oa = dot(vc, e)
            rl = 1.0 / oa[HS:HS + 1]
            l_s[h, :, c] = jnp.broadcast_to(rl, (8, n))
            o = oa[:HS] * rl
            o32_s[hs, c] = o
            o_s[hs, c] = o.astype(BF)

        square = lambda v: jnp.max(jnp.sum(v * v, axis=0))
        bound = square(qkv_s[hs, :].astype(F32)) * square(qkv_s[ks, :].astype(F32))

        @pl.when(bound <= 60.0 * 60.0)
        def _():
            over(L, TA, lambda c, n, k: (tile(c, n, False), k)[1], 0)

        @pl.when(jnp.logical_not(bound <= 60.0 * 60.0))
        def _():
            over(L, TA, lambda c, n, k: (tile(c, n, True), k)[1], 0)

        return carry

    lax.fori_loop(0, H, fwd_head, 0)

    def middle(c, n, sums):
        sum_b1, sum_dy, sum_g2, sum_s2, sum_db = sums
        live = (lax.broadcasted_iota(jnp.int32, (1, n), 1) + c.start < valid).astype(F32)
        mid = x_s[:, c] + (dot(wo_ref[...], o_s[:, c], 0, 0) + col(4))
        xh, r = norm_c(mid)
        a2 = (xh * col(5) + col(6)).astype(BF)
        a2_s[:, c] = a2
        u = dot(w1_ref[...], a2, 0, 0) + b1_ref[...]
        g, gp = gelu_pair(u)
        g = g.astype(BF)
        g_s[:, c] = g
        y = mid + (dot(w2_ref[...], g, 0, 0) + col(7))
        decoded_ref[c, :] = (y * live).astype(BF).T
        dyf = dy_ref[c, :].astype(F32).T * live
        dy = dyf.astype(BF)
        dy_s[:, c] = dy
        duf = gp * dot(w2_ref[...], dy)
        du = duf.astype(BF)
        gp_s[:, c] = du
        da2 = dot(w1_ref[...], du)
        dg = da2 * col(5)
        dm = dyf + r * (dg - jnp.mean(dg, axis=0, keepdims=True) - xh * jnp.mean(dg * xh, axis=0, keepdims=True))
        db = dm.astype(BF)
        db_s[:, c] = db
        do_s[:, c] = dot(wo_ref[...], db).astype(BF)
        m_s[:, c] = dm
        rs = lambda v: jnp.sum(v, axis=1, keepdims=True)
        return (sum_b1 + rs(duf), sum_dy + rs(dyf), sum_g2 + rs(da2 * xh), sum_s2 + rs(da2), sum_db + rs(dm))

    zero = jnp.zeros((W, 1), F32)
    sum_b1, sum_dy, sum_g2, sum_s2, sum_db = over(L, TQ, middle, (jnp.zeros((FF, 1), F32), zero, zero, zero, zero))
    gvec_ref[:, 4:5] = sum_db
    gvec_ref[:, 5:6] = sum_g2
    gvec_ref[:, 6:7] = sum_s2
    gvec_ref[:, 7:8] = sum_dy
    gb1_ref[...] = sum_b1
    g2_ref[...] = dot(g_s[...], dy_s[...], 1, 1).astype(BF)
    g1_ref[...] = dot(a2_s[...], gp_s[...], 1, 1).astype(BF)
    go_ref[...] = dot(o_s[...], db_s[...], 1, 1).astype(BF)

    def bwd_head(h, carry):
        hs = pl.ds(pl.multiple_of(h * HS, HS), HS)
        ks = pl.ds(pl.multiple_of(W + h * HS, HS), HS)
        vs = pl.ds(pl.multiple_of(2 * W + h * HS, HS), HS)
        vr = jnp.concatenate([qkv_s[vs, :], one01], axis=0).T
        kc = qkv_s[ks, :]
        dob = (do_s[hs, :].astype(F32) * l_s[h, 0:1, :]).astype(BF)
        dl = -jnp.sum(dob.astype(F32) * o32_s[hs, :], axis=0, keepdims=True)
        dlh = dl.astype(BF).astype(F32)
        doa_s[:HS, :] = dob
        doa_s[HS:, :] = jnp.where(arow == 0, dlh, jnp.where(arow == 1, dl - dlh, 0.0)).astype(BF)
        def tile(c, n, k):
            dp = dot(vr, doa_s[:, c])
            ds = (e_s[h, :, c].astype(F32) * dp).astype(BF)
            ds_s[:L, c] = ds
            dqkv_s[hs, c] = (dot(kc, ds) * 0.125).astype(BF)
            return k

        over(L, TA, tile, 0)
        dor = doa_s[:HS, :].T
        qr = qkv_s[hs, :].T

        def tile2(c, n, k):
            dqkv_s[vs, c] = dot(e_s[h, c, :], dor).T.astype(BF)
            dqkv_s[ks, c] = (dot(ds_s[c, :], qr) * LN2).T.astype(BF)
            return k

        return over(L, TA, tile2, carry)

    lax.fori_loop(0, H, bwd_head, 0)
    gqkv_ref[...] = dot(a1_s[...], dqkv_s[:3 * W, :], 1, 1).astype(BF)

    def last(c, n, sums):
        sum_g1, sum_s1, sum_q, sum_v, gsel = sums
        rs = lambda v: jnp.sum(v, axis=1, keepdims=True)
        da = dot(wqkv_ref[...], dqkv_s[:3 * W, c])
        xh, r = norm_c(x_s[:, c])
        dg = da * col(0)
        dx = m_s[:, c] + r * (dg - jnp.mean(dg, axis=0, keepdims=True) - xh * jnp.mean(dg * xh, axis=0, keepdims=True))
        return (sum_g1 + rs(da * xh), sum_s1 + rs(da), sum_q + rs(dqkv_s[:W, c].astype(F32)), sum_v + rs(dqkv_s[2 * W:3 * W, c].astype(F32)),
                gsel + dot(dx.astype(BF), sel_s[:, c], 1, 1))

    sum_g1, sum_s1, sum_q, sum_v, gsel = over(L, TQ, last, (zero, zero, zero, zero, jnp.zeros((W, sel_s.shape[0]), F32)))
    gvec_ref[:, 0:1] = sum_g1
    gvec_ref[:, 1:2] = sum_s1
    gvec_ref[:, 2:3] = sum_q
    gvec_ref[:, 3:4] = sum_v
    gvec_ref[:, 8:] = jnp.zeros((W, gvec_ref.shape[1] - 8), F32)
    gs = gsel.T
    dz_ref[...] = gs[:V].astype(BF)
    gpos_ref[...] = gs[V:]


def dec_block_call(used, tgt, proj, posm, space, vec, wqkv, wo, w1, b1, w2, dy, TQ=256, TA=256):
    W, L, FF = wqkv.shape[0], dy.shape[0], w1.shape[1]
    H = W // 64
    patches = space.shape[0]
    V = tgt.shape[0]
    vm = pl.BlockSpec(memory_space=pltpu.VMEM)
    S = jax.ShapeDtypeStruct
    return pl.pallas_call(
        functools.partial(dec_kernel, W=W, L=L, H=H, FF=FF, patches=patches, TQ=TQ, TA=TA),
        in_specs=[pl.BlockSpec(memory_space=pltpu.SMEM)] + [vm] * 11,
        out_specs=[vm] * 9,
        out_shape=[S((L, W), BF), S((V, W), BF), S((patches + 32, W), F32), S((W, 128), F32), S((W, 3 * W), BF), S((W, W), BF), S((W, FF), BF), S((FF, 1), F32), S((FF, W), BF)],
        scratch_shapes=[
            pltpu.VMEM((W, L), F32),
            pltpu.VMEM((W, L), BF),
            pltpu.VMEM((3 * W, L), BF),
            pltpu.VMEM((H, L, L), BF),
            pltpu.VMEM((H, 8, L), F32),
            pltpu.VMEM((W, L), BF),
            pltpu.VMEM((W, L), F32),
            pltpu.VMEM((W, L), BF),
            pltpu.VMEM((FF, L), BF),
            pltpu.VMEM((FF, L), BF),
            pltpu.VMEM((W, L), BF),
            pltpu.VMEM((W, L), BF),
            pltpu.VMEM((V + patches + 32, L), BF),
            pltpu.VMEM((80, L), BF),
            pltpu.VMEM((W, L), BF),
            pltpu.VMEM((W, L), F32),
        ],
        compiler_params=pltpu.CompilerParams(vmem_limit_bytes=63 * 1024 * 1024),
        cost_estimate=pl.CostEstimate(flops=28_000_000_000, bytes_accessed=12_000_000, transcendentals=10_000_000),
        name="decoder",
    )(used, tgt, proj, posm, space, vec, wqkv, wo, w1, b1, w2, dy)


HEAD_SIZE = 64


EPSILON = 1e-06
NEGATIVE = -1000000000.0


def from_partner(value, axis, apart):
    mask = 2**apart
    pairs = [(source, source ^ mask) for source in range(lax.axis_size(axis))]
    return lax.ppermute(value, axis, pairs)


def layer_norm(value, gain, shift):
    center = value - jnp.mean(value, axis=-1, keepdims=True)
    spread = jnp.mean(center * center, axis=-1, keepdims=True)
    return center * lax.rsqrt(spread + EPSILON) * gain + shift


def exact_gelu(value):
    return jax.nn.gelu(value, approximate=False)


def multiply(left, right):
    return jnp.dot(left, right, preferred_element_type=jnp.float32)


def left_transposed(left, right):
    return lax.dot_general(
        left, right, (((0,), (0,)), ((), ())), preferred_element_type=jnp.float32
    )


def right_transposed(left, right):
    return lax.dot_general(
        left, right, (((1,), (1,)), ((), ())), preferred_element_type=jnp.float32
    )


def attention_scores(queries, keys, key_valid, scale):
    scores = jnp.einsum("qhd,khd->hqk", queries, keys, preferred_element_type=jnp.float32) * scale
    return jnp.where(key_valid[None, None, :], scores, NEGATIVE)


def block_forward(inputs, weights, heads, key_valid):
    vectors, qkv_weight, out_weight, up_weight, up_bias, down_weight = weights
    rows = vectors.astype(jnp.float32)
    count, width = inputs.shape
    size = width // heads
    scale = size ** (-0.5)
    normed = layer_norm(inputs, rows[0], rows[1]).astype(jnp.bfloat16)
    joined = multiply(normed, qkv_weight)
    queries = (joined[:, :width] + rows[2]).astype(jnp.bfloat16).reshape(count, heads, size)
    keys = joined[:, width : 2 * width].astype(jnp.bfloat16).reshape(count, heads, size)
    values = (joined[:, 2 * width :] + rows[3]).astype(jnp.bfloat16).reshape(count, heads, size)
    scores = attention_scores(queries, keys, key_valid, scale)
    peak = jnp.max(scores, axis=-1, keepdims=True)
    expo = jnp.exp(scores - peak)
    total = jnp.sum(expo, axis=-1, keepdims=True)
    probs = expo / total
    log_total = peak + jnp.log(total)
    mixed = jnp.einsum(
        "hqk,khd->qhd", probs.astype(jnp.bfloat16), values, preferred_element_type=jnp.float32
    )
    mixed = mixed.reshape(count, width).astype(jnp.bfloat16)
    middle = inputs + (multiply(mixed, out_weight) + rows[4])
    normed_two = layer_norm(middle, rows[5], rows[6]).astype(jnp.bfloat16)
    hidden_pre = multiply(normed_two, up_weight) + up_bias.astype(jnp.float32)
    activated = exact_gelu(hidden_pre).astype(jnp.bfloat16)
    output = middle + (multiply(activated, down_weight) + rows[7])
    saved = (
        inputs,
        normed,
        queries,
        keys,
        values,
        log_total,
        mixed,
        middle,
        normed_two,
        hidden_pre,
        activated,
    )
    return (output, saved)


def block_backward(grad_out, weights, heads, key_valid, saved):
    vectors, qkv_weight, out_weight, up_weight, up_bias, down_weight = weights
    rows = vectors.astype(jnp.float32)
    (
        inputs,
        normed,
        queries,
        keys,
        values,
        log_total,
        mixed,
        middle,
        normed_two,
        hidden_pre,
        activated,
    ) = saved
    count, width = inputs.shape
    size = width // heads
    scale = size ** (-0.5)
    grad_low = grad_out.astype(jnp.bfloat16)
    grad_down = left_transposed(activated, grad_low)
    grad_act = right_transposed(grad_low, down_weight)
    grad_hidden = jax.vjp(exact_gelu, hidden_pre)[1](grad_act)[0].astype(jnp.bfloat16)
    grad_up_bias = jnp.sum(grad_hidden.astype(jnp.float32), axis=0)
    grad_up = left_transposed(normed_two, grad_hidden)
    grad_normed_two = right_transposed(grad_hidden, up_weight)
    norm_pull = jax.vjp(layer_norm, middle, rows[5], rows[6])[1]
    grad_mid_norm, grad_gain_two, grad_shift_two = norm_pull(grad_normed_two)
    grad_middle = grad_out + grad_mid_norm
    grad_branch = grad_middle.astype(jnp.bfloat16)
    grad_out_weight = left_transposed(mixed, grad_branch)
    grad_mixed = (
        right_transposed(grad_branch, out_weight).astype(jnp.bfloat16).reshape(count, heads, size)
    )
    scores = attention_scores(queries, keys, key_valid, scale)
    probs = jnp.exp(scores - log_total)
    grad_values = jnp.einsum(
        "hqk,qhd->khd", probs.astype(jnp.bfloat16), grad_mixed, preferred_element_type=jnp.float32
    ).astype(jnp.bfloat16)
    grad_probs = jnp.einsum("qhd,khd->hqk", grad_mixed, values, preferred_element_type=jnp.float32)
    grad_scores = (
        probs * (grad_probs - jnp.sum(grad_probs * probs, axis=-1, keepdims=True))
    ).astype(jnp.bfloat16)
    grad_queries = (
        jnp.einsum("hqk,khd->qhd", grad_scores, keys, preferred_element_type=jnp.float32) * scale
    ).astype(jnp.bfloat16)
    grad_keys = (
        jnp.einsum("hqk,qhd->khd", grad_scores, queries, preferred_element_type=jnp.float32) * scale
    ).astype(jnp.bfloat16)
    grad_queries = grad_queries.reshape(count, width)
    grad_keys = grad_keys.reshape(count, width)
    grad_values = grad_values.reshape(count, width)
    grad_joined = jnp.concatenate([grad_queries, grad_keys, grad_values], axis=1)
    grad_qkv = left_transposed(normed, grad_joined)
    grad_normed = right_transposed(grad_joined, qkv_weight)
    grad_in_norm, grad_gain, grad_shift = jax.vjp(layer_norm, inputs, rows[0], rows[1])[1](
        grad_normed
    )
    grad_rows = jnp.stack(
        [
            grad_gain,
            grad_shift,
            jnp.sum(grad_queries.astype(jnp.float32), axis=0),
            jnp.sum(grad_values.astype(jnp.float32), axis=0),
            jnp.sum(grad_branch.astype(jnp.float32), axis=0),
            grad_gain_two,
            grad_shift_two,
            jnp.sum(grad_low.astype(jnp.float32), axis=0),
        ]
    )
    return (
        grad_middle + grad_in_norm,
        (grad_rows, grad_qkv, grad_out_weight, grad_up, grad_up_bias, grad_down),
    )


def slot_table(slots_used, slot_count):
    slot = jnp.arange(slot_count, dtype=jnp.int32)
    divisor = slots_used - 1
    numerator = slot * (slot_count - 1)
    lower = numerator // divisor
    fraction = (numerator - lower * divisor).astype(jnp.float32) / divisor.astype(jnp.float32)
    upper = jnp.minimum(lower + 1, slot_count - 1)
    column = slot[None, :]
    first = (column == lower[:, None]).astype(jnp.float32)
    second = (column == upper[:, None]).astype(jnp.float32)
    return (1.0 - fraction)[:, None] * first + fraction[:, None] * second


def square_sum(arrays):
    return sum((jnp.sum(item * item) for item in arrays))


def shards(
    tokens,
    frames,
    visible,
    out_grad,
    enc_vectors,
    enc_qkv,
    enc_out,
    enc_up,
    enc_up_bias,
    enc_down,
    proj_weight,
    dec_vectors,
    dec_qkv,
    dec_out,
    dec_up,
    dec_up_bias,
    dec_down,
    time_pos,
    space_pos,
):
    enc_weights = (enc_vectors, enc_qkv, enc_out, enc_up, enc_up_bias, enc_down)
    dec_params = (
        proj_weight,
        dec_vectors,
        dec_qkv,
        dec_out,
        dec_up,
        dec_up_bias,
        dec_down,
        time_pos,
        space_pos,
    )
    batch, vis_cap, enc_width = tokens.shape
    dec_width = out_grad.shape[2]
    slot_count = time_pos.shape[0]
    patch_count = space_pos.shape[0]
    seen_count = visible.shape[1]
    enc_heads = enc_width // HEAD_SIZE
    section = lax.axis_index("section")

    def mine(array):
        return lax.dynamic_index_in_dim(array, section, 0, keepdims=False)

    used = mine(frames) // 2
    seen_row = mine(visible)
    enc_valid = jnp.arange(vis_cap) < used * seen_count
    enc_output, enc_saved = block_forward(
        mine(tokens).astype(jnp.float32), enc_weights, enc_heads, enc_valid
    )
    sent = enc_output.astype(jnp.bfloat16)
    target = (
        jnp.arange(slot_count, dtype=jnp.int32)[:, None] * patch_count + seen_row[None, :]
    ).reshape(-1, 1)
    projected = multiply(sent, proj_weight)
    table = slot_table(used, slot_count)
    slot_pos = jnp.dot(table, time_pos.astype(jnp.float32), precision=lax.Precision.HIGHEST)
    slot_high = slot_pos.astype(jnp.bfloat16)
    slot_low = (slot_pos - slot_high.astype(jnp.float32)).astype(jnp.bfloat16)
    positions = jnp.concatenate(
        [slot_high, slot_low, dec_vectors[8:9], jnp.zeros((15, dec_width), jnp.bfloat16)]
    )
    columns = jnp.pad(dec_vectors[:8].astype(jnp.float32).T, ((0, 0), (0, 120)))
    (
        decoded_row,
        grad_projected,
        grad_positions,
        grad_columns,
        grad_dec_qkv,
        grad_dec_out,
        grad_dec_up,
        grad_dec_up_bias,
        grad_dec_down,
    ) = dec_block_call(
        used.reshape(1),
        target,
        projected,
        positions,
        space_pos,
        columns,
        dec_qkv,
        dec_out,
        dec_up,
        dec_up_bias.astype(jnp.float32)[:, None],
        dec_down,
        mine(out_grad),
        TQ=384,
        TA=640,
    )
    grad_space = grad_positions[:patch_count]
    by_slot = grad_positions[patch_count : patch_count + slot_count]
    grad_time = jnp.dot(table.T, by_slot, precision=lax.Precision.HIGHEST)
    grad_mask = grad_positions[patch_count + 2 * slot_count]
    grad_proj = left_transposed(sent, grad_projected)
    grad_sent = right_transposed(grad_projected, proj_weight).astype(jnp.bfloat16)
    grad_rows = jnp.concatenate([grad_columns[:, :8].T, grad_mask[None, :]], axis=0)
    grad_in, enc_grads = block_backward(
        grad_sent.astype(jnp.float32), enc_weights, enc_heads, enc_valid, enc_saved
    )
    grads = (
        *enc_grads,
        grad_proj,
        grad_rows,
        grad_dec_qkv,
        grad_dec_out,
        grad_dec_up,
        grad_dec_up_bias[:, 0],
        grad_dec_down,
        grad_time,
        grad_space,
    )

    def halves(array):
        axis = array.ndim - 1
        half = array.shape[axis] // 2
        keep = lax.dynamic_slice_in_dim(array, section * half, half, axis)
        give = lax.dynamic_slice_in_dim(array, (1 - section) * half, half, axis)
        return (keep, from_partner(give.astype(jnp.bfloat16), "section", 0))

    def both_clips(array):
        keep, came = halves(array)
        pair = jnp.stack([keep, came])
        return jnp.where(section == 0, pair, pair[::-1])

    decoded_half = both_clips(decoded_row)
    token_half = both_clips(grad_in.astype(jnp.bfloat16))
    local = []
    for item in grads:
        keep, came = halves(item)
        local.append((keep.astype(jnp.float32) + came.astype(jnp.float32)).astype(jnp.bfloat16))
    summed = [item.astype(jnp.float32) for item in lax.psum(tuple(local), "dp")]
    squares = lax.psum(jnp.stack([square_sum(summed[:6]), square_sum(summed[6:])]), "section")
    norms = lax.dynamic_slice_in_dim(squares, section, 1, 0)
    return (decoded_half, token_half, *summed, norms)


from jax.sharding import PartitionSpec as P


def solution(mesh):
    placed = (
        P("dp", None, None),
        P("dp"),
        P("dp", None),
        P("dp", None, None),
        P(),
        P(),
        P(),
        P(),
        P(),
        P(),
        P(),
        P(),
        P(),
        P(),
        P(),
        P(),
        P(),
        P(),
        P(),
    )
    return jax.shard_map(
        shards,
        mesh=mesh,
        in_specs=placed,
        out_specs=(
            P("dp", None, "section"),
            P("dp", None, "section"),
            P(None, "section"),
            P(None, "section"),
            P(None, "section"),
            P(None, "section"),
            P("section"),
            P(None, "section"),
            P(None, "section"),
            P(None, "section"),
            P(None, "section"),
            P(None, "section"),
            P(None, "section"),
            P("section"),
            P(None, "section"),
            P(None, "section"),
            P(None, "section"),
            P("section"),
        ),
        check_vma=False,
    )
```

```python
import functools
import jax, jax.numpy as jnp, numpy as np
from jax import lax
from jax.experimental import pallas as pl
from jax.experimental.pallas import tpu as pltpu

EPS = 1e-6
NEG = -1e9
LOG2E = 1.4426950408889634
LN2 = 0.6931471805599453
F32, BF = jnp.float32, jnp.bfloat16


def dot(a, b, ca=1, cb=0):
    return lax.dot_general(a, b, (((ca,), (cb,)), ((), ())), preferred_element_type=F32)


def tiles_of(total, size):
    return [(s, min(size, total - s)) for s in range(0, total, size)]


def over(total, size, body, carry):
    full = total // size
    if full:
        carry = lax.fori_loop(0, full, lambda i, k: body(pl.ds(pl.multiple_of(i * size, 128), size), size, k), carry)
    if total % size:
        carry = body(pl.ds(full * size, total % size), total % size, carry)
    return carry


def norm_c(x):
    mean = jnp.mean(x, axis=0, keepdims=True)
    c = x - mean
    r = lax.rsqrt(jnp.mean(c * c, axis=0, keepdims=True) + EPS)
    return c * r, r


def gelu_pair(u):
    a = jnp.abs(u)
    t = 1.0 / (1.0 + (0.3275911 * 0.7071067811865476) * a)
    e = jnp.exp2((-0.5 * LOG2E) * (u * u))
    poly = t * (0.5 * 0.254829592 + t * (0.5 * -0.284496736 + t * (0.5 * 1.421413741 + t * (0.5 * -1.453152027 + t * (0.5 * 1.061405429)))))
    tail = poly * e
    phi = jnp.where(u >= 0, 1.0 - tail, tail)
    return u * phi, phi + u * (e * 0.3989422804014327)


def dec_kernel(sec_ref, frames_ref, vis_ref, proj_ref, time_ref, space_ref, vecs_ref, wqkv_ref, wo_ref, w1_ref, bias_ref, w2_ref, dy_any,
               out_refs, dz_ref, pack_refs,
               x_s, a1_s, qkv_s, e_s, l_s, o_s, m_s, a2_s, g_s, gp_s, dy_s, db_s, sel_s, doa_s, do_s, o32_s, dy_ref, vec_ref, b1_ref, dec_s, dy_sem, *, W, L, H, FF, V, slots, patches, TQ, TA):
    dqkv_s, ds_s = g_s, gp_s
    sec = sec_ref[0]
    used = frames_ref[sec] // 2
    valid = used * patches
    dy_copy = pltpu.make_async_copy(dy_any.at[sec], dy_ref, dy_sem)
    dy_copy.start()
    seen_count = V // slots
    vecs = vecs_ref[...].astype(F32)
    vec_ref[...] = jnp.concatenate([vecs, jnp.zeros((16 - vecs.shape[0], W), F32)], axis=0).T
    b1_ref[...] = jnp.broadcast_to(bias_ref[...].reshape(1, FF).astype(F32), (8, FF)).T[:, 0:1]
    col = lambda i: vec_ref[:, i:i + 1]
    HS = 64
    lane = lax.broadcasted_iota(jnp.int32, (1, L), 1)
    vrow = lax.broadcasted_iota(jnp.int32, (V, 1), 0)
    vslot = jnp.zeros((V, 1), jnp.int32)
    for t in range(1, slots):
        vslot += (vrow >= t * seen_count).astype(jnp.int32)
    vrank = vrow - vslot * seen_count
    target = vslot * patches
    for j in range(seen_count):
        target += jnp.where(vrank == j, vis_ref[sec, j], 0)
    onehot = (target == lax.broadcasted_iota(jnp.int32, (V, L), 1)).astype(F32)
    slot = jnp.zeros((1, L), jnp.int32)
    for t in range(1, slots):
        slot += (lane >= t * patches).astype(jnp.int32)
    patch_oh = (lax.broadcasted_iota(jnp.int32, (patches, L), 0) == lane - slot * patches).astype(BF)
    seen = jnp.sum(onehot, axis=0, keepdims=True)
    srow = lax.broadcasted_iota(jnp.int32, (32, L), 0)
    slot_oh = jnp.where(srow < 16, ((srow & 7) == slot).astype(F32), jnp.where(srow == 16, 1.0 - seen, 0.0)).astype(BF)
    sel_s[:V, :] = onehot.astype(BF)
    sel_s[V:V + patches, :] = patch_oh
    sel_s[V + patches:, :] = slot_oh
    ti = lax.broadcasted_iota(jnp.int32, (slots, slots), 0)
    ii = lax.broadcasted_iota(jnp.int32, (slots, slots), 1)
    num = ti * (slots - 1)
    lower = jnp.zeros((slots, slots), jnp.int32)
    for q in range(1, (slots - 1) * (slots - 1) + 1):
        lower += (num >= q * (used - 1)).astype(jnp.int32)
    frac = (num - lower * (used - 1)).astype(F32) / jnp.full((slots, slots), used - 1, jnp.int32).astype(F32)
    upper = jnp.minimum(lower + 1, slots - 1)
    table = (1.0 - frac) * (ii == lower).astype(F32) + frac * (ii == upper).astype(F32)
    exact = lambda a, b, ca, cb: lax.dot_general(a, b, (((ca,), (cb,)), ((), ())), precision=lax.Precision.HIGHEST, preferred_element_type=F32)
    spos = exact(table, time_ref[...].astype(F32), 1, 0)
    shi = spos.astype(BF)
    slo = (spos - shi.astype(F32)).astype(BF)
    proj = proj_ref[...]
    hi = proj.astype(BF)
    lo = (proj - hi.astype(F32)).astype(BF)
    mask = vecs[8:9, :].astype(BF)
    src = jnp.concatenate([hi.astype(F32), space_ref[...].astype(F32), shi.astype(F32), slo.astype(F32), mask.astype(F32), jnp.zeros((15, W), F32)], axis=0).astype(BF)

    def first(c, n, k):
        x = dot(src, sel_s[:, c], 0, 0) + dot(lo, sel_s[:V, c], 0, 0)
        x_s[:, c] = x
        xh, _ = norm_c(x)
        a1 = (xh * col(0) + col(1)).astype(BF)
        a1_s[:, c] = a1
        j = dot(wqkv_ref[...], a1, 0, 0)
        qkv_s[:W, c] = ((j[:W] + col(2)) * (0.125 * LOG2E)).astype(BF)
        qkv_s[W:2 * W, c] = j[W:2 * W].astype(BF)
        qkv_s[2 * W:, c] = (j[2 * W:] + col(3)).astype(BF)
        return k

    over(L, TQ, first, 0)
    arow = lax.broadcasted_iota(jnp.int32, (16, L), 0)
    kbias = jnp.where((arow == 0) & (lane >= valid), NEG, 0.0).astype(BF)
    one0 = (arow == 0).astype(BF)
    one01 = (arow < 2).astype(BF)

    def fwd_head(h, carry):
        hs = pl.ds(pl.multiple_of(h * HS, HS), HS)
        ks = pl.ds(pl.multiple_of(W + h * HS, HS), HS)
        vs = pl.ds(pl.multiple_of(2 * W + h * HS, HS), HS)
        kr = jnp.concatenate([qkv_s[ks, :], kbias], axis=0).T
        vc = jnp.concatenate([qkv_s[vs, :], one0], axis=0)

        def tile(c, n, exact):
            qc = jnp.concatenate([qkv_s[hs, c], one0[:, :n]], axis=0)
            st = dot(kr, qc)
            if exact:
                st = st - jnp.max(st, axis=0, keepdims=True)
            e = jnp.exp2(st).astype(BF)
            e_s[h, :, c] = e
            oa = dot(vc, e)
            rl = 1.0 / oa[HS:HS + 1]
            l_s[h, :, c] = jnp.broadcast_to(rl, (8, n))
            o = oa[:HS] * rl
            o32_s[hs, c] = o
            o_s[hs, c] = o.astype(BF)

        square = lambda v: jnp.max(jnp.sum(v * v, axis=0))
        bound = square(qkv_s[hs, :].astype(F32)) * square(qkv_s[ks, :].astype(F32))

        @pl.when(bound <= 60.0 * 60.0)
        def _():
            over(L, TA, lambda c, n, k: (tile(c, n, False), k)[1], 0)

        @pl.when(jnp.logical_not(bound <= 60.0 * 60.0))
        def _():
            over(L, TA, lambda c, n, k: (tile(c, n, True), k)[1], 0)

        return carry

    lax.fori_loop(0, H, fwd_head, 0)

    def middle(c, n, sums):
        sum_b1, sum_dy, sum_g2, sum_s2, sum_db = sums
        live = (lax.broadcasted_iota(jnp.int32, (1, n), 1) + c.start < valid).astype(F32)
        mid = x_s[:, c] + (dot(wo_ref[...], o_s[:, c], 0, 0) + col(4))
        xh, r = norm_c(mid)
        a2 = (xh * col(5) + col(6)).astype(BF)
        a2_s[:, c] = a2
        u = dot(w1_ref[...], a2, 0, 0) + b1_ref[...]
        g, gp = gelu_pair(u)
        g = g.astype(BF)
        g_s[:, c] = g
        y = mid + (dot(w2_ref[...], g, 0, 0) + col(7))
        dec_s[:, c] = (y * live).astype(BF)
        dyf = dy_ref[c, :].astype(F32).T * live
        dy = dyf.astype(BF)
        dy_s[:, c] = dy
        duf = gp * dot(w2_ref[...], dy)
        du = duf.astype(BF)
        gp_s[:, c] = du
        da2 = dot(w1_ref[...], du)
        dg = da2 * col(5)
        dm = dyf + r * (dg - jnp.mean(dg, axis=0, keepdims=True) - xh * jnp.mean(dg * xh, axis=0, keepdims=True))
        db = dm.astype(BF)
        db_s[:, c] = db
        do_s[:, c] = dot(wo_ref[...], db).astype(BF)
        m_s[:, c] = dm
        rs = lambda v: jnp.sum(v, axis=1, keepdims=True)
        return (sum_b1 + rs(duf), sum_dy + rs(dyf), sum_g2 + rs(da2 * xh), sum_s2 + rs(da2), sum_db + rs(dm))

    dy_copy.wait()
    zero = jnp.zeros((W, 1), F32)
    sum_b1, sum_dy, sum_g2, sum_s2, sum_db = over(L, TQ, middle, (jnp.zeros((FF, 1), F32), zero, zero, zero, zero))
    blocks = dec_blocks(W, FF)
    for who, s in enumerate((sec, 1 - sec)):
        rows = lambda size, at=0: pl.ds(pl.multiple_of(s * (size // 2) + at, 16), W // 2)
        out_refs[who][...] = dec_s[rows(W), :]
        pack = pack_refs[who]
        for b in range(FF // W):
            r = blocks["down"] + b * (W // 2)
            pack[r:r + W // 2, :] = dot(dy_s[rows(W), :], g_s[b * W:b * W + W, :], 1, 1).astype(BF)
        for b in range(FF // 2 // W):
            r = blocks["up"] + b * W
            pack[r:r + W, :] = dot(a2_s[...], gp_s[pl.ds(pl.multiple_of(s * (FF // 2) + b * W, 16), W), :], 1, 1).astype(BF)
        r = blocks["out"]
        pack[r:r + W // 2, :] = dot(db_s[rows(W), :], o_s[...], 1, 1).astype(BF)

    def bwd_head(h, carry):
        hs = pl.ds(pl.multiple_of(h * HS, HS), HS)
        ks = pl.ds(pl.multiple_of(W + h * HS, HS), HS)
        vs = pl.ds(pl.multiple_of(2 * W + h * HS, HS), HS)
        vr = jnp.concatenate([qkv_s[vs, :], one01], axis=0).T
        kc = qkv_s[ks, :]
        dob = (do_s[hs, :].astype(F32) * l_s[h, 0:1, :]).astype(BF)
        dl = -jnp.sum(dob.astype(F32) * o32_s[hs, :], axis=0, keepdims=True)
        dlh = dl.astype(BF).astype(F32)
        doa_s[:HS, :] = dob
        doa_s[HS:, :] = jnp.where(arow == 0, dlh, jnp.where(arow == 1, dl - dlh, 0.0)).astype(BF)
        def tile(c, n, k):
            dp = dot(vr, doa_s[:, c])
            ds = (e_s[h, :, c].astype(F32) * dp).astype(BF)
            ds_s[:L, c] = ds
            dqkv_s[hs, c] = (dot(kc, ds) * 0.125).astype(BF)
            return k

        over(L, TA, tile, 0)
        dor = doa_s[:HS, :].T
        qr = qkv_s[hs, :].T

        def tile2(c, n, k):
            dqkv_s[vs, c] = dot(e_s[h, c, :], dor).T.astype(BF)
            dqkv_s[ks, c] = (dot(ds_s[c, :], qr) * LN2).T.astype(BF)
            return k

        return over(L, TA, tile2, carry)

    lax.fori_loop(0, H, bwd_head, 0)
    def last(c, n, sums):
        sum_g1, sum_s1, sum_q, sum_v, gsel = sums
        rs = lambda v: jnp.sum(v, axis=1, keepdims=True)
        da = dot(wqkv_ref[...], dqkv_s[:3 * W, c])
        xh, r = norm_c(x_s[:, c])
        dg = da * col(0)
        dx = m_s[:, c] + r * (dg - jnp.mean(dg, axis=0, keepdims=True) - xh * jnp.mean(dg * xh, axis=0, keepdims=True))
        return (sum_g1 + rs(da * xh), sum_s1 + rs(da), sum_q + rs(dqkv_s[:W, c].astype(F32)), sum_v + rs(dqkv_s[2 * W:3 * W, c].astype(F32)),
                gsel + dot(dx.astype(BF), sel_s[:, c], 1, 1))

    sum_g1, sum_s1, sum_q, sum_v, gsel = over(L, TQ, last, (zero, zero, zero, zero, jnp.zeros((W, sel_s.shape[0]), F32)))
    dz_ref[...] = gsel[:, :V].T.astype(BF)
    small = o32_s
    small[:, :8] = jnp.concatenate([sum_g1, sum_s1, sum_q, sum_v, sum_db, sum_g2, sum_s2, sum_dy], axis=1)
    small[:, 8:16] = gsel[:, V + patches + 16:V + patches + 24]
    small[:, 16:24] = exact(gsel[:, V + patches:V + patches + slots], table, 1, 0)
    small[:, 24:24 + patches] = gsel[:, V:V + patches]
    rows = 32 + patches
    small[:, 24 + patches:256] = jnp.zeros((W, 256 - 24 - patches), F32)
    wide = jnp.broadcast_to(sum_b1, (FF, 128))
    for who, s in enumerate((sec, 1 - sec)):
        pack = pack_refs[who]
        for b in range(3):
            r = blocks["qkv"] + b * (W // 2)
            pack[r:r + W // 2, :] = dot(dqkv_s[pl.ds(pl.multiple_of(s * (3 * W // 2) + b * (W // 2), 16), W // 2), :], a1_s[...], 1, 1).astype(BF)
        r = blocks["small"]
        pack[r:r + rows, :W // 2] = small[pl.ds(pl.multiple_of(s * (W // 2), 8), W // 2), :256].T[:rows].astype(BF)
        pack[r:r + rows, W // 2:] = jnp.zeros((rows, W - W // 2), BF)
        b1_ref[...] = sum_b1
        bias = jnp.broadcast_to(b1_ref[pl.ds(pl.multiple_of(s * (FF // 2), 8), FF // 2), :], (FF // 2, 128)).T[:16]
        r = blocks["bias"]
        for b in range(FF // 2 // W):
            pack[r + 16 * b:r + 16 * b + 16, :] = bias[:, b * W:b * W + W].astype(BF)


def dec_blocks(W, FF):
    at, rows = 0, {}
    for name, count in (("qkv", 3 * W // 2), ("out", W // 2), ("up", FF // 2), ("down", FF // 2), ("small", 176), ("bias", 16 * (FF // 2 // W))):
        rows[name] = at
        at += count
    rows["end"] = at
    return rows


def finish_kernel(pack_ref, qkv_ref, out_ref, up_ref, down_ref, vec_ref, bias_ref, time_ref, space_ref, sq_ref, *, W, FF, slots, patches):
    blocks = dec_blocks(W, FF)
    total = jnp.zeros((8, 128), F32)
    fold = lambda v: jnp.sum(jnp.sum((v * v).reshape(-1, 8, W), axis=0).reshape(8, W // 128, 128), axis=1)
    read = lambda name, at, n: pack_ref[blocks[name] + at:blocks[name] + at + n, :].astype(F32)
    g = read("qkv", 0, 3 * W // 2)
    qkv_ref[...] = g
    total += fold(g)
    g = read("out", 0, W // 2)
    out_ref[...] = g
    total += fold(g)
    for b in range(FF // 2 // W):
        g = read("up", b * W, W)
        up_ref[:, b * W:b * W + W] = g
        total += fold(g)
    for b in range(FF // W):
        g = read("down", b * (W // 2), W // 2)
        down_ref[:, b * W:b * W + W] = g
        total += fold(g)
    small = read("small", 0, 176)
    total += fold(small)
    vec_ref[...] = small[:9, :W // 2]
    time_ref[...] = small[16:16 + slots, :W // 2]
    space_ref[...] = small[16 + slots:16 + slots + patches, :W // 2]
    for b in range(FF // 2 // W):
        g = read("bias", 16 * b, 16)[:8]
        bias_ref[:, b * W:b * W + W] = g
        total += 0.125 * fold(g)
    sq_ref[...] = total


def finish_call(pack, W, FF, slots, patches):
    vm = pl.BlockSpec(memory_space=pltpu.VMEM)
    S = lambda *shape: jax.ShapeDtypeStruct(shape, F32)
    half = W // 2
    return pl.pallas_call(
        functools.partial(finish_kernel, W=W, FF=FF, slots=slots, patches=patches),
        in_specs=[vm],
        out_specs=[vm] * 9,
        out_shape=[S(3 * half, W), S(half, W), S(W, FF // 2), S(half, FF), S(9, half), S(8, FF // 2), S(slots, half), S(patches, half), S(8, 128)],
        compiler_params=pltpu.CompilerParams(vmem_limit_bytes=63 * 1024 * 1024),
        cost_estimate=pl.CostEstimate(flops=2_000_000, bytes_accessed=6_000_000, transcendentals=0),
        name="decoder_gradients",
    )(pack)


def dec_block_call(sec, frames, visible, proj, time_pos, space, vecs, wqkv, wo, w1, bias, w2, dy, TQ, TA):
    W, L, FF = wqkv.shape[0], dy.shape[1], w1.shape[1]
    H = W // 64
    patches, slots = space.shape[0], time_pos.shape[0]
    V = proj.shape[0]
    sm, vm = pl.BlockSpec(memory_space=pltpu.SMEM), pl.BlockSpec(memory_space=pltpu.VMEM)
    S = jax.ShapeDtypeStruct
    return pl.pallas_call(
        functools.partial(dec_kernel, W=W, L=L, H=H, FF=FF, V=V, slots=slots, patches=patches, TQ=TQ, TA=TA),
        in_specs=[sm, sm, sm] + [vm] * 9 + [pl.BlockSpec(memory_space=pl.ANY)],
        out_specs=[[vm] * 2, vm, [vm] * 2],
        out_shape=[[S((W // 2, L), BF)] * 2, S((V, W), BF), [S((dec_blocks(W, FF)["end"], W), BF)] * 2],
        scratch_shapes=[
            pltpu.VMEM((W, L), F32),
            pltpu.VMEM((W, L), BF),
            pltpu.VMEM((3 * W, L), BF),
            pltpu.VMEM((H, L, L), BF),
            pltpu.VMEM((H, 8, L), F32),
            pltpu.VMEM((W, L), BF),
            pltpu.VMEM((W, L), F32),
            pltpu.VMEM((W, L), BF),
            pltpu.VMEM((FF, L), BF),
            pltpu.VMEM((FF, L), BF),
            pltpu.VMEM((W, L), BF),
            pltpu.VMEM((W, L), BF),
            pltpu.VMEM((V + patches + 32, L), BF),
            pltpu.VMEM((80, L), BF),
            pltpu.VMEM((W, L), BF),
            pltpu.VMEM((W, L), F32),
            pltpu.VMEM((L, W), BF),
            pltpu.VMEM((W, 16), F32),
            pltpu.VMEM((FF, 1), F32),
            pltpu.VMEM((W, L), BF),
            pltpu.SemaphoreType.DMA,
        ],
        compiler_params=pltpu.CompilerParams(vmem_limit_bytes=63 * 1024 * 1024),
        cost_estimate=pl.CostEstimate(flops=28_000_000_000, bytes_accessed=12_000_000, transcendentals=10_000_000),
        name="decoder",
    )(sec, frames, visible, proj, time_pos, space, vecs, wqkv, wo, w1, bias, w2, dy)


VMEM = 63 * 1024 * 1024


def aligned(start, size):
    return pl.ds(pl.multiple_of(start, size), size)


def norm_r(x):
    mean = jnp.mean(x, axis=1, keepdims=True)
    c = x - mean
    r = lax.rsqrt(jnp.mean(c * c, axis=1, keepdims=True) + EPS)
    return c * r, r


def enc_probs(qm, k, valid):
    s = dot(qm, k, 1, 1)
    live = lax.broadcasted_iota(jnp.int32, s.shape, 1) < valid
    s = jnp.where(live, s, NEG)
    e = jnp.exp2(s - jnp.max(s, axis=1, keepdims=True))
    return e / jnp.sum(e, axis=1, keepdims=True)


def two_heads(v):
    low = lax.broadcasted_iota(jnp.int32, v.shape, 1) < 64
    zero = jnp.zeros_like(v)
    return jnp.concatenate([jnp.where(low, v, zero), jnp.where(low, zero, v)], axis=0)


def enc_fwd_kernel(sec_ref, frames_ref, tok_ref, vec_ref, b1_ref, wqkv_any, wo_any, w1_any, w2_any, wp_any,
                   acts_ref, qkv_ref, mid_ref, gp_ref, proj_ref,
                   wqkv_ref, wo_ref, w1_ref, w2_ref, wp_ref, sem, *, W, FF, seen):
    pairs = ((wqkv_any, wqkv_ref), (wo_any, wo_ref), (w1_any, w1_ref), (w2_any, w2_ref), (wp_any, wp_ref))
    copies = [pltpu.make_async_copy(a, b, sem.at[i]) for i, (a, b) in enumerate(pairs)]
    for c in copies:
        c.start()
    sec = sec_ref[0]
    valid = frames_ref[sec] // 2 * seen
    vec = vec_ref[...].astype(F32)
    row = lambda i: vec[i:i + 1, :]
    x = tok_ref[sec].astype(F32)
    n = x.shape[0]
    xh, _ = norm_r(x)
    a1 = (xh * row(0) + row(1)).astype(BF)
    acts_ref[:, :W] = a1
    copies[0].wait()
    j = dot(a1, wqkv_ref[...])
    qkv_ref[:, :W] = (j[:, :W] + row(2)).astype(BF)
    qkv_ref[:, W:2 * W] = j[:, W:2 * W].astype(BF)
    qkv_ref[:, 2 * W:] = (j[:, 2 * W:] + row(3)).astype(BF)
    for h in range(W // 128):
        s = slice(h * 128, h * 128 + 128)
        q = (qkv_ref[:, s].astype(F32) * (0.125 * LOG2E)).astype(BF)
        p = enc_probs(two_heads(q), qkv_ref[:, W + h * 128:W + h * 128 + 128], valid).astype(BF)
        v = two_heads(qkv_ref[:, 2 * W + h * 128:2 * W + h * 128 + 128])
        acts_ref[:, W + h * 128:W + h * 128 + 128] = (dot(p[:n], v[:n]) + dot(p[n:], v[n:])).astype(BF)
    copies[1].wait()
    mid = x + (dot(acts_ref[:, W:2 * W], wo_ref[...]) + row(4))
    mid_ref[...] = mid
    xh, _ = norm_r(mid)
    a2 = (xh * row(5) + row(6)).astype(BF)
    acts_ref[:, 2 * W:3 * W] = a2
    copies[2].wait()
    for f in range(0, FF, W):
        g, gp = gelu_pair(dot(a2, w1_ref[:, f:f + W]) + b1_ref[f:f + W].astype(F32).reshape(1, W))
        acts_ref[:, 3 * W + f:3 * W + f + W] = g.astype(BF)
        gp_ref[:, f:f + W] = gp.astype(BF)
    copies[3].wait()
    y = mid + (dot(acts_ref[:, 3 * W:3 * W + FF], w2_ref[...]) + row(7))
    enc = y.astype(BF)
    acts_ref[:, 3 * W + FF:] = enc
    copies[4].wait()
    proj_ref[...] = dot(enc, wp_ref[...])


def enc_fwd_call(sec, frames, seen, tokens, vec, b1, wqkv, wo, w1, w2, wp):
    n, W = tokens.shape[1], tokens.shape[2]
    FF = w1.shape[1]
    vm, hbm = pl.BlockSpec(memory_space=pltpu.VMEM), pl.BlockSpec(memory_space=pl.ANY)
    S = jax.ShapeDtypeStruct
    return pl.pallas_call(
        functools.partial(enc_fwd_kernel, W=W, FF=FF, seen=seen),
        in_specs=[pl.BlockSpec(memory_space=pltpu.SMEM)] * 2 + [vm] * 3 + [hbm] * 5,
        out_specs=[vm] * 5,
        out_shape=[S((n, 4 * W + FF), BF), S((n, 3 * W), BF), S((n, W), F32), S((n, FF), BF), S((n, wp.shape[1]), F32)],
        scratch_shapes=[pltpu.VMEM(w.shape, BF) for w in (wqkv, wo, w1, w2, wp)] + [pltpu.SemaphoreType.DMA((5,))],
        compiler_params=pltpu.CompilerParams(vmem_limit_bytes=VMEM),
        cost_estimate=pl.CostEstimate(flops=1_700_000_000, bytes_accessed=18_000_000, transcendentals=1_000_000),
        name="encoder_forward",
    )(sec, frames, tokens, vec, b1, wqkv, wo, w1, w2, wp)


def half_of(ref, start, size, s):
    return ref[:, pl.ds(pl.multiple_of(start + s * (size // 2), 128), size // 2)]


def enc_bwd_hidden_kernel(sec_ref, dz_ref, gp_ref, wp_any, w2_any, mine_ref, other_ref, full_ref, small_ref, wp_ref, w2_ref, sem, *, W, FF):
    copies = [pltpu.make_async_copy(a, b, sem.at[i]) for i, (a, b) in enumerate(((wp_any, wp_ref), (w2_any, w2_ref)))]
    for c in copies:
        c.start()
    sec = sec_ref[0]
    small_ref[...] = jnp.zeros_like(small_ref)
    copies[0].wait()
    de = dot(dz_ref[...], wp_ref[...], 1, 1).astype(BF)
    full_ref[:, :W] = de
    small_ref[7:8, :] = jnp.sum(de.astype(F32), axis=0, keepdims=True)
    copies[1].wait()
    for f in range(0, FF, W):
        duf = gp_ref[:, f:f + W].astype(F32) * dot(de, w2_ref[f:f + W, :], 1, 1)
        full_ref[:, W + f:2 * W + f] = duf.astype(BF)
        small_ref[8 + f // W:9 + f // W, :] = jnp.sum(duf, axis=0, keepdims=True)
    for ref, s in ((mine_ref, sec), (other_ref, 1 - sec)):
        ref[:, :W // 2] = half_of(full_ref, 0, W, s)
        ref[:, W // 2:] = half_of(full_ref, W, FF, s)


def enc_bwd_hidden_call(idx, dz, gp, wp, w2):
    n, FF = gp.shape
    W = w2.shape[1]
    vm, hbm = pl.BlockSpec(memory_space=pltpu.VMEM), pl.BlockSpec(memory_space=pl.ANY)
    S = jax.ShapeDtypeStruct
    return pl.pallas_call(
        functools.partial(enc_bwd_hidden_kernel, W=W, FF=FF),
        in_specs=[pl.BlockSpec(memory_space=pltpu.SMEM), vm, vm, hbm, hbm],
        out_specs=[vm] * 4,
        out_shape=[S((n, (W + FF) // 2), BF), S((n, (W + FF) // 2), BF), S((n, W + FF), BF), S((16, W), F32)],
        scratch_shapes=[pltpu.VMEM(w.shape, BF) for w in (wp, w2)] + [pltpu.SemaphoreType.DMA((2,))],
        compiler_params=pltpu.CompilerParams(vmem_limit_bytes=VMEM),
        cost_estimate=pl.CostEstimate(flops=600_000_000, bytes_accessed=8_000_000, transcendentals=0),
        name="encoder_backward_hidden",
    )(idx, dz, gp, wp, w2)


def enc_bwd_kernel(sec_ref, frames_ref, dz_ref, tok_ref, vec_ref, qkv_ref, mid_ref, du_ref, small_ref, w1_any, wo_any, wqkv_any,
                   mine_ref, other_ref, tok_mine_ref, tok_other_ref, w1_ref, wo_ref, wqkv_ref, full, tokg, small, sem, *, W, FF, seen):
    copies = [pltpu.make_async_copy(a, b, sem.at[i]) for i, (a, b) in enumerate(((w1_any, w1_ref), (wo_any, wo_ref), (wqkv_any, wqkv_ref)))]
    for c in copies:
        c.start()
    sec = sec_ref[0]
    valid = frames_ref[sec] // 2 * seen
    vec = vec_ref[...].astype(F32)
    row = lambda i: vec[i:i + 1, :]
    rsum = lambda v: jnp.sum(v, axis=0, keepdims=True)
    n = dz_ref.shape[0]
    small[...] = small_ref[...]
    def_ = du_ref[:, :W].astype(F32)
    copies[0].wait()
    da2 = dot(du_ref[:, W:], w1_ref[...], 1, 1)
    xh, r = norm_r(mid_ref[...])
    small[5:6, :] = rsum(da2 * xh)
    small[6:7, :] = rsum(da2)
    dg = da2 * row(5)
    dm = def_ + r * (dg - jnp.mean(dg, axis=1, keepdims=True) - xh * jnp.mean(dg * xh, axis=1, keepdims=True))
    small[4:5, :] = rsum(dm)
    db = dm.astype(BF)
    full[:, :W] = db
    copies[1].wait()
    do = dot(db, wo_ref[...], 1, 1).astype(BF)
    Q = W
    for h in range(W // 128):
        c = h * 128
        q = two_heads((qkv_ref[:, c:c + 128].astype(F32) * (0.125 * LOG2E)).astype(BF))
        k = qkv_ref[:, W + c:W + c + 128]
        v = qkv_ref[:, 2 * W + c:2 * W + c + 128]
        k2 = two_heads(k)
        do2 = two_heads(do[:, c:c + 128])
        p = enc_probs(q, k, valid)
        dp = dot(do2, v, 1, 1)
        ds = (p * (dp - jnp.sum(dp * p, axis=1, keepdims=True))).astype(BF)
        p16 = p.astype(BF)
        full[:, Q + c:Q + c + 128] = ((dot(ds[:n], k2[:n]) + dot(ds[n:], k2[n:])) * 0.125).astype(BF)
        full[:, Q + W + c:Q + W + c + 128] = (dot(ds, q, 0, 0) * LN2).astype(BF)
        full[:, Q + 2 * W + c:Q + 2 * W + c + 128] = dot(p16, do2, 0, 0).astype(BF)
    small[2:3, :] = rsum(full[:, Q:Q + W].astype(F32))
    small[3:4, :] = rsum(full[:, Q + 2 * W:Q + 3 * W].astype(F32))
    copies[2].wait()
    da = dot(full[:, Q:Q + 3 * W], wqkv_ref[...], 1, 1)
    xh, r = norm_r(tok_ref[sec].astype(F32))
    small[0:1, :] = rsum(da * xh)
    small[1:2, :] = rsum(da)
    dg = da * row(0)
    dx = dm + r * (dg - jnp.mean(dg, axis=1, keepdims=True) - xh * jnp.mean(dg * xh, axis=1, keepdims=True))
    tokg[...] = dx.astype(BF)
    half = W // 2
    for ref, tref, s in ((mine_ref, tok_mine_ref, sec), (other_ref, tok_other_ref, 1 - sec)):
        tref[...] = half_of(tokg, 0, W, s)
        ref[:n, :half] = half_of(full, 0, W, s)
        ref[:n, half:4 * half] = half_of(full, Q, 3 * W, s)
        ref[:n, 4 * half:] = dz_ref[...]
        ref[n:, :half] = half_of(small, 0, W, s).astype(BF)
        ref[n:, half:] = jnp.zeros((16, ref.shape[1] - half), BF)
        for t in range(FF // 2 // W):
            b = jnp.where(s == 0, small[8 + t:9 + t, :], small[8 + FF // 2 // W + t:9 + FF // 2 // W + t, :])
            ref[n + 8 + t:n + 9 + t, :W] = b.astype(BF)


def enc_bwd_call(sec, frames, seen, dz, tokens, vec, qkv, mid, du, small, w1, wo, wqkv):
    n, W = tokens.shape[1], tokens.shape[2]
    FF = w1.shape[1]
    vm, hbm = pl.BlockSpec(memory_space=pltpu.VMEM), pl.BlockSpec(memory_space=pl.ANY)
    S = jax.ShapeDtypeStruct
    width = 2 * W + dz.shape[1]
    return pl.pallas_call(
        functools.partial(enc_bwd_kernel, W=W, FF=FF, seen=seen),
        in_specs=[pl.BlockSpec(memory_space=pltpu.SMEM)] * 2 + [vm] * 7 + [hbm] * 3,
        out_specs=[vm] * 4,
        out_shape=[S((n + 16, width), BF), S((n + 16, width), BF), S((n, W // 2), BF), S((n, W // 2), BF)],
        scratch_shapes=[pltpu.VMEM(w.shape, BF) for w in (w1, wo, wqkv)]
        + [pltpu.VMEM((n, 4 * W), BF), pltpu.VMEM((n, W), BF), pltpu.VMEM((16, W), F32), pltpu.SemaphoreType.DMA((3,))],
        compiler_params=pltpu.CompilerParams(vmem_limit_bytes=VMEM),
        cost_estimate=pl.CostEstimate(flops=1_600_000_000, bytes_accessed=12_000_000, transcendentals=1_000_000),
        name="encoder_backward",
    )(sec, frames, dz, tokens, vec, qkv, mid, du, small, w1, wo, wqkv)


PIECES = 8


def flat_blocks(W, FF, WD):
    half = W // 2
    return ((("down", FF, half // 128),), (("up", W, FF // 2 // 128),), (("qkv", W, 3 * half // 128), ("out", W, half // 128), ("proj", WD // 2, W // 128)))


def flat_rows(part, W, FF, WD):
    rows = sum(r * b for _, r, b in flat_blocks(W, FF, WD)[part])
    if part == 2:
        rows += 8 * (W // 2 // 128) + FF // 2 // 128
    unit = PIECES * 16
    return -(-rows // unit) * unit


def weight_grad_kernel(idx_ref, acts_ref, came_ref, mine_ref, dcame_ref, give, keep, flat, acts, dy, dzt, small, sem, *, part, W, FF, WD):
    n = acts_ref.shape[0]
    half = W // 2
    lhs = {"qkv": (0, W), "out": (W, W), "up": (2 * W, W), "down": (3 * W, FF), "proj": (3 * W + FF, W)}
    cols = {"down": (0, half), "up": (half, FF // 2), "out": (0, half), "qkv": (half, 3 * half)}
    dy[:n, :] = mine_ref[:n, :]
    dy[n:, :] = dcame_ref[:n, :]
    at = 0
    step = 384
    for name, rows, blocks in flat_blocks(W, FF, WD)[part]:
        a0, an = lhs[name]
        acts[:n, :an] = acts_ref[:, a0:a0 + an]
        acts[n:, :an] = came_ref[:, a0:a0 + an]
        if name == "proj":
            dzt[...] = dy[:, 4 * half:4 * half + WD].T
            g = dot(dzt[pl.ds(pl.multiple_of(idx_ref[0] * (WD // 2), 16), WD // 2), :], acts[:, :an]).astype(BF)
            for b in range(blocks):
                flat[at:at + rows, :] = g[:, b * 128:b * 128 + 128]
                at += rows
            continue
        c0, cn = cols[name]
        for r in range(0, rows, W):
            lt = acts[:, r:r + W].T
            for c in range(0, cn, step):
                g = dot(lt, dy[:, c0 + c:c0 + c + step]).astype(BF)
                for b in range(step // 128):
                    o = at + (c // 128 + b) * rows + r
                    flat[o:o + W, :] = g[:, b * 128:b * 128 + 128]
        at += rows * blocks
    if part == 2:
        small[...] = mine_ref[n:, :W].astype(F32) + dcame_ref[n:, :W].astype(F32)
        for b in range(half // 128):
            flat[at:at + 8, :] = small[0:8, b * 128:b * 128 + 128].astype(BF)
            at += 8
        tail = flat.shape[0] - at
        bias = [small[8 + t:9 + t, b * 128:b * 128 + 128] for t in range(FF // 2 // W) for b in range(W // 128)]
        bias = jnp.concatenate(bias + [jnp.zeros((tail - len(bias), 128), F32)], axis=0)
        flat[at:, :] = bias.astype(BF)
    size = flat.shape[0] // PIECES
    me = idx_ref[1 + part]

    def send(p, k):
        src = lambda q: flat.at[pl.ds(pl.multiple_of((q ^ me) * size, 16), size), :]
        to = pl.ds(pl.multiple_of(p * size, 16), size)
        pltpu.make_async_copy(src(p), keep.at[to, :], sem).start()
        pltpu.make_async_copy(src(p + PIECES // 2), give.at[to, :], sem).start()
        return k

    lax.fori_loop(0, PIECES // 2, send, 0)
    pltpu.make_async_copy(flat, flat, sem).wait()


def weight_grad_call(part, idx, acts, came, mine, dcame, W, FF, WD):
    n = acts.shape[0]
    rows = flat_rows(part, W, FF, WD)
    vm, hbm = pl.BlockSpec(memory_space=pltpu.VMEM), pl.BlockSpec(memory_space=pl.ANY)
    S = jax.ShapeDtypeStruct
    return pl.pallas_call(
        functools.partial(weight_grad_kernel, part=part, W=W, FF=FF, WD=WD),
        in_specs=[pl.BlockSpec(memory_space=pltpu.SMEM)] + [vm] * 4,
        out_specs=[hbm] * 2,
        out_shape=[S((rows // 2, 128), BF)] * 2,
        scratch_shapes=[pltpu.VMEM((rows, 128), BF), pltpu.VMEM((2 * n, FF if part == 0 else W), BF), pltpu.VMEM((2 * n, mine.shape[1]), BF),
                        pltpu.VMEM((WD, 2 * n), BF), pltpu.VMEM((16, W), F32), pltpu.SemaphoreType.DMA],
        compiler_params=pltpu.CompilerParams(vmem_limit_bytes=VMEM),
        cost_estimate=pl.CostEstimate(flops=600_000_000, bytes_accessed=8_000_000, transcendentals=0),
        name=("gradient_down", "gradient_up", "gradient_qkv_out_proj")[part],
    )(idx, acts, came, mine, dcame)


def unpack_kernel(idx_ref, own0, own1, own2, came0, came1, came2, dec_mine, dec_came, tok_mine, tok_came, vec_ref, qkv_ref, out_ref, up_ref, bias_ref, down_ref, proj_ref, sq_ref, dec_ref, tok_ref,
                  flat0, flat1, flat2, sem, *, W, FF, WD):
    sec = idx_ref[0]
    flats = (flat0, flat1, flat2)
    for i, (own, came) in enumerate(((own0, came0), (own1, came1), (own2, came2))):
        me = idx_ref[1 + i]
        size = flats[i].shape[0] // PIECES

        def fetch(p, k, own=own, came=came, me=me, flat=flats[i], size=size, i=i):
            to = lambda q: flat.at[pl.ds(pl.multiple_of((q ^ me) * size, 16), size), :]
            src = pl.ds(pl.multiple_of(p * size, 16), size)
            pltpu.make_async_copy(own.at[src, :], to(p), sem.at[i]).start()
            pltpu.make_async_copy(came.at[src, :], to(p + PIECES // 2), sem.at[i]).start()
            return k

        lax.fori_loop(0, PIECES // 2, fetch, 0)
    for ref, mine, came in ((dec_ref, dec_mine, dec_came), (tok_ref, tok_mine, tok_came)):
        ref[sec] = mine[...]
        ref[1 - sec] = came[...]
    refs = {"qkv": qkv_ref, "out": out_ref, "up": up_ref, "down": down_ref}
    enc = jnp.zeros((8, 128), F32)
    dec = jnp.zeros((8, 128), F32)
    fold = lambda v: jnp.sum((v * v).reshape(-1, 8, 128), axis=0)
    for part, flat in enumerate(flats):
        pltpu.make_async_copy(flat, flat, sem.at[part]).wait()
        at = 0
        for name, rows, blocks in flat_blocks(W, FF, WD)[part]:
            for b in range(blocks):
                g = flat[at:at + rows, :].astype(F32)
                if name == "proj":
                    dec += fold(g)
                    proj_ref[:, b * 128:b * 128 + 128] = g
                else:
                    enc += fold(g)
                    refs[name][:, b * 128:b * 128 + 128] = g
                at += rows
    for b in range(W // 2 // 128):
        g = flat2[at:at + 8, :].astype(F32)
        enc += g * g
        vec_ref[:, b * 128:b * 128 + 128] = g
        at += 8
    g = flat2[at:at + 16, :].astype(F32)[:FF // 2 // 128]
    bias_ref[...] = g
    enc += jnp.concatenate([jnp.sum(g * g, axis=0, keepdims=True), jnp.zeros((7, 128), F32)], axis=0)
    sq_ref[:8, :] = enc
    sq_ref[8:, :] = dec


def unpack_call(idx, own, came, dec_mine, dec_came, tok_mine, tok_came, W, FF, WD):
    vm, hbm = pl.BlockSpec(memory_space=pltpu.VMEM), pl.BlockSpec(memory_space=pl.ANY)
    S = jax.ShapeDtypeStruct
    half = W // 2
    return pl.pallas_call(
        functools.partial(unpack_kernel, W=W, FF=FF, WD=WD),
        in_specs=[pl.BlockSpec(memory_space=pltpu.SMEM)] + [hbm] * 6 + [vm] * 4,
        out_specs=[vm] * 10,
        out_shape=[S((8, half), F32), S((W, 3 * half), F32), S((W, half), F32), S((W, FF // 2), F32), S((FF // 2 // 128, 128), F32),
                   S((FF, half), F32), S((WD // 2, W), F32), S((16, 128), F32), S((2, *dec_mine.shape), BF), S((2, *tok_mine.shape), BF)],
        scratch_shapes=[pltpu.VMEM((flat_rows(i, W, FF, WD), 128), BF) for i in range(3)] + [pltpu.SemaphoreType.DMA((3,))],
        compiler_params=pltpu.CompilerParams(vmem_limit_bytes=VMEM),
        cost_estimate=pl.CostEstimate(flops=10_000_000, bytes_accessed=23_000_000, transcendentals=0),
        name="unpack",
    )(idx, *own, *came, dec_mine, dec_came, tok_mine, tok_came)


SIDE = 4


def coordinates(index):
    return (index // (SIDE * SIDE), index // SIDE % SIDE, index % SIDE)


def flip(place, axis, kind):
    place = list(place)
    place[axis] = place[axis] ^ 1 if kind == 0 else SIDE - 1 - place[axis]
    return tuple(place)


def swap(value, axes, far):
    pairs = []
    for core in range(2):
        for index in range(SIDE**3):
            place = coordinates(index)
            for axis in axes:
                place = flip(place, axis, core ^ far)
            target = (place[0] * SIDE + place[1]) * SIDE + place[2]
            pairs.append((core * SIDE**3 + index, core * SIDE**3 + target))
    return lax.ppermute(value, ("section", "dp"), pairs)


def add(left, right):
    return (left.astype(jnp.float32) + right.astype(jnp.float32)).astype(jnp.bfloat16)


def piece_numbers():
    place = coordinates(lax.axis_index("dp"))
    near = [((p == 1) | (p == 2)).astype(jnp.int32) for p in place]
    far = [(p >= 2).astype(jnp.int32) for p in place]
    core = lax.axis_index("section")
    bits = [jnp.where(core == 0, a, b) for a, b in zip(near, far)]
    return [bits[i] * 4 + bits[(i + 1) % 3] * 2 + bits[(i + 2) % 3] for i in range(3)]


def reduce_part(i, give, keep):
    v = add(keep, swap(give, (i,), 0))
    for step in (1, 2):
        half = v.shape[0] // 2
        v = add(v[:half], swap(v[half:], ((i + step) % 3,), 0))
    for step in range(3):
        v = add(v, swap(v, ((i + step) % 3,), 1))
    return v


def gather_part(i, v):
    for step in (2, 1):
        v = jnp.concatenate([v, swap(v, ((i + step) % 3,), 0)])
    return (v, swap(v, (i,), 0))


def from_partner(value):
    return lax.ppermute(value, "section", [(0, 1), (1, 0)])


def shards(
    tokens,
    frames,
    visible,
    out_grad,
    enc_vectors,
    enc_qkv,
    enc_out,
    enc_up,
    enc_up_bias,
    enc_down,
    proj_weight,
    dec_vectors,
    dec_qkv,
    dec_out,
    dec_up,
    dec_up_bias,
    dec_down,
    time_pos,
    space_pos,
):
    enc_width, enc_hidden = enc_up.shape
    dec_width, dec_hidden = dec_up.shape
    slot_count = time_pos.shape[0]
    patch_count = space_pos.shape[0]
    seen_count = visible.shape[1]
    section = lax.axis_index("section").astype(jnp.int32)
    core = section.reshape(1)
    sizes = (enc_width, enc_hidden, dec_width)
    acts, qkv, mid, slopes, projected = enc_fwd_call(
        core, frames, seen_count, tokens, enc_vectors, enc_up_bias, enc_qkv, enc_out, enc_up, enc_down, proj_weight
    )
    acts_came = from_partner(acts)
    (decoded_mine, decoded_other), grad_projected, (dec_mine, dec_other) = dec_block_call(
        core,
        frames,
        visible,
        projected,
        time_pos,
        space_pos,
        dec_vectors,
        dec_qkv,
        dec_out,
        dec_up,
        dec_up_bias,
        dec_down,
        out_grad,
        TQ=384,
        TA=640,
    )
    dec_came = from_partner(dec_other)
    hidden_mine, hidden_other, hidden, small_sums = enc_bwd_hidden_call(core, grad_projected, slopes, proj_weight, enc_down)
    hidden_came = from_partner(hidden_other)
    dec_local = add(dec_mine, dec_came)
    dec_sum = lax.psum(dec_local, "dp")
    decoded_came = from_partner(decoded_other)
    places = jnp.stack([section, *piece_numbers()]).astype(jnp.int32)
    places, dec_local = lax.optimization_barrier((places, dec_local))
    parts = [weight_grad_call(i, places, acts, acts_came, hidden_mine, hidden_came, *sizes) for i in range(2)]
    dy_mine, dy_other, token_mine, token_other = enc_bwd_call(
        core, frames, seen_count, grad_projected, tokens, enc_vectors, qkv, mid, hidden, small_sums, enc_up, enc_out, enc_qkv
    )
    dy_came = from_partner(dy_other)
    token_came = from_partner(token_other)
    parts.append(weight_grad_call(2, places, acts, acts_came, dy_mine, dy_came, *sizes))
    parts = [reduce_part(i, give, keep) for i, (give, keep) in enumerate(parts)]
    own, came = zip(*(gather_part(i, v) for i, v in enumerate(parts)))
    g_vectors, g_enc_qkv, g_enc_out, g_enc_up, g_enc_bias, g_enc_down, g_proj, squares, decoded, token_grad = unpack_call(
        places, own, came, decoded_mine, decoded_came, token_mine, token_came, *sizes
    )
    g_dec_qkv, g_dec_out, g_dec_up, g_dec_down, g_dec_vectors, g_dec_bias, g_time, g_space, dec_squares = finish_call(
        dec_sum, dec_width, dec_hidden, slot_count, patch_count
    )
    norms = jnp.stack([jnp.sum(squares[:8]), jnp.sum(squares[8:]) + jnp.sum(dec_squares)])
    norms = norms + from_partner(norms)
    return (
        decoded.transpose(0, 2, 1),
        token_grad,
        g_vectors,
        g_enc_qkv,
        g_enc_out,
        g_enc_up,
        g_enc_bias.reshape(-1),
        g_enc_down,
        g_proj.T,
        g_dec_vectors,
        g_dec_qkv.T,
        g_dec_out.T,
        g_dec_up,
        g_dec_bias[0],
        g_dec_down.T,
        g_time,
        g_space,
        lax.dynamic_slice_in_dim(norms, section, 1, 0),
    )


from jax.sharding import PartitionSpec as P


def solution(mesh):
    placed = (
        P("dp", None, None),
        P("dp"),
        P("dp", None),
        P("dp", None, None),
        P(),
        P(),
        P(),
        P(),
        P(),
        P(),
        P(),
        P(),
        P(),
        P(),
        P(),
        P(),
        P(),
        P(),
        P(),
    )
    return jax.shard_map(
        shards,
        mesh=mesh,
        in_specs=placed,
        out_specs=(
            P("dp", None, "section"),
            P("dp", None, "section"),
            P(None, "section"),
            P(None, "section"),
            P(None, "section"),
            P(None, "section"),
            P("section"),
            P(None, "section"),
            P(None, "section"),
            P(None, "section"),
            P(None, "section"),
            P(None, "section"),
            P(None, "section"),
            P("section"),
            P(None, "section"),
            P(None, "section"),
            P(None, "section"),
            P("section"),
        ),
        check_vma=False,
    )
```

```python
import functools
import jax, jax.numpy as jnp, numpy as np
from jax import lax
from jax.experimental import pallas as pl
from jax.experimental.pallas import tpu as pltpu

EPS = 1e-6
NEG = -1e9
LOG2E = 1.4426950408889634
LN2 = 0.6931471805599453
F32, BF = jnp.float32, jnp.bfloat16


def dot(a, b, ca=1, cb=0):
    return lax.dot_general(a, b, (((ca,), (cb,)), ((), ())), preferred_element_type=F32)


def tiles_of(total, size):
    return [(s, min(size, total - s)) for s in range(0, total, size)]


def over(total, size, body, carry):
    full = total // size
    if full:
        carry = lax.fori_loop(0, full, lambda i, k: body(pl.ds(pl.multiple_of(i * size, 128), size), size, k), carry)
    if total % size:
        carry = body(pl.ds(full * size, total % size), total % size, carry)
    return carry


def norm_c(x):
    mean = jnp.mean(x, axis=0, keepdims=True)
    c = x - mean
    r = lax.rsqrt(jnp.mean(c * c, axis=0, keepdims=True) + EPS)
    return c * r, r


def gelu_pair(u):
    a = jnp.abs(u)
    t = 1.0 / (1.0 + (0.3275911 * 0.7071067811865476) * a)
    e = jnp.exp2((-0.5 * LOG2E) * (u * u))
    poly = t * (0.5 * 0.254829592 + t * (0.5 * -0.284496736 + t * (0.5 * 1.421413741 + t * (0.5 * -1.453152027 + t * (0.5 * 1.061405429)))))
    tail = poly * e
    phi = jnp.where(u >= 0, 1.0 - tail, tail)
    return u * phi, phi + u * (e * 0.3989422804014327)


def dec_kernel(sec_ref, frames_ref, vis_ref, proj_ref, time_ref, space_ref, vecs_ref, wqkv_ref, wo_ref, w1_ref, bias_ref, w2_ref, dy_any,
               out_refs, dz_ref, pack_refs,
               x_s, a1_s, qkv_s, e_s, l_s, o_s, m_s, a2_s, g_s, gp_s, dy_s, db_s, sel_s, doa_s, do_s, o32_s, dy_ref, vec_ref, b1_ref, dec_s, dy_sem, *, W, L, H, FF, V, slots, patches, TQ, TA):
    dqkv_s, ds_s = g_s, gp_s
    sec = sec_ref[0]
    used = frames_ref[sec] // 2
    valid = used * patches
    dy_copy = pltpu.make_async_copy(dy_any.at[sec], dy_ref, dy_sem)
    dy_copy.start()
    seen_count = V // slots
    vecs = vecs_ref[...].astype(F32)
    vec_ref[...] = jnp.concatenate([vecs, jnp.zeros((16 - vecs.shape[0], W), F32)], axis=0).T
    b1_ref[...] = jnp.broadcast_to(bias_ref[...].reshape(1, FF).astype(F32), (8, FF)).T[:, 0:1]
    col = lambda i: vec_ref[:, i:i + 1]
    HS = 64
    lane = lax.broadcasted_iota(jnp.int32, (1, L), 1)
    vrow = lax.broadcasted_iota(jnp.int32, (V, 1), 0)
    vslot = jnp.zeros((V, 1), jnp.int32)
    for t in range(1, slots):
        vslot += (vrow >= t * seen_count).astype(jnp.int32)
    vrank = vrow - vslot * seen_count
    target = vslot * patches
    for j in range(seen_count):
        target += jnp.where(vrank == j, vis_ref[sec, j], 0)
    onehot = (target == lax.broadcasted_iota(jnp.int32, (V, L), 1)).astype(F32)
    slot = jnp.zeros((1, L), jnp.int32)
    for t in range(1, slots):
        slot += (lane >= t * patches).astype(jnp.int32)
    patch_oh = (lax.broadcasted_iota(jnp.int32, (patches, L), 0) == lane - slot * patches).astype(BF)
    seen = jnp.sum(onehot, axis=0, keepdims=True)
    srow = lax.broadcasted_iota(jnp.int32, (32, L), 0)
    slot_oh = jnp.where(srow < 16, ((srow & 7) == slot).astype(F32), jnp.where(srow == 16, 1.0 - seen, 0.0)).astype(BF)
    sel_s[:V, :] = onehot.astype(BF)
    sel_s[V:V + patches, :] = patch_oh
    sel_s[V + patches:, :] = slot_oh
    ti = lax.broadcasted_iota(jnp.int32, (slots, slots), 0)
    ii = lax.broadcasted_iota(jnp.int32, (slots, slots), 1)
    num = ti * (slots - 1)
    lower = jnp.zeros((slots, slots), jnp.int32)
    for q in range(1, (slots - 1) * (slots - 1) + 1):
        lower += (num >= q * (used - 1)).astype(jnp.int32)
    frac = (num - lower * (used - 1)).astype(F32) / jnp.full((slots, slots), used - 1, jnp.int32).astype(F32)
    upper = jnp.minimum(lower + 1, slots - 1)
    table = (1.0 - frac) * (ii == lower).astype(F32) + frac * (ii == upper).astype(F32)
    exact = lambda a, b, ca, cb: lax.dot_general(a, b, (((ca,), (cb,)), ((), ())), precision=lax.Precision.HIGHEST, preferred_element_type=F32)
    spos = exact(table, time_ref[...].astype(F32), 1, 0)
    shi = spos.astype(BF)
    slo = (spos - shi.astype(F32)).astype(BF)
    proj = proj_ref[...]
    hi = proj.astype(BF)
    lo = (proj - hi.astype(F32)).astype(BF)
    mask = vecs[8:9, :].astype(BF)
    src = jnp.concatenate([hi.astype(F32), space_ref[...].astype(F32), shi.astype(F32), slo.astype(F32), mask.astype(F32), jnp.zeros((15, W), F32)], axis=0).astype(BF)

    def first(c, n, k):
        x = dot(src, sel_s[:, c], 0, 0) + dot(lo, sel_s[:V, c], 0, 0)
        x_s[:, c] = x
        xh, _ = norm_c(x)
        a1 = (xh * col(0) + col(1)).astype(BF)
        a1_s[:, c] = a1
        j = dot(wqkv_ref[...], a1, 0, 0)
        qkv_s[:W, c] = ((j[:W] + col(2)) * (0.125 * LOG2E)).astype(BF)
        qkv_s[W:2 * W, c] = j[W:2 * W].astype(BF)
        qkv_s[2 * W:, c] = (j[2 * W:] + col(3)).astype(BF)
        return k

    over(L, TQ, first, 0)
    arow = lax.broadcasted_iota(jnp.int32, (16, L), 0)
    kbias = jnp.where((arow == 0) & (lane >= valid), NEG, 0.0).astype(BF)
    one0 = (arow == 0).astype(BF)
    one01 = (arow < 2).astype(BF)

    def fwd_head(h, carry):
        hs = pl.ds(pl.multiple_of(h * HS, HS), HS)
        ks = pl.ds(pl.multiple_of(W + h * HS, HS), HS)
        vs = pl.ds(pl.multiple_of(2 * W + h * HS, HS), HS)
        kr = jnp.concatenate([qkv_s[ks, :], kbias], axis=0).T
        vc = jnp.concatenate([qkv_s[vs, :], one0], axis=0)

        def tile(c, n, exact):
            qc = jnp.concatenate([qkv_s[hs, c], one0[:, :n]], axis=0)
            st = dot(kr, qc)
            if exact:
                st = st - jnp.max(st, axis=0, keepdims=True)
            e = jnp.exp2(st).astype(BF)
            e_s[h, :, c] = e
            oa = dot(vc, e)
            rl = 1.0 / oa[HS:HS + 1]
            l_s[h, :, c] = jnp.broadcast_to(rl, (8, n))
            o = oa[:HS] * rl
            o32_s[hs, c] = o
            o_s[hs, c] = o.astype(BF)

        square = lambda v: jnp.max(jnp.sum(v * v, axis=0))
        bound = square(qkv_s[hs, :].astype(F32)) * square(qkv_s[ks, :].astype(F32))

        @pl.when(bound <= 60.0 * 60.0)
        def _():
            over(L, TA, lambda c, n, k: (tile(c, n, False), k)[1], 0)

        @pl.when(jnp.logical_not(bound <= 60.0 * 60.0))
        def _():
            over(L, TA, lambda c, n, k: (tile(c, n, True), k)[1], 0)

        return carry

    lax.fori_loop(0, H, fwd_head, 0)

    def middle(c, n, sums):
        sum_b1, sum_dy, sum_g2, sum_s2, sum_db = sums
        live = (lax.broadcasted_iota(jnp.int32, (1, n), 1) + c.start < valid).astype(F32)
        mid = x_s[:, c] + (dot(wo_ref[...], o_s[:, c], 0, 0) + col(4))
        xh, r = norm_c(mid)
        a2 = (xh * col(5) + col(6)).astype(BF)
        a2_s[:, c] = a2
        u = dot(w1_ref[...], a2, 0, 0) + b1_ref[...]
        g, gp = gelu_pair(u)
        g = g.astype(BF)
        g_s[:, c] = g
        y = mid + (dot(w2_ref[...], g, 0, 0) + col(7))
        dec_s[:, c] = (y * live).astype(BF)
        dyf = dy_ref[c, :].astype(F32).T * live
        dy = dyf.astype(BF)
        dy_s[:, c] = dy
        duf = gp * dot(w2_ref[...], dy)
        du = duf.astype(BF)
        gp_s[:, c] = du
        da2 = dot(w1_ref[...], du)
        dg = da2 * col(5)
        dm = dyf + r * (dg - jnp.mean(dg, axis=0, keepdims=True) - xh * jnp.mean(dg * xh, axis=0, keepdims=True))
        db = dm.astype(BF)
        db_s[:, c] = db
        do_s[:, c] = dot(wo_ref[...], db).astype(BF)
        m_s[:, c] = dm
        rs = lambda v: jnp.sum(v, axis=1, keepdims=True)
        return (sum_b1 + rs(duf), sum_dy + rs(dyf), sum_g2 + rs(da2 * xh), sum_s2 + rs(da2), sum_db + rs(dm))

    dy_copy.wait()
    zero = jnp.zeros((W, 1), F32)
    sum_b1, sum_dy, sum_g2, sum_s2, sum_db = over(L, TQ, middle, (jnp.zeros((FF, 1), F32), zero, zero, zero, zero))
    blocks = dec_blocks(W, FF)
    for who, s in enumerate((sec, 1 - sec)):
        rows = lambda size, at=0: pl.ds(pl.multiple_of(s * (size // 2) + at, 16), W // 2)
        out_refs[who][...] = dec_s[rows(W), :]
        pack = pack_refs[who]
        for b in range(FF // W):
            put(pack, blocks["down"] + b * 3 * (W // 2), dot(dy_s[rows(W), :], g_s[b * W:b * W + W, :], 1, 1))
        for b in range(FF // 2 // W):
            put(pack, blocks["up"] + b * 3 * W, dot(a2_s[...], gp_s[pl.ds(pl.multiple_of(s * (FF // 2) + b * W, 16), W), :], 1, 1))
        put(pack, blocks["out"], dot(db_s[rows(W), :], o_s[...], 1, 1))

    def bwd_head(h, carry):
        hs = pl.ds(pl.multiple_of(h * HS, HS), HS)
        ks = pl.ds(pl.multiple_of(W + h * HS, HS), HS)
        vs = pl.ds(pl.multiple_of(2 * W + h * HS, HS), HS)
        vr = jnp.concatenate([qkv_s[vs, :], one01], axis=0).T
        kc = qkv_s[ks, :]
        dob = (do_s[hs, :].astype(F32) * l_s[h, 0:1, :]).astype(BF)
        dl = -jnp.sum(dob.astype(F32) * o32_s[hs, :], axis=0, keepdims=True)
        dlh = dl.astype(BF).astype(F32)
        doa_s[:HS, :] = dob
        doa_s[HS:, :] = jnp.where(arow == 0, dlh, jnp.where(arow == 1, dl - dlh, 0.0)).astype(BF)
        def tile(c, n, k):
            dp = dot(vr, doa_s[:, c])
            ds = (e_s[h, :, c].astype(F32) * dp).astype(BF)
            ds_s[:L, c] = ds
            dqkv_s[hs, c] = (dot(kc, ds) * 0.125).astype(BF)
            return k

        over(L, TA, tile, 0)
        dor = doa_s[:HS, :].T
        qr = qkv_s[hs, :].T

        def tile2(c, n, k):
            dqkv_s[vs, c] = dot(e_s[h, c, :], dor).T.astype(BF)
            dqkv_s[ks, c] = (dot(ds_s[c, :], qr) * LN2).T.astype(BF)
            return k

        return over(L, TA, tile2, carry)

    lax.fori_loop(0, H, bwd_head, 0)
    def last(c, n, sums):
        sum_g1, sum_s1, sum_q, sum_v, gsel = sums
        rs = lambda v: jnp.sum(v, axis=1, keepdims=True)
        da = dot(wqkv_ref[...], dqkv_s[:3 * W, c])
        xh, r = norm_c(x_s[:, c])
        dg = da * col(0)
        dx = m_s[:, c] + r * (dg - jnp.mean(dg, axis=0, keepdims=True) - xh * jnp.mean(dg * xh, axis=0, keepdims=True))
        return (sum_g1 + rs(da * xh), sum_s1 + rs(da), sum_q + rs(dqkv_s[:W, c].astype(F32)), sum_v + rs(dqkv_s[2 * W:3 * W, c].astype(F32)),
                gsel + dot(dx.astype(BF), sel_s[:, c], 1, 1))

    sum_g1, sum_s1, sum_q, sum_v, gsel = over(L, TQ, last, (zero, zero, zero, zero, jnp.zeros((W, sel_s.shape[0]), F32)))
    dz_ref[...] = gsel[:, :V].T.astype(BF)
    small = o32_s
    small[:, :8] = jnp.concatenate([sum_g1, sum_s1, sum_q, sum_v, sum_db, sum_g2, sum_s2, sum_dy], axis=1)
    small[:, 8:16] = gsel[:, V + patches + 16:V + patches + 24]
    small[:, 16:24] = exact(gsel[:, V + patches:V + patches + slots], table, 1, 0)
    small[:, 24:24 + patches] = gsel[:, V:V + patches]
    small[:, 24 + patches:256] = jnp.zeros((W, 256 - 24 - patches), F32)
    for who, s in enumerate((sec, 1 - sec)):
        pack = pack_refs[who]
        put(pack, blocks["qkv"], dot(dqkv_s[pl.ds(pl.multiple_of(s * (3 * W // 2), 16), 3 * W // 2), :], a1_s[...], 1, 1))
        half = small[pl.ds(pl.multiple_of(s * (W // 2), 8), W // 2), :256].T[:32 + patches]
        put(pack, blocks["small"], jnp.concatenate([half, jnp.zeros((32 + patches, 256 - W // 2), F32)], axis=1))
        b1_ref[...] = sum_b1
        put(pack, blocks["bias"], jnp.broadcast_to(b1_ref[pl.ds(pl.multiple_of(s * (FF // 2), 8), FF // 2), :], (FF // 2, 128)).T[:16])
        pack[blocks["end"]:, :] = jnp.zeros((pack.shape[0] - blocks["end"], 128), BF)


def put(pack, at, value):
    n = value.shape[0]
    for b in range(value.shape[1] // 128):
        pack[at + b * n:at + b * n + n, :] = value[:, b * 128:b * 128 + 128].astype(BF)


def dec_blocks(W, FF):
    at, rows = 0, {}
    for name, count in (("qkv", 3 * (3 * W // 2)), ("out", 3 * (W // 2)), ("up", 3 * (FF // 2)), ("down", 3 * (FF // 2)), ("small", 2 * 176), ("bias", 16 * (FF // 2 // 128))):
        rows[name] = at
        at += count
    rows["end"] = at
    unit = 3 * 8 * 16
    rows["all"] = -(-at // unit) * unit
    return rows


def finish(read, qkv_ref, out_ref, up_ref, down_ref, vec_ref, bias_ref, time_ref, space_ref, *, W, FF, slots, patches):
    blocks = dec_blocks(W, FF)
    total = jnp.zeros((8, 128), F32)
    fold = lambda v: jnp.sum((v * v).reshape(-1, 8, 128), axis=0)
    for name, ref, n, parts in (("qkv", qkv_ref, 3 * W // 2, 1), ("out", out_ref, W // 2, 1), ("up", up_ref, W, FF // 2 // W), ("down", down_ref, W // 2, FF // W)):
        for b in range(3 * parts):
            g = read(blocks[name] + b * n, n).astype(F32)
            ref[:, b * 128:b * 128 + 128] = g
            total += fold(g)
    low = read(blocks["small"], 176).astype(F32)
    high = read(blocks["small"] + 176, 176).astype(F32)
    total += fold(low) + fold(high)
    for ref, at, n in ((vec_ref, 0, 9), (time_ref, 16, slots), (space_ref, 16 + slots, patches)):
        ref[:, :128] = low[at:at + n]
        ref[:, 128:] = high[at:at + n, :W // 2 - 128]
    for b in range(FF // 2 // 128):
        g = read(blocks["bias"] + 16 * b, 16).astype(F32)
        bias_ref[:, b * 128:b * 128 + 128] = g[:8]
        total += 0.0625 * fold(g)
    return total


def dec_block_call(sec, frames, visible, proj, time_pos, space, vecs, wqkv, wo, w1, bias, w2, dy, TQ, TA):
    W, L, FF = wqkv.shape[0], dy.shape[1], w1.shape[1]
    H = W // 64
    patches, slots = space.shape[0], time_pos.shape[0]
    V = proj.shape[0]
    sm, vm = pl.BlockSpec(memory_space=pltpu.SMEM), pl.BlockSpec(memory_space=pltpu.VMEM)
    S = jax.ShapeDtypeStruct
    return pl.pallas_call(
        functools.partial(dec_kernel, W=W, L=L, H=H, FF=FF, V=V, slots=slots, patches=patches, TQ=TQ, TA=TA),
        in_specs=[sm, sm, sm] + [vm] * 9 + [pl.BlockSpec(memory_space=pl.ANY)],
        out_specs=[[vm] * 2, vm, [vm] * 2],
        out_shape=[[S((W // 2, L), BF)] * 2, S((V, W), BF), [S((dec_blocks(W, FF)["all"], 128), BF)] * 2],
        scratch_shapes=[
            pltpu.VMEM((W, L), F32),
            pltpu.VMEM((W, L), BF),
            pltpu.VMEM((3 * W, L), BF),
            pltpu.VMEM((H, L, L), BF),
            pltpu.VMEM((H, 8, L), F32),
            pltpu.VMEM((W, L), BF),
            pltpu.VMEM((W, L), F32),
            pltpu.VMEM((W, L), BF),
            pltpu.VMEM((FF, L), BF),
            pltpu.VMEM((FF, L), BF),
            pltpu.VMEM((W, L), BF),
            pltpu.VMEM((W, L), BF),
            pltpu.VMEM((V + patches + 32, L), BF),
            pltpu.VMEM((80, L), BF),
            pltpu.VMEM((W, L), BF),
            pltpu.VMEM((W, L), F32),
            pltpu.VMEM((L, W), BF),
            pltpu.VMEM((W, 16), F32),
            pltpu.VMEM((FF, 1), F32),
            pltpu.VMEM((W, L), BF),
            pltpu.SemaphoreType.DMA,
        ],
        compiler_params=pltpu.CompilerParams(vmem_limit_bytes=63 * 1024 * 1024),
        cost_estimate=pl.CostEstimate(flops=28_000_000_000, bytes_accessed=12_000_000, transcendentals=10_000_000),
        name="decoder",
    )(sec, frames, visible, proj, time_pos, space, vecs, wqkv, wo, w1, bias, w2, dy)


VMEM = 63 * 1024 * 1024


def aligned(start, size):
    return pl.ds(pl.multiple_of(start, size), size)


def norm_r(x):
    mean = jnp.mean(x, axis=1, keepdims=True)
    c = x - mean
    r = lax.rsqrt(jnp.mean(c * c, axis=1, keepdims=True) + EPS)
    return c * r, r


def enc_probs(qm, k, valid):
    s = dot(qm, k, 1, 1)
    live = lax.broadcasted_iota(jnp.int32, s.shape, 1) < valid
    s = jnp.where(live, s, NEG)
    e = jnp.exp2(s - jnp.max(s, axis=1, keepdims=True))
    return e / jnp.sum(e, axis=1, keepdims=True)


def two_heads(v):
    low = lax.broadcasted_iota(jnp.int32, v.shape, 1) < 64
    zero = jnp.zeros_like(v)
    return jnp.concatenate([jnp.where(low, v, zero), jnp.where(low, zero, v)], axis=0)


def enc_fwd_kernel(sec_ref, frames_ref, tok_ref, vec_ref, b1_ref, wqkv_any, wo_any, w1_any, w2_any, wp_any,
                   acts_ref, qkv_ref, mid_ref, gp_ref, proj_ref,
                   wqkv_ref, wo_ref, w1_ref, w2_ref, wp_ref, sem, *, W, FF, seen):
    pairs = ((wqkv_any, wqkv_ref), (wo_any, wo_ref), (w1_any, w1_ref), (w2_any, w2_ref), (wp_any, wp_ref))
    copies = [pltpu.make_async_copy(a, b, sem.at[i]) for i, (a, b) in enumerate(pairs)]
    for c in copies:
        c.start()
    sec = sec_ref[0]
    valid = frames_ref[sec] // 2 * seen
    vec = vec_ref[...].astype(F32)
    row = lambda i: vec[i:i + 1, :]
    x = tok_ref[sec].astype(F32)
    n = x.shape[0]
    xh, _ = norm_r(x)
    a1 = (xh * row(0) + row(1)).astype(BF)
    acts_ref[:, :W] = a1
    copies[0].wait()
    j = dot(a1, wqkv_ref[...])
    qkv_ref[:, :W] = (j[:, :W] + row(2)).astype(BF)
    qkv_ref[:, W:2 * W] = j[:, W:2 * W].astype(BF)
    qkv_ref[:, 2 * W:] = (j[:, 2 * W:] + row(3)).astype(BF)
    for h in range(W // 128):
        s = slice(h * 128, h * 128 + 128)
        q = (qkv_ref[:, s].astype(F32) * (0.125 * LOG2E)).astype(BF)
        p = enc_probs(two_heads(q), qkv_ref[:, W + h * 128:W + h * 128 + 128], valid).astype(BF)
        v = two_heads(qkv_ref[:, 2 * W + h * 128:2 * W + h * 128 + 128])
        acts_ref[:, W + h * 128:W + h * 128 + 128] = (dot(p[:n], v[:n]) + dot(p[n:], v[n:])).astype(BF)
    copies[1].wait()
    mid = x + (dot(acts_ref[:, W:2 * W], wo_ref[...]) + row(4))
    mid_ref[...] = mid
    xh, _ = norm_r(mid)
    a2 = (xh * row(5) + row(6)).astype(BF)
    acts_ref[:, 2 * W:3 * W] = a2
    copies[2].wait()
    for f in range(0, FF, W):
        g, gp = gelu_pair(dot(a2, w1_ref[:, f:f + W]) + b1_ref[f:f + W].astype(F32).reshape(1, W))
        acts_ref[:, 3 * W + f:3 * W + f + W] = g.astype(BF)
        gp_ref[:, f:f + W] = gp.astype(BF)
    copies[3].wait()
    y = mid + (dot(acts_ref[:, 3 * W:3 * W + FF], w2_ref[...]) + row(7))
    enc = y.astype(BF)
    acts_ref[:, 3 * W + FF:] = enc
    copies[4].wait()
    proj_ref[...] = dot(enc, wp_ref[...])


def enc_fwd_call(sec, frames, seen, tokens, vec, b1, wqkv, wo, w1, w2, wp):
    n, W = tokens.shape[1], tokens.shape[2]
    FF = w1.shape[1]
    vm, hbm = pl.BlockSpec(memory_space=pltpu.VMEM), pl.BlockSpec(memory_space=pl.ANY)
    S = jax.ShapeDtypeStruct
    return pl.pallas_call(
        functools.partial(enc_fwd_kernel, W=W, FF=FF, seen=seen),
        in_specs=[pl.BlockSpec(memory_space=pltpu.SMEM)] * 2 + [vm] * 3 + [hbm] * 5,
        out_specs=[vm] * 5,
        out_shape=[S((n, 4 * W + FF), BF), S((n, 3 * W), BF), S((n, W), F32), S((n, FF), BF), S((n, wp.shape[1]), F32)],
        scratch_shapes=[pltpu.VMEM(w.shape, BF) for w in (wqkv, wo, w1, w2, wp)] + [pltpu.SemaphoreType.DMA((5,))],
        compiler_params=pltpu.CompilerParams(vmem_limit_bytes=VMEM),
        cost_estimate=pl.CostEstimate(flops=1_700_000_000, bytes_accessed=18_000_000, transcendentals=1_000_000),
        name="encoder_forward",
    )(sec, frames, tokens, vec, b1, wqkv, wo, w1, w2, wp)


def half_of(ref, start, size, s):
    return ref[:, pl.ds(pl.multiple_of(start + s * (size // 2), 128), size // 2)]


def enc_bwd_hidden_kernel(sec_ref, dz_ref, gp_ref, wp_any, w2_any, mine_ref, other_ref, full_ref, small_ref, wp_ref, w2_ref, sem, *, W, FF):
    copies = [pltpu.make_async_copy(a, b, sem.at[i]) for i, (a, b) in enumerate(((wp_any, wp_ref), (w2_any, w2_ref)))]
    for c in copies:
        c.start()
    sec = sec_ref[0]
    small_ref[...] = jnp.zeros_like(small_ref)
    copies[0].wait()
    de = dot(dz_ref[...], wp_ref[...], 1, 1).astype(BF)
    full_ref[:, :W] = de
    small_ref[7:8, :] = jnp.sum(de.astype(F32), axis=0, keepdims=True)
    copies[1].wait()
    for f in range(0, FF, W):
        duf = gp_ref[:, f:f + W].astype(F32) * dot(de, w2_ref[f:f + W, :], 1, 1)
        full_ref[:, W + f:2 * W + f] = duf.astype(BF)
        small_ref[8 + f // W:9 + f // W, :] = jnp.sum(duf, axis=0, keepdims=True)
    for ref, s in ((mine_ref, sec), (other_ref, 1 - sec)):
        ref[:, :W // 2] = half_of(full_ref, 0, W, s)
        ref[:, W // 2:] = half_of(full_ref, W, FF, s)


def enc_bwd_hidden_call(idx, dz, gp, wp, w2):
    n, FF = gp.shape
    W = w2.shape[1]
    vm, hbm = pl.BlockSpec(memory_space=pltpu.VMEM), pl.BlockSpec(memory_space=pl.ANY)
    S = jax.ShapeDtypeStruct
    return pl.pallas_call(
        functools.partial(enc_bwd_hidden_kernel, W=W, FF=FF),
        in_specs=[pl.BlockSpec(memory_space=pltpu.SMEM), vm, vm, hbm, hbm],
        out_specs=[vm] * 4,
        out_shape=[S((n, (W + FF) // 2), BF), S((n, (W + FF) // 2), BF), S((n, W + FF), BF), S((16, W), F32)],
        scratch_shapes=[pltpu.VMEM(w.shape, BF) for w in (wp, w2)] + [pltpu.SemaphoreType.DMA((2,))],
        compiler_params=pltpu.CompilerParams(vmem_limit_bytes=VMEM),
        cost_estimate=pl.CostEstimate(flops=600_000_000, bytes_accessed=8_000_000, transcendentals=0),
        name="encoder_backward_hidden",
    )(idx, dz, gp, wp, w2)


def enc_bwd_kernel(sec_ref, frames_ref, dz_ref, tok_ref, vec_ref, qkv_ref, mid_ref, du_ref, small_ref, w1_any, wo_any, wqkv_any,
                   mine_ref, other_ref, tok_mine_ref, tok_other_ref, w1_ref, wo_ref, wqkv_ref, full, tokg, small, sem, *, W, FF, seen):
    copies = [pltpu.make_async_copy(a, b, sem.at[i]) for i, (a, b) in enumerate(((w1_any, w1_ref), (wo_any, wo_ref), (wqkv_any, wqkv_ref)))]
    for c in copies:
        c.start()
    sec = sec_ref[0]
    valid = frames_ref[sec] // 2 * seen
    vec = vec_ref[...].astype(F32)
    row = lambda i: vec[i:i + 1, :]
    rsum = lambda v: jnp.sum(v, axis=0, keepdims=True)
    n = dz_ref.shape[0]
    small[...] = small_ref[...]
    def_ = du_ref[:, :W].astype(F32)
    copies[0].wait()
    da2 = dot(du_ref[:, W:], w1_ref[...], 1, 1)
    xh, r = norm_r(mid_ref[...])
    small[5:6, :] = rsum(da2 * xh)
    small[6:7, :] = rsum(da2)
    dg = da2 * row(5)
    dm = def_ + r * (dg - jnp.mean(dg, axis=1, keepdims=True) - xh * jnp.mean(dg * xh, axis=1, keepdims=True))
    small[4:5, :] = rsum(dm)
    db = dm.astype(BF)
    full[:, :W] = db
    copies[1].wait()
    do = dot(db, wo_ref[...], 1, 1).astype(BF)
    Q = W
    for h in range(W // 128):
        c = h * 128
        q = two_heads((qkv_ref[:, c:c + 128].astype(F32) * (0.125 * LOG2E)).astype(BF))
        k = qkv_ref[:, W + c:W + c + 128]
        v = qkv_ref[:, 2 * W + c:2 * W + c + 128]
        k2 = two_heads(k)
        do2 = two_heads(do[:, c:c + 128])
        p = enc_probs(q, k, valid)
        dp = dot(do2, v, 1, 1)
        ds = (p * (dp - jnp.sum(dp * p, axis=1, keepdims=True))).astype(BF)
        p16 = p.astype(BF)
        full[:, Q + c:Q + c + 128] = ((dot(ds[:n], k2[:n]) + dot(ds[n:], k2[n:])) * 0.125).astype(BF)
        full[:, Q + W + c:Q + W + c + 128] = (dot(ds, q, 0, 0) * LN2).astype(BF)
        full[:, Q + 2 * W + c:Q + 2 * W + c + 128] = dot(p16, do2, 0, 0).astype(BF)
    small[2:3, :] = rsum(full[:, Q:Q + W].astype(F32))
    small[3:4, :] = rsum(full[:, Q + 2 * W:Q + 3 * W].astype(F32))
    copies[2].wait()
    da = dot(full[:, Q:Q + 3 * W], wqkv_ref[...], 1, 1)
    xh, r = norm_r(tok_ref[sec].astype(F32))
    small[0:1, :] = rsum(da * xh)
    small[1:2, :] = rsum(da)
    dg = da * row(0)
    dx = dm + r * (dg - jnp.mean(dg, axis=1, keepdims=True) - xh * jnp.mean(dg * xh, axis=1, keepdims=True))
    tokg[...] = dx.astype(BF)
    half = W // 2
    for ref, tref, s in ((mine_ref, tok_mine_ref, sec), (other_ref, tok_other_ref, 1 - sec)):
        tref[...] = half_of(tokg, 0, W, s)
        ref[:n, :half] = half_of(full, 0, W, s)
        ref[:n, half:4 * half] = half_of(full, Q, 3 * W, s)
        ref[:n, 4 * half:] = dz_ref[...]
        ref[n:, :half] = half_of(small, 0, W, s).astype(BF)
        ref[n:, half:] = jnp.zeros((16, ref.shape[1] - half), BF)
        for t in range(FF // 2 // W):
            b = jnp.where(s == 0, small[8 + t:9 + t, :], small[8 + FF // 2 // W + t:9 + FF // 2 // W + t, :])
            ref[n + 8 + t:n + 9 + t, :W] = b.astype(BF)


def enc_bwd_call(sec, frames, seen, dz, tokens, vec, qkv, mid, du, small, w1, wo, wqkv):
    n, W = tokens.shape[1], tokens.shape[2]
    FF = w1.shape[1]
    vm, hbm = pl.BlockSpec(memory_space=pltpu.VMEM), pl.BlockSpec(memory_space=pl.ANY)
    S = jax.ShapeDtypeStruct
    width = 2 * W + dz.shape[1]
    return pl.pallas_call(
        functools.partial(enc_bwd_kernel, W=W, FF=FF, seen=seen),
        in_specs=[pl.BlockSpec(memory_space=pltpu.SMEM)] * 2 + [vm] * 7 + [hbm] * 3,
        out_specs=[vm] * 4,
        out_shape=[S((n + 16, width), BF), S((n + 16, width), BF), S((n, W // 2), BF), S((n, W // 2), BF)],
        scratch_shapes=[pltpu.VMEM(w.shape, BF) for w in (w1, wo, wqkv)]
        + [pltpu.VMEM((n, 4 * W), BF), pltpu.VMEM((n, W), BF), pltpu.VMEM((16, W), F32), pltpu.SemaphoreType.DMA((3,))],
        compiler_params=pltpu.CompilerParams(vmem_limit_bytes=VMEM),
        cost_estimate=pl.CostEstimate(flops=1_600_000_000, bytes_accessed=12_000_000, transcendentals=1_000_000),
        name="encoder_backward",
    )(sec, frames, dz, tokens, vec, qkv, mid, du, small, w1, wo, wqkv)


PIECES = 8


def flat_blocks(W, FF, WD):
    half = W // 2
    return ((("down", FF, half // 128),), (("up", W, FF // 2 // 128),), (("qkv", W, 3 * half // 128), ("out", W, half // 128), ("proj", WD // 2, W // 128)))


def flat_rows(part, W, FF, WD):
    rows = sum(r * b for _, r, b in flat_blocks(W, FF, WD)[part])
    if part == 2:
        rows += 8 * (W // 2 // 128) + FF // 2 // 128
    unit = PIECES * 16
    return -(-rows // unit) * unit


def part_rows(part, W, FF, WD, WF):
    return flat_rows(part, W, FF, WD) + dec_blocks(WD, WF)["all"] // 3


def weight_grad_kernel(idx_ref, acts_ref, came_ref, mine_ref, dcame_ref, pack_any, pack_came_any, give, keep, flat, acts, dy, dzt, small, pack, pack_came, sem, pack_sem, *, part, W, FF, WD):
    n = acts_ref.shape[0]
    third = pack.shape[0]
    packs = [pltpu.make_async_copy(a.at[pl.ds(part * third, third), :], b, pack_sem.at[i]) for i, (a, b) in enumerate(((pack_any, pack), (pack_came_any, pack_came)))]
    for c in packs:
        c.start()
    half = W // 2
    lhs = {"qkv": (0, W), "out": (W, W), "up": (2 * W, W), "down": (3 * W, FF), "proj": (3 * W + FF, W)}
    cols = {"down": (0, half), "up": (half, FF // 2), "out": (0, half), "qkv": (half, 3 * half)}
    dy[:n, :] = mine_ref[:n, :]
    dy[n:, :] = dcame_ref[:n, :]
    at = 0
    step = 384
    for name, rows, blocks in flat_blocks(W, FF, WD)[part]:
        a0, an = lhs[name]
        acts[:n, :an] = acts_ref[:, a0:a0 + an]
        acts[n:, :an] = came_ref[:, a0:a0 + an]
        if name == "proj":
            dzt[...] = dy[:, 4 * half:4 * half + WD].T
            g = dot(dzt[pl.ds(pl.multiple_of(idx_ref[0] * (WD // 2), 16), WD // 2), :], acts[:, :an]).astype(BF)
            for b in range(blocks):
                flat[at:at + rows, :] = g[:, b * 128:b * 128 + 128]
                at += rows
            continue
        c0, cn = cols[name]
        for r in range(0, rows, W):
            lt = acts[:, r:r + W].T
            for c in range(0, cn, step):
                g = dot(lt, dy[:, c0 + c:c0 + c + step]).astype(BF)
                for b in range(step // 128):
                    o = at + (c // 128 + b) * rows + r
                    flat[o:o + W, :] = g[:, b * 128:b * 128 + 128]
        at += rows * blocks
    if part == 2:
        small[...] = mine_ref[n:, :W].astype(F32) + dcame_ref[n:, :W].astype(F32)
        for b in range(half // 128):
            flat[at:at + 8, :] = small[0:8, b * 128:b * 128 + 128].astype(BF)
            at += 8
        tail = flat.shape[0] - third - at
        bias = [small[8 + t:9 + t, b * 128:b * 128 + 128] for t in range(FF // 2 // W) for b in range(W // 128)]
        bias = jnp.concatenate(bias + [jnp.zeros((tail - len(bias), 128), F32)], axis=0)
        flat[at:at + tail, :] = bias.astype(BF)
    for c in packs:
        c.wait()
    flat[flat.shape[0] - third:, :] = (pack[...].astype(F32) + pack_came[...].astype(F32)).astype(BF)
    size = flat.shape[0] // PIECES
    me = idx_ref[1 + part]

    def send(p, k):
        src = lambda q: flat.at[pl.ds(pl.multiple_of((q ^ me) * size, 16), size), :]
        to = pl.ds(pl.multiple_of(p * size, 16), size)
        pltpu.make_async_copy(src(p), keep.at[to, :], sem).start()
        pltpu.make_async_copy(src(p + PIECES // 2), give.at[to, :], sem).start()
        return k

    lax.fori_loop(0, PIECES // 2, send, 0)
    pltpu.make_async_copy(flat, flat, sem).wait()


def weight_grad_call(part, idx, acts, came, mine, dcame, pack, pack_came, W, FF, WD, WF):
    n = acts.shape[0]
    rows = part_rows(part, W, FF, WD, WF)
    third = pack.shape[0] // 3
    vm, hbm = pl.BlockSpec(memory_space=pltpu.VMEM), pl.BlockSpec(memory_space=pl.ANY)
    S = jax.ShapeDtypeStruct
    return pl.pallas_call(
        functools.partial(weight_grad_kernel, part=part, W=W, FF=FF, WD=WD),
        in_specs=[pl.BlockSpec(memory_space=pltpu.SMEM)] + [vm] * 4 + [hbm] * 2,
        out_specs=[hbm] * 2,
        out_shape=[S((rows // 2, 128), BF)] * 2,
        scratch_shapes=[pltpu.VMEM((rows, 128), BF), pltpu.VMEM((2 * n, FF if part == 0 else W), BF), pltpu.VMEM((2 * n, mine.shape[1]), BF),
                        pltpu.VMEM((WD, 2 * n), BF), pltpu.VMEM((16, W), F32), pltpu.VMEM((third, 128), BF), pltpu.VMEM((third, 128), BF),
                        pltpu.SemaphoreType.DMA, pltpu.SemaphoreType.DMA((2,))],
        compiler_params=pltpu.CompilerParams(vmem_limit_bytes=VMEM),
        cost_estimate=pl.CostEstimate(flops=600_000_000, bytes_accessed=8_000_000, transcendentals=0),
        name=("gradient_down", "gradient_up", "gradient_qkv_out_proj")[part],
    )(idx, acts, came, mine, dcame, pack, pack_came)


def unpack_kernel(idx_ref, own0, own1, own2, came0, came1, came2, *refs, W, FF, WD, WF, slots, patches):
    down, up, qkv, out, proj, vec_ref, bias_ref, sq_ref = refs[:8]
    dec_refs, refs = refs[8:16], refs[16:]
    flats, stages, pack, fetch_sem, store_sem = refs[:3], refs[3:8], refs[8], refs[9], refs[10]
    third = pack.shape[0] // 3
    for i, (own, came) in enumerate(((own0, came0), (own1, came1), (own2, came2))):
        me = idx_ref[1 + i]
        size = flats[i].shape[0] // PIECES

        def fetch(p, k, own=own, came=came, me=me, flat=flats[i], size=size, i=i):
            to = lambda q: flat.at[pl.ds(pl.multiple_of((q ^ me) * size, 16), size), :]
            src = pl.ds(pl.multiple_of(p * size, 16), size)
            pltpu.make_async_copy(own.at[src, :], to(p), fetch_sem.at[i]).start()
            pltpu.make_async_copy(came.at[src, :], to(p + PIECES // 2), fetch_sem.at[i]).start()
            return k

        lax.fori_loop(0, PIECES // 2, fetch, 0)
    named = dict(zip(("down", "up", "qkv", "out", "proj"), zip((down, up, qkv, out, proj), stages)))
    enc = jnp.zeros((8, 128), F32)
    dec = jnp.zeros((8, 128), F32)
    fold = lambda v: jnp.sum((v * v).reshape(-1, 8, 128), axis=0)
    stores = []
    for part, flat in enumerate(flats):
        pltpu.make_async_copy(flat, flat, fetch_sem.at[part]).wait()
        pack[part * third:part * third + third, :] = flat[flat.shape[0] - third:, :]
        at = 0
        for name, rows, blocks in flat_blocks(W, FF, WD)[part]:
            ref, stage = named[name]
            for b in range(blocks):
                g = flat[at:at + rows, :].astype(F32)
                c = slice(b * 128, b * 128 + 128)
                stage[:, c] = g
                if name == "proj":
                    dec += fold(g)
                else:
                    enc += fold(g)
                at += rows
                if b % 3 == 2:
                    cols = pl.ds(b * 128 - 256, 384)
                    stores.append(pltpu.make_async_copy(stage.at[:, cols], ref.at[:, cols], store_sem.at[len(stores)]))
                    stores[-1].start()
    for b in range(W // 2 // 128):
        g = flat[at:at + 8, :].astype(F32)
        enc += g * g
        vec_ref[:, b * 128:b * 128 + 128] = g
        at += 8
    g = flat[at:at + 16, :].astype(F32)[:FF // 2 // 128]
    bias_ref[...] = g
    enc += jnp.concatenate([jnp.sum(g * g, axis=0, keepdims=True), jnp.zeros((7, 128), F32)], axis=0)
    dec += finish(lambda at, n: pack[at:at + n, :], *dec_refs, W=WD, FF=WF, slots=slots, patches=patches)
    sq_ref[:8, :] = enc
    sq_ref[8:, :] = dec
    for s in stores:
        s.wait()


def unpack_call(idx, own, came, slots, patches, W, FF, WD, WF):
    vm, hbm = pl.BlockSpec(memory_space=pltpu.VMEM), pl.BlockSpec(memory_space=pl.ANY)
    S = lambda *shape: jax.ShapeDtypeStruct(shape, F32)
    half = W // 2
    wh = WD // 2
    dec = [S(3 * wh, WD), S(wh, WD), S(WD, WF // 2), S(wh, WF), S(9, wh), S(8, WF // 2), S(slots, wh), S(patches, wh)]
    big = [S(FF, half), S(W, FF // 2), S(W, 3 * half), S(W, half), S(WD // 2, W)]
    return pl.pallas_call(
        functools.partial(unpack_kernel, W=W, FF=FF, WD=WD, WF=WF, slots=slots, patches=patches),
        in_specs=[pl.BlockSpec(memory_space=pltpu.SMEM)] + [hbm] * 6,
        out_specs=[hbm] * 5 + [vm] * 11,
        out_shape=big + [S(8, half), S(FF // 2 // 128, 128), S(16, 128)] + dec,
        scratch_shapes=[pltpu.VMEM((part_rows(i, W, FF, WD, WF), 128), BF) for i in range(3)] + [pltpu.VMEM(s.shape, F32) for s in big]
        + [pltpu.VMEM((dec_blocks(WD, WF)["all"], 128), BF)]
        + [pltpu.SemaphoreType.DMA((3,)), pltpu.SemaphoreType.DMA((sum(s.shape[1] // 384 for s in big),))],
        compiler_params=pltpu.CompilerParams(vmem_limit_bytes=VMEM),
        cost_estimate=pl.CostEstimate(flops=10_000_000, bytes_accessed=23_000_000, transcendentals=0),
        name="unpack",
    )(idx, *own, *came)


def pair_kernel(sec_ref, dec_mine, dec_came, tok_mine, tok_came, dec_ref, tok_ref):
    sec = sec_ref[0]
    for ref, mine, came in ((dec_ref, dec_mine, dec_came), (tok_ref, tok_mine, tok_came)):
        ref[sec] = mine[...]
        ref[1 - sec] = came[...]


def pair_call(sec, *arrays):
    vm = pl.BlockSpec(memory_space=pltpu.VMEM)
    return pl.pallas_call(
        pair_kernel,
        in_specs=[pl.BlockSpec(memory_space=pltpu.SMEM)] + [vm] * 4,
        out_specs=[vm] * 2,
        out_shape=[jax.ShapeDtypeStruct((2, *arrays[i].shape), BF) for i in (0, 2)],
        compiler_params=pltpu.CompilerParams(vmem_limit_bytes=VMEM),
        cost_estimate=pl.CostEstimate(flops=0, bytes_accessed=3_000_000, transcendentals=0),
        name="both_clips",
    )(sec, *arrays)


SIDE = 4


def coordinates(index):
    return (index // (SIDE * SIDE), index // SIDE % SIDE, index % SIDE)


def flip(place, axis, kind):
    place = list(place)
    place[axis] = place[axis] ^ 1 if kind == 0 else SIDE - 1 - place[axis]
    return tuple(place)


def swap(value, axes, far):
    pairs = []
    for core in range(2):
        for index in range(SIDE**3):
            place = coordinates(index)
            for axis in axes:
                place = flip(place, axis, core ^ far)
            target = (place[0] * SIDE + place[1]) * SIDE + place[2]
            pairs.append((core * SIDE**3 + index, core * SIDE**3 + target))
    return lax.ppermute(value, ("section", "dp"), pairs)


def add(left, right):
    return (left.astype(jnp.float32) + right.astype(jnp.float32)).astype(jnp.bfloat16)


def piece_numbers(place, core):
    near = [1 * ((p == 1) | (p == 2)) for p in place]
    far = [1 * (p >= 2) for p in place]
    first = [(1 - core) * a + core * b for a, b in zip(near, far)]
    return [first[i] * 4 + first[(i + 1) % 3] * 2 + first[(i + 2) % 3] for i in range(3)]


def halve(v, axis, far):
    half = v.shape[0] // 2
    return add(v[:half], swap(v[half:], (axis,), far))


def sum_over_chips(pairs):
    own, came = [], []
    for i, (give, keep) in enumerate(pairs):
        v = add(keep, swap(give, (i,), 0))
        for step in (1, 2):
            v = halve(v, (i + step) % 3, 0)
        for step in range(3):
            v = add(v, swap(v, ((i + step) % 3,), 1))
        for step in (2, 1):
            v = jnp.concatenate([v, swap(v, ((i + step) % 3,), 0)])
        own.append(v)
        came.append(swap(v, (i,), 0))
    return (own, came)


def from_partner(value):
    return lax.ppermute(value, "section", [(0, 1), (1, 0)])


def shards(
    tokens,
    frames,
    visible,
    out_grad,
    enc_vectors,
    enc_qkv,
    enc_out,
    enc_up,
    enc_up_bias,
    enc_down,
    proj_weight,
    dec_vectors,
    dec_qkv,
    dec_out,
    dec_up,
    dec_up_bias,
    dec_down,
    time_pos,
    space_pos,
):
    enc_width, enc_hidden = enc_up.shape
    dec_width, dec_hidden = dec_up.shape
    slot_count = time_pos.shape[0]
    patch_count = space_pos.shape[0]
    seen_count = visible.shape[1]
    section = lax.axis_index("section").astype(jnp.int32)
    core = section.reshape(1)
    sizes = (enc_width, enc_hidden, dec_width, dec_hidden)
    acts, qkv, mid, slopes, projected = enc_fwd_call(
        core, frames, seen_count, tokens, enc_vectors, enc_up_bias, enc_qkv, enc_out, enc_up, enc_down, proj_weight
    )
    acts_came = from_partner(acts)
    (decoded_mine, decoded_other), grad_projected, (dec_mine, dec_other) = dec_block_call(
        core,
        frames,
        visible,
        projected,
        time_pos,
        space_pos,
        dec_vectors,
        dec_qkv,
        dec_out,
        dec_up,
        dec_up_bias,
        dec_down,
        out_grad,
        TQ=384,
        TA=640,
    )
    dec_came = from_partner(dec_other)
    hidden_mine, hidden_other, hidden, small_sums = enc_bwd_hidden_call(core, grad_projected, slopes, proj_weight, enc_down)
    hidden_came = from_partner(hidden_other)
    places = jnp.stack([section, *piece_numbers(coordinates(lax.axis_index("dp")), section)]).astype(jnp.int32)
    dy_mine, dy_other, token_mine, token_other = enc_bwd_call(
        core, frames, seen_count, grad_projected, tokens, enc_vectors, qkv, mid, hidden, small_sums, enc_up, enc_out, enc_qkv
    )
    dy_came = from_partner(dy_other)
    order, dy_mine = lax.optimization_barrier((places, dy_mine))
    first = weight_grad_call(0, order, acts, acts_came, hidden_mine, hidden_came, dec_mine, dec_came, *sizes)
    order, first = lax.optimization_barrier((places, first))
    last = weight_grad_call(2, order, acts, acts_came, dy_mine, dy_came, dec_mine, dec_came, *sizes)
    order, last = lax.optimization_barrier((places, last))
    middle = weight_grad_call(1, order, acts, acts_came, hidden_mine, hidden_came, dec_mine, dec_came, *sizes)
    own, came = sum_over_chips((first, middle, last))
    decoded_came = from_partner(decoded_other)
    token_came = from_partner(token_other)
    decoded, token_grad = pair_call(core, decoded_mine, decoded_came, token_mine, token_came)
    (
        g_enc_down, g_enc_up, g_enc_qkv, g_enc_out, g_proj, g_vectors, g_enc_bias, squares,
        g_dec_qkv, g_dec_out, g_dec_up, g_dec_down, g_dec_vectors, g_dec_bias, g_time, g_space,
    ) = unpack_call(places, own, came, slot_count, patch_count, *sizes)
    enc_squares, dec_squares = squares[:8], squares[8:]
    give = jnp.where(section == 0, dec_squares, enc_squares)
    keep = jnp.where(section == 0, enc_squares, dec_squares)
    norms = jnp.sum(keep + from_partner(give)).reshape(1)
    return (
        decoded.transpose(0, 2, 1),
        token_grad,
        g_vectors,
        g_enc_qkv,
        g_enc_out,
        g_enc_up,
        g_enc_bias.reshape(-1),
        g_enc_down,
        g_proj.T,
        g_dec_vectors,
        g_dec_qkv.T,
        g_dec_out.T,
        g_dec_up,
        g_dec_bias[0],
        g_dec_down.T,
        g_time,
        g_space,
        norms,
    )


from jax.sharding import PartitionSpec as P


def solution(mesh):
    placed = (
        P("dp", None, None),
        P("dp"),
        P("dp", None),
        P("dp", None, None),
        P(),
        P(),
        P(),
        P(),
        P(),
        P(),
        P(),
        P(),
        P(),
        P(),
        P(),
        P(),
        P(),
        P(),
        P(),
    )
    return jax.shard_map(
        shards,
        mesh=mesh,
        in_specs=placed,
        out_specs=(
            P("dp", None, "section"),
            P("dp", None, "section"),
            P(None, "section"),
            P(None, "section"),
            P(None, "section"),
            P(None, "section"),
            P("section"),
            P(None, "section"),
            P(None, "section"),
            P(None, "section"),
            P(None, "section"),
            P(None, "section"),
            P(None, "section"),
            P("section"),
            P(None, "section"),
            P(None, "section"),
            P(None, "section"),
            P("section"),
        ),
        check_vma=False,
    )
```

```python
import functools
import jax, jax.numpy as jnp, numpy as np
from jax import lax
from jax.experimental import pallas as pl
from jax.experimental.pallas import tpu as pltpu

EPS = 1e-6
NEG = -1e9
LOG2E = 1.4426950408889634
LN2 = 0.6931471805599453
F32, BF = jnp.float32, jnp.bfloat16


def dot(a, b, ca=1, cb=0):
    return lax.dot_general(a, b, (((ca,), (cb,)), ((), ())), preferred_element_type=F32)


def tiles_of(total, size):
    return [(s, min(size, total - s)) for s in range(0, total, size)]


def over(total, size, body, carry):
    full = total // size
    if full:
        carry = lax.fori_loop(0, full, lambda i, k: body(pl.ds(pl.multiple_of(i * size, 128), size), size, k), carry)
    if total % size:
        carry = body(pl.ds(full * size, total % size), total % size, carry)
    return carry


def norm_c(x):
    mean = jnp.mean(x, axis=0, keepdims=True)
    c = x - mean
    r = lax.rsqrt(jnp.mean(c * c, axis=0, keepdims=True) + EPS)
    return c * r, r


def gelu_pair(u):
    a = jnp.abs(u)
    t = 1.0 / (1.0 + (0.3275911 * 0.7071067811865476) * a)
    e = jnp.exp2((-0.5 * LOG2E) * (u * u))
    poly = t * (0.5 * 0.254829592 + t * (0.5 * -0.284496736 + t * (0.5 * 1.421413741 + t * (0.5 * -1.453152027 + t * (0.5 * 1.061405429)))))
    tail = poly * e
    phi = jnp.where(u >= 0, 1.0 - tail, tail)
    return u * phi, phi + u * (e * 0.3989422804014327)


def dec_kernel(sec_ref, frames_ref, vis_ref, proj_ref, time_ref, space_ref, vecs_ref, wqkv_ref, wo_ref, w1_ref, bias_ref, w2_ref, dy_any,
               out_refs, dz_ref, pack_refs,
               x_s, a1_s, qkv_s, e_s, l_s, o_s, m_s, a2_s, g_s, gp_s, dy_s, db_s, sel_s, doa_s, do_s, o32_s, dy_ref, vec_ref, b1_ref, dec_s, dy_sem, *, W, L, H, FF, V, slots, patches, TQ, TA):
    dqkv_s, ds_s = g_s, gp_s
    sec = sec_ref[0]
    used = frames_ref[sec] // 2
    valid = used * patches
    dy_copy = pltpu.make_async_copy(dy_any.at[sec], dy_ref, dy_sem)
    dy_copy.start()
    seen_count = V // slots
    vecs = vecs_ref[...].astype(F32)
    vec_ref[...] = jnp.concatenate([vecs, jnp.zeros((16 - vecs.shape[0], W), F32)], axis=0).T
    b1_ref[...] = jnp.broadcast_to(bias_ref[...].reshape(1, FF).astype(F32), (8, FF)).T[:, 0:1]
    col = lambda i: vec_ref[:, i:i + 1]
    HS = 64
    lane = lax.broadcasted_iota(jnp.int32, (1, L), 1)
    vrow = lax.broadcasted_iota(jnp.int32, (V, 1), 0)
    vslot = jnp.zeros((V, 1), jnp.int32)
    for t in range(1, slots):
        vslot += (vrow >= t * seen_count).astype(jnp.int32)
    vrank = vrow - vslot * seen_count
    target = vslot * patches
    for j in range(seen_count):
        target += jnp.where(vrank == j, vis_ref[sec, j], 0)
    onehot = (target == lax.broadcasted_iota(jnp.int32, (V, L), 1)).astype(F32)
    slot = jnp.zeros((1, L), jnp.int32)
    for t in range(1, slots):
        slot += (lane >= t * patches).astype(jnp.int32)
    patch_oh = (lax.broadcasted_iota(jnp.int32, (patches, L), 0) == lane - slot * patches).astype(BF)
    seen = jnp.sum(onehot, axis=0, keepdims=True)
    srow = lax.broadcasted_iota(jnp.int32, (32, L), 0)
    slot_oh = jnp.where(srow < 16, ((srow & 7) == slot).astype(F32), jnp.where(srow == 16, 1.0 - seen, 0.0)).astype(BF)
    sel_s[:V, :] = onehot.astype(BF)
    sel_s[V:V + patches, :] = patch_oh
    sel_s[V + patches:, :] = slot_oh
    ti = lax.broadcasted_iota(jnp.int32, (slots, slots), 0)
    ii = lax.broadcasted_iota(jnp.int32, (slots, slots), 1)
    num = ti * (slots - 1)
    lower = jnp.zeros((slots, slots), jnp.int32)
    for q in range(1, (slots - 1) * (slots - 1) + 1):
        lower += (num >= q * (used - 1)).astype(jnp.int32)
    frac = (num - lower * (used - 1)).astype(F32) / jnp.full((slots, slots), used - 1, jnp.int32).astype(F32)
    upper = jnp.minimum(lower + 1, slots - 1)
    table = (1.0 - frac) * (ii == lower).astype(F32) + frac * (ii == upper).astype(F32)
    exact = lambda a, b, ca, cb: lax.dot_general(a, b, (((ca,), (cb,)), ((), ())), precision=lax.Precision.HIGHEST, preferred_element_type=F32)
    spos = exact(table, time_ref[...].astype(F32), 1, 0)
    shi = spos.astype(BF)
    slo = (spos - shi.astype(F32)).astype(BF)
    proj = proj_ref[...]
    hi = proj.astype(BF)
    lo = (proj - hi.astype(F32)).astype(BF)
    mask = vecs[8:9, :].astype(BF)
    src = jnp.concatenate([hi.astype(F32), space_ref[...].astype(F32), shi.astype(F32), slo.astype(F32), mask.astype(F32), jnp.zeros((15, W), F32)], axis=0).astype(BF)

    def first(c, n, k):
        x = dot(src, sel_s[:, c], 0, 0) + dot(lo, sel_s[:V, c], 0, 0)
        x_s[:, c] = x
        xh, _ = norm_c(x)
        a1 = (xh * col(0) + col(1)).astype(BF)
        a1_s[:, c] = a1
        j = dot(wqkv_ref[...], a1, 0, 0)
        qkv_s[:W, c] = ((j[:W] + col(2)) * (0.125 * LOG2E)).astype(BF)
        qkv_s[W:2 * W, c] = j[W:2 * W].astype(BF)
        qkv_s[2 * W:, c] = (j[2 * W:] + col(3)).astype(BF)
        return k

    over(L, TQ, first, 0)
    arow = lax.broadcasted_iota(jnp.int32, (16, L), 0)
    kbias = jnp.where((arow == 0) & (lane >= valid), NEG, 0.0).astype(BF)
    one0 = (arow == 0).astype(BF)
    one01 = (arow < 2).astype(BF)

    def fwd_head(h, carry):
        hs = pl.ds(pl.multiple_of(h * HS, HS), HS)
        ks = pl.ds(pl.multiple_of(W + h * HS, HS), HS)
        vs = pl.ds(pl.multiple_of(2 * W + h * HS, HS), HS)
        kr = jnp.concatenate([qkv_s[ks, :], kbias], axis=0).T
        vc = jnp.concatenate([qkv_s[vs, :], one0], axis=0)

        def tile(c, n, exact):
            qc = jnp.concatenate([qkv_s[hs, c], one0[:, :n]], axis=0)
            st = dot(kr, qc)
            if exact:
                st = st - jnp.max(st, axis=0, keepdims=True)
            e = jnp.exp2(st).astype(BF)
            e_s[h, :, c] = e
            oa = dot(vc, e)
            rl = 1.0 / oa[HS:HS + 1]
            l_s[h, :, c] = jnp.broadcast_to(rl, (8, n))
            o = oa[:HS] * rl
            o32_s[hs, c] = o
            o_s[hs, c] = o.astype(BF)

        square = lambda v: jnp.max(jnp.sum(v * v, axis=0))
        bound = square(qkv_s[hs, :].astype(F32)) * square(qkv_s[ks, :].astype(F32))

        @pl.when(bound <= 60.0 * 60.0)
        def _():
            over(L, TA, lambda c, n, k: (tile(c, n, False), k)[1], 0)

        @pl.when(jnp.logical_not(bound <= 60.0 * 60.0))
        def _():
            over(L, TA, lambda c, n, k: (tile(c, n, True), k)[1], 0)

        return carry

    lax.fori_loop(0, H, fwd_head, 0)

    def middle(c, n, sums):
        sum_b1, sum_dy, sum_g2, sum_s2, sum_db = sums
        live = (lax.broadcasted_iota(jnp.int32, (1, n), 1) + c.start < valid).astype(F32)
        mid = x_s[:, c] + (dot(wo_ref[...], o_s[:, c], 0, 0) + col(4))
        xh, r = norm_c(mid)
        a2 = (xh * col(5) + col(6)).astype(BF)
        a2_s[:, c] = a2
        u = dot(w1_ref[...], a2, 0, 0) + b1_ref[...]
        g, gp = gelu_pair(u)
        g = g.astype(BF)
        g_s[:, c] = g
        y = mid + (dot(w2_ref[...], g, 0, 0) + col(7))
        dec_s[:, c] = (y * live).astype(BF)
        dyf = dy_ref[c, :].astype(F32).T * live
        dy = dyf.astype(BF)
        dy_s[:, c] = dy
        duf = gp * dot(w2_ref[...], dy)
        du = duf.astype(BF)
        gp_s[:, c] = du
        da2 = dot(w1_ref[...], du)
        dg = da2 * col(5)
        dm = dyf + r * (dg - jnp.mean(dg, axis=0, keepdims=True) - xh * jnp.mean(dg * xh, axis=0, keepdims=True))
        db = dm.astype(BF)
        db_s[:, c] = db
        do_s[:, c] = dot(wo_ref[...], db).astype(BF)
        m_s[:, c] = dm
        rs = lambda v: jnp.sum(v, axis=1, keepdims=True)
        return (sum_b1 + rs(duf), sum_dy + rs(dyf), sum_g2 + rs(da2 * xh), sum_s2 + rs(da2), sum_db + rs(dm))

    dy_copy.wait()
    zero = jnp.zeros((W, 1), F32)
    sum_b1, sum_dy, sum_g2, sum_s2, sum_db = over(L, TQ, middle, (jnp.zeros((FF, 1), F32), zero, zero, zero, zero))
    blocks = dec_blocks(W, FF)
    for who, s in enumerate((sec, 1 - sec)):
        rows = lambda size, at=0: pl.ds(pl.multiple_of(s * (size // 2) + at, 16), W // 2)
        out_refs[who][...] = dec_s[rows(W), :]
        pack = pack_refs[who]
        for b in range(FF // W):
            put(pack, blocks["down"] + b * 3 * (W // 2), dot(dy_s[rows(W), :], g_s[b * W:b * W + W, :], 1, 1))
        for b in range(FF // 2 // W):
            put(pack, blocks["up"] + b * 3 * W, dot(a2_s[...], gp_s[pl.ds(pl.multiple_of(s * (FF // 2) + b * W, 16), W), :], 1, 1))
        put(pack, blocks["out"], dot(db_s[rows(W), :], o_s[...], 1, 1))

    def bwd_head(h, carry):
        hs = pl.ds(pl.multiple_of(h * HS, HS), HS)
        ks = pl.ds(pl.multiple_of(W + h * HS, HS), HS)
        vs = pl.ds(pl.multiple_of(2 * W + h * HS, HS), HS)
        vr = jnp.concatenate([qkv_s[vs, :], one01], axis=0).T
        kc = qkv_s[ks, :]
        dob = (do_s[hs, :].astype(F32) * l_s[h, 0:1, :]).astype(BF)
        dl = -jnp.sum(dob.astype(F32) * o32_s[hs, :], axis=0, keepdims=True)
        dlh = dl.astype(BF).astype(F32)
        doa_s[:HS, :] = dob
        doa_s[HS:, :] = jnp.where(arow == 0, dlh, jnp.where(arow == 1, dl - dlh, 0.0)).astype(BF)
        def tile(c, n, k):
            dp = dot(vr, doa_s[:, c])
            ds = (e_s[h, :, c].astype(F32) * dp).astype(BF)
            ds_s[:L, c] = ds
            dqkv_s[hs, c] = (dot(kc, ds) * 0.125).astype(BF)
            return k

        over(L, TA, tile, 0)
        dor = doa_s[:HS, :].T
        qr = qkv_s[hs, :].T

        def tile2(c, n, k):
            dqkv_s[vs, c] = dot(e_s[h, c, :], dor).T.astype(BF)
            dqkv_s[ks, c] = (dot(ds_s[c, :], qr) * LN2).T.astype(BF)
            return k

        return over(L, TA, tile2, carry)

    lax.fori_loop(0, H, bwd_head, 0)
    def last(c, n, sums):
        sum_g1, sum_s1, sum_q, sum_v, gsel = sums
        rs = lambda v: jnp.sum(v, axis=1, keepdims=True)
        da = dot(wqkv_ref[...], dqkv_s[:3 * W, c])
        xh, r = norm_c(x_s[:, c])
        dg = da * col(0)
        dx = m_s[:, c] + r * (dg - jnp.mean(dg, axis=0, keepdims=True) - xh * jnp.mean(dg * xh, axis=0, keepdims=True))
        return (sum_g1 + rs(da * xh), sum_s1 + rs(da), sum_q + rs(dqkv_s[:W, c].astype(F32)), sum_v + rs(dqkv_s[2 * W:3 * W, c].astype(F32)),
                gsel + dot(dx.astype(BF), sel_s[:, c], 1, 1))

    sum_g1, sum_s1, sum_q, sum_v, gsel = over(L, TQ, last, (zero, zero, zero, zero, jnp.zeros((W, sel_s.shape[0]), F32)))
    dz_ref[...] = gsel[:, :V].T.astype(BF)
    small = o32_s
    small[:, :8] = jnp.concatenate([sum_g1, sum_s1, sum_q, sum_v, sum_db, sum_g2, sum_s2, sum_dy], axis=1)
    small[:, 8:16] = gsel[:, V + patches + 16:V + patches + 24]
    small[:, 16:24] = exact(gsel[:, V + patches:V + patches + slots], table, 1, 0)
    small[:, 24:24 + patches] = gsel[:, V:V + patches]
    small[:, 24 + patches:256] = jnp.zeros((W, 256 - 24 - patches), F32)
    for who, s in enumerate((sec, 1 - sec)):
        pack = pack_refs[who]
        put(pack, blocks["qkv"], dot(dqkv_s[pl.ds(pl.multiple_of(s * (3 * W // 2), 16), 3 * W // 2), :], a1_s[...], 1, 1))
        half = small[pl.ds(pl.multiple_of(s * (W // 2), 8), W // 2), :256].T[:32 + patches]
        put(pack, blocks["small"], jnp.concatenate([half, jnp.zeros((32 + patches, 256 - W // 2), F32)], axis=1))
        b1_ref[...] = sum_b1
        put(pack, blocks["bias"], jnp.broadcast_to(b1_ref[pl.ds(pl.multiple_of(s * (FF // 2), 8), FF // 2), :], (FF // 2, 128)).T[:16])
        pack[blocks["end"]:, :] = jnp.zeros((pack.shape[0] - blocks["end"], 128), BF)


def put(pack, at, value):
    n = value.shape[0]
    for b in range(value.shape[1] // 128):
        pack[at + b * n:at + b * n + n, :] = value[:, b * 128:b * 128 + 128].astype(BF)


def dec_blocks(W, FF):
    at, rows = 0, {}
    for name, count in (("qkv", 3 * (3 * W // 2)), ("out", 3 * (W // 2)), ("up", 3 * (FF // 2)), ("down", 3 * (FF // 2)), ("small", 2 * 176), ("bias", 16 * (FF // 2 // 128))):
        rows[name] = at
        at += count
    rows["end"] = at
    unit = 3 * 8 * 16
    rows["all"] = -(-at // unit) * unit
    return rows


def finish(read, qkv_ref, out_ref, up_ref, down_ref, vec_ref, bias_ref, time_ref, space_ref, *, W, FF, slots, patches):
    blocks = dec_blocks(W, FF)
    total = jnp.zeros((8, 128), F32)
    fold = lambda v: jnp.sum((v * v).reshape(-1, 8, 128), axis=0)
    for name, ref, n, parts in (("qkv", qkv_ref, 3 * W // 2, 1), ("out", out_ref, W // 2, 1), ("up", up_ref, W, FF // 2 // W), ("down", down_ref, W // 2, FF // W)):
        for b in range(3 * parts):
            g = read(blocks[name] + b * n, n).astype(F32)
            ref[:, b * 128:b * 128 + 128] = g
            total += fold(g)
    low = read(blocks["small"], 176).astype(F32)
    high = read(blocks["small"] + 176, 176).astype(F32)
    total += fold(low) + fold(high)
    for ref, at, n in ((vec_ref, 0, 9), (time_ref, 16, slots), (space_ref, 16 + slots, patches)):
        ref[:, :128] = low[at:at + n]
        ref[:, 128:] = high[at:at + n, :W // 2 - 128]
    for b in range(FF // 2 // 128):
        g = read(blocks["bias"] + 16 * b, 16).astype(F32)
        bias_ref[:, b * 128:b * 128 + 128] = g[:8]
        total += 0.0625 * fold(g)
    return total


def dec_block_call(sec, frames, visible, proj, time_pos, space, vecs, wqkv, wo, w1, bias, w2, dy, TQ, TA):
    W, L, FF = wqkv.shape[0], dy.shape[1], w1.shape[1]
    H = W // 64
    patches, slots = space.shape[0], time_pos.shape[0]
    V = proj.shape[0]
    sm, vm = pl.BlockSpec(memory_space=pltpu.SMEM), pl.BlockSpec(memory_space=pltpu.VMEM)
    S = jax.ShapeDtypeStruct
    return pl.pallas_call(
        functools.partial(dec_kernel, W=W, L=L, H=H, FF=FF, V=V, slots=slots, patches=patches, TQ=TQ, TA=TA),
        in_specs=[sm, sm, sm] + [vm] * 9 + [pl.BlockSpec(memory_space=pl.ANY)],
        out_specs=[[vm] * 2, vm, [vm] * 2],
        out_shape=[[S((W // 2, L), BF)] * 2, S((V, W), BF), [S((dec_blocks(W, FF)["all"], 128), BF)] * 2],
        scratch_shapes=[
            pltpu.VMEM((W, L), F32),
            pltpu.VMEM((W, L), BF),
            pltpu.VMEM((3 * W, L), BF),
            pltpu.VMEM((H, L, L), BF),
            pltpu.VMEM((H, 8, L), F32),
            pltpu.VMEM((W, L), BF),
            pltpu.VMEM((W, L), F32),
            pltpu.VMEM((W, L), BF),
            pltpu.VMEM((FF, L), BF),
            pltpu.VMEM((FF, L), BF),
            pltpu.VMEM((W, L), BF),
            pltpu.VMEM((W, L), BF),
            pltpu.VMEM((V + patches + 32, L), BF),
            pltpu.VMEM((80, L), BF),
            pltpu.VMEM((W, L), BF),
            pltpu.VMEM((W, L), F32),
            pltpu.VMEM((L, W), BF),
            pltpu.VMEM((W, 16), F32),
            pltpu.VMEM((FF, 1), F32),
            pltpu.VMEM((W, L), BF),
            pltpu.SemaphoreType.DMA,
        ],
        compiler_params=pltpu.CompilerParams(vmem_limit_bytes=63 * 1024 * 1024),
        cost_estimate=pl.CostEstimate(flops=28_000_000_000, bytes_accessed=12_000_000, transcendentals=10_000_000),
        name="decoder",
    )(sec, frames, visible, proj, time_pos, space, vecs, wqkv, wo, w1, bias, w2, dy)


VMEM = 63 * 1024 * 1024


def aligned(start, size):
    return pl.ds(pl.multiple_of(start, size), size)


def norm_r(x):
    mean = jnp.mean(x, axis=1, keepdims=True)
    c = x - mean
    r = lax.rsqrt(jnp.mean(c * c, axis=1, keepdims=True) + EPS)
    return c * r, r


def enc_probs(qm, k, valid):
    s = dot(qm, k, 1, 1)
    live = lax.broadcasted_iota(jnp.int32, s.shape, 1) < valid
    s = jnp.where(live, s, NEG)
    e = jnp.exp2(s - jnp.max(s, axis=1, keepdims=True))
    return e / jnp.sum(e, axis=1, keepdims=True)


def two_heads(v):
    low = lax.broadcasted_iota(jnp.int32, v.shape, 1) < 64
    zero = jnp.zeros_like(v)
    return jnp.concatenate([jnp.where(low, v, zero), jnp.where(low, zero, v)], axis=0)


def enc_fwd_kernel(sec_ref, frames_ref, tok_ref, vec_ref, b1_ref, wqkv_any, wo_any, w1_any, w2_any, wp_any,
                   acts_ref, qkv_ref, mid_ref, gp_ref, proj_ref,
                   wqkv_ref, wo_ref, w1_ref, w2_ref, wp_ref, sem, *, W, FF, seen):
    pairs = ((wqkv_any, wqkv_ref), (wo_any, wo_ref), (w1_any, w1_ref), (w2_any, w2_ref), (wp_any, wp_ref))
    copies = [pltpu.make_async_copy(a, b, sem.at[i]) for i, (a, b) in enumerate(pairs)]
    for c in copies[:2]:
        c.start()

    def arrived(i):
        copies[i].wait()
        if i + 2 < len(copies):
            copies[i + 2].start()

    sec = sec_ref[0]
    valid = frames_ref[sec] // 2 * seen
    vec = vec_ref[...].astype(F32)
    row = lambda i: vec[i:i + 1, :]
    x = tok_ref[sec].astype(F32)
    n = x.shape[0]
    xh, _ = norm_r(x)
    a1 = (xh * row(0) + row(1)).astype(BF)
    acts_ref[:, :W] = a1
    arrived(0)
    j = dot(a1, wqkv_ref[...])
    qkv_ref[:, :W] = (j[:, :W] + row(2)).astype(BF)
    qkv_ref[:, W:2 * W] = j[:, W:2 * W].astype(BF)
    qkv_ref[:, 2 * W:] = (j[:, 2 * W:] + row(3)).astype(BF)
    for h in range(W // 128):
        s = slice(h * 128, h * 128 + 128)
        q = (qkv_ref[:, s].astype(F32) * (0.125 * LOG2E)).astype(BF)
        p = enc_probs(two_heads(q), qkv_ref[:, W + h * 128:W + h * 128 + 128], valid).astype(BF)
        v = two_heads(qkv_ref[:, 2 * W + h * 128:2 * W + h * 128 + 128])
        acts_ref[:, W + h * 128:W + h * 128 + 128] = (dot(p[:n], v[:n]) + dot(p[n:], v[n:])).astype(BF)
    arrived(1)
    mid = x + (dot(acts_ref[:, W:2 * W], wo_ref[...]) + row(4))
    mid_ref[...] = mid
    xh, _ = norm_r(mid)
    a2 = (xh * row(5) + row(6)).astype(BF)
    acts_ref[:, 2 * W:3 * W] = a2
    arrived(2)
    for f in range(0, FF, W):
        g, gp = gelu_pair(dot(a2, w1_ref[:, f:f + W]) + b1_ref[f:f + W].astype(F32).reshape(1, W))
        acts_ref[:, 3 * W + f:3 * W + f + W] = g.astype(BF)
        gp_ref[:, f:f + W] = gp.astype(BF)
    arrived(3)
    y = mid + (dot(acts_ref[:, 3 * W:3 * W + FF], w2_ref[...]) + row(7))
    enc = y.astype(BF)
    acts_ref[:, 3 * W + FF:] = enc
    arrived(4)
    proj_ref[...] = dot(enc, wp_ref[...])


def enc_fwd_call(sec, frames, seen, tokens, vec, b1, wqkv, wo, w1, w2, wp):
    n, W = tokens.shape[1], tokens.shape[2]
    FF = w1.shape[1]
    vm, hbm = pl.BlockSpec(memory_space=pltpu.VMEM), pl.BlockSpec(memory_space=pl.ANY)
    S = jax.ShapeDtypeStruct
    return pl.pallas_call(
        functools.partial(enc_fwd_kernel, W=W, FF=FF, seen=seen),
        in_specs=[pl.BlockSpec(memory_space=pltpu.SMEM)] * 2 + [vm] * 3 + [hbm] * 5,
        out_specs=[vm] * 5,
        out_shape=[S((n, 4 * W + FF), BF), S((n, 3 * W), BF), S((n, W), F32), S((n, FF), BF), S((n, wp.shape[1]), F32)],
        scratch_shapes=[pltpu.VMEM(w.shape, BF) for w in (wqkv, wo, w1, w2, wp)] + [pltpu.SemaphoreType.DMA((5,))],
        compiler_params=pltpu.CompilerParams(vmem_limit_bytes=VMEM),
        cost_estimate=pl.CostEstimate(flops=1_700_000_000, bytes_accessed=18_000_000, transcendentals=1_000_000),
        name="encoder_forward",
    )(sec, frames, tokens, vec, b1, wqkv, wo, w1, w2, wp)


def half_of(ref, start, size, s):
    return ref[:, pl.ds(pl.multiple_of(start + s * (size // 2), 128), size // 2)]


def enc_bwd_kernel(sec_ref, frames_ref, dz_ref, tok_ref, vec_ref, qkv_ref, mid_ref, gp_ref, wp_any, w2_any, w1_any, wo_any, wqkv_any,
                   mine_ref, other_ref, tok_mine_ref, tok_other_ref,
                   wp_ref, w2_ref, w1_ref, wo_ref, wqkv_ref, full, tokg, small, sem, *, W, FF, seen):
    pairs = ((wp_any, wp_ref), (w2_any, w2_ref), (w1_any, w1_ref), (wo_any, wo_ref), (wqkv_any, wqkv_ref))
    copies = [pltpu.make_async_copy(a, b, sem.at[i]) for i, (a, b) in enumerate(pairs)]
    for c in copies:
        c.start()
    sec = sec_ref[0]
    valid = frames_ref[sec] // 2 * seen
    vec = vec_ref[...].astype(F32)
    row = lambda i: vec[i:i + 1, :]
    rsum = lambda v: jnp.sum(v, axis=0, keepdims=True)
    n = dz_ref.shape[0]
    small[...] = jnp.zeros_like(small)
    U, B, Q = W, W + FF, 2 * W + FF
    copies[0].wait()
    de = dot(dz_ref[...], wp_ref[...], 1, 1).astype(BF)
    full[:, :W] = de
    def_ = de.astype(F32)
    small[7:8, :W] = rsum(def_)
    copies[1].wait()
    for f in range(0, FF, W):
        duf = gp_ref[:, f:f + W].astype(F32) * dot(de, w2_ref[f:f + W, :], 1, 1)
        full[:, U + f:U + f + W] = duf.astype(BF)
        small[8 + f // W:9 + f // W, :W] = rsum(duf)
    copies[2].wait()
    da2 = dot(full[:, U:U + FF], w1_ref[...], 1, 1)
    xh, r = norm_r(mid_ref[...])
    small[5:6, :W] = rsum(da2 * xh)
    small[6:7, :W] = rsum(da2)
    dg = da2 * row(5)
    dm = def_ + r * (dg - jnp.mean(dg, axis=1, keepdims=True) - xh * jnp.mean(dg * xh, axis=1, keepdims=True))
    small[4:5, :W] = rsum(dm)
    db = dm.astype(BF)
    full[:, B:B + W] = db
    copies[3].wait()
    do = dot(db, wo_ref[...], 1, 1).astype(BF)
    for h in range(W // 128):
        c = h * 128
        q = two_heads((qkv_ref[:, c:c + 128].astype(F32) * (0.125 * LOG2E)).astype(BF))
        k = qkv_ref[:, W + c:W + c + 128]
        v = qkv_ref[:, 2 * W + c:2 * W + c + 128]
        k2 = two_heads(k)
        do2 = two_heads(do[:, c:c + 128])
        p = enc_probs(q, k, valid)
        dp = dot(do2, v, 1, 1)
        ds = (p * (dp - jnp.sum(dp * p, axis=1, keepdims=True))).astype(BF)
        p16 = p.astype(BF)
        full[:, Q + c:Q + c + 128] = ((dot(ds[:n], k2[:n]) + dot(ds[n:], k2[n:])) * 0.125).astype(BF)
        full[:, Q + W + c:Q + W + c + 128] = (dot(ds, q, 0, 0) * LN2).astype(BF)
        full[:, Q + 2 * W + c:Q + 2 * W + c + 128] = dot(p16, do2, 0, 0).astype(BF)
    small[2:3, :W] = rsum(full[:, Q:Q + W].astype(F32))
    small[3:4, :W] = rsum(full[:, Q + 2 * W:Q + 3 * W].astype(F32))
    copies[4].wait()
    da = dot(full[:, Q:Q + 3 * W], wqkv_ref[...], 1, 1)
    xh, r = norm_r(tok_ref[sec].astype(F32))
    small[0:1, :W] = rsum(da * xh)
    small[1:2, :W] = rsum(da)
    dg = da * row(0)
    dx = dm + r * (dg - jnp.mean(dg, axis=1, keepdims=True) - xh * jnp.mean(dg * xh, axis=1, keepdims=True))
    tokg[...] = dx.astype(BF)
    half = W // 2
    for ref, tref, s in ((mine_ref, tok_mine_ref, sec), (other_ref, tok_other_ref, 1 - sec)):
        tref[...] = tokg[:, aligned(s * half, half)]
        at = 0
        for start, size in ((0, half), (U, FF // 2), (B, half), (Q, 3 * half)):
            ref[:n, at:at + size] = full[:, pl.ds(pl.multiple_of(start + s * size, 128), size)]
            at += size
        ref[:n, at:] = dz_ref[...]
        ref[n:, :half] = small[:, aligned(s * half, half)].astype(BF)
        ref[n:, half:] = jnp.zeros((16, ref.shape[1] - half), BF)
        for t in range(FF // 2 // W):
            b = jnp.where(s == 0, small[8 + t:9 + t, :], small[8 + FF // 2 // W + t:9 + FF // 2 // W + t, :])
            ref[n + 8 + t:n + 9 + t, :W] = b.astype(BF)


def enc_bwd_call(sec, frames, seen, dz, tokens, vec, qkv, mid, gp, wp, w2, w1, wo, wqkv):
    n, W = tokens.shape[1], tokens.shape[2]
    FF = w1.shape[1]
    vm, hbm = pl.BlockSpec(memory_space=pltpu.VMEM), pl.BlockSpec(memory_space=pl.ANY)
    S = jax.ShapeDtypeStruct
    width = (5 * W + FF) // 2 + wp.shape[1]
    return pl.pallas_call(
        functools.partial(enc_bwd_kernel, W=W, FF=FF, seen=seen),
        in_specs=[pl.BlockSpec(memory_space=pltpu.SMEM)] * 2 + [vm] * 6 + [hbm] * 5,
        out_specs=[vm] * 4,
        out_shape=[S((n + 16, width), BF), S((n + 16, width), BF), S((n, W // 2), BF), S((n, W // 2), BF)],
        scratch_shapes=[pltpu.VMEM(w.shape, BF) for w in (wp, w2, w1, wo, wqkv)]
        + [pltpu.VMEM((n, 5 * W + FF), BF), pltpu.VMEM((n, W), BF), pltpu.VMEM((16, W), F32), pltpu.SemaphoreType.DMA((5,))],
        compiler_params=pltpu.CompilerParams(vmem_limit_bytes=VMEM),
        cost_estimate=pl.CostEstimate(flops=2_000_000_000, bytes_accessed=18_000_000, transcendentals=1_000_000),
        name="encoder_backward",
    )(sec, frames, dz, tokens, vec, qkv, mid, gp, wp, w2, w1, wo, wqkv)


PIECES = 8


def flat_blocks(W, FF, WD):
    half = W // 2
    return ((("down", FF, half // 128),), (("up", W, FF // 2 // 128),), (("qkv", W, 3 * half // 128), ("out", W, half // 128), ("proj", WD // 2, W // 128)))


def flat_rows(part, W, FF, WD):
    rows = sum(r * b for _, r, b in flat_blocks(W, FF, WD)[part])
    if part == 2:
        rows += 8 * (W // 2 // 128) + FF // 2 // 128
    unit = PIECES * 16
    return -(-rows // unit) * unit


def dec_share(part, W, FF, WD, WF):
    total = dec_blocks(WD, WF)["all"]
    flats = [flat_rows(i, W, FF, WD) for i in range(3)]
    counts = [((sum(flats) + total) // 3 - f) // (PIECES * 16) * (PIECES * 16) for f in flats[:2]]
    counts.append(total - sum(counts))
    return (sum(counts[:part]), counts[part])


def part_rows(part, W, FF, WD, WF):
    return flat_rows(part, W, FF, WD) + dec_share(part, W, FF, WD, WF)[1]


def weight_grad_kernel(idx_ref, acts_any, came_any, mine_any, dcame_any, pack_any, pack_came_any, give0, give1, give2, keep0, keep1, keep2,
                       flat0, flat1, flat2, acts, dy, dzt, small, pack, pack_came, out_sem, in_sem, *, W, FF, WD, WF):
    n = acts_any.shape[0]
    half = W // 2
    lhs = {"qkv": (0, W), "out": (W, W), "up": (2 * W, W), "down": (3 * W, FF), "proj": (3 * W + FF, W)}
    cols = {"down": (0, half), "up": (half, FF // 2), "out": (half + FF // 2, half), "qkv": (2 * half + FF // 2, 3 * half)}
    zc = 5 * half + FF // 2
    copies = []

    def fetch(src, dst):
        copies.append(pltpu.make_async_copy(src, dst, in_sem.at[len(copies)]))
        copies[-1].start()

    both = lambda rows, c, dst: [fetch(src.at[pl.ds(rows.start, rows.stop - rows.start), pl.ds(*c)], dst.at[pl.ds(k * (rows.stop - rows.start), rows.stop - rows.start), pl.ds(*c)])
                                 for k, src in enumerate((mine_any, dcame_any))]
    own = lambda c: [fetch(src.at[:, pl.ds(*c)], acts.at[pl.ds(k * n, n), pl.ds(*c)]) for k, src in enumerate((acts_any, came_any))]
    ready = {}
    for name, d in (("down", (0, half)), ("up", (half, FF // 2)), ("qkv", (half + FF // 2, mine_any.shape[1] - half - FF // 2))):
        both(slice(0, n), d, dy)
        own(lhs[name])
        ready[name] = len(copies)
    for name in ("out", "proj"):
        own(lhs[name])
        ready[name] = len(copies)
    both(slice(n, n + 16), (0, W), small)
    fetch(pack_any, pack)
    fetch(pack_came_any, pack_came)
    waited = 0
    step = 384
    for part, (flat, give, keep) in enumerate(((flat0, give0, keep0), (flat1, give1, keep1), (flat2, give2, keep2))):
        at = 0
        for name, rows, blocks in flat_blocks(W, FF, WD)[part]:
            while waited < ready[name]:
                copies[waited].wait()
                waited += 1
            a0, an = lhs[name]
            if name == "proj":
                dzt[...] = dy[:, zc:zc + WD].T
                g = dot(dzt[pl.ds(pl.multiple_of(idx_ref[0] * (WD // 2), 16), WD // 2), :], acts[:, a0:a0 + an]).astype(BF)
                for b in range(blocks):
                    flat[at:at + rows, :] = g[:, b * 128:b * 128 + 128]
                    at += rows
                continue
            d0, dn = cols[name]
            for r in range(0, rows, W):
                lt = acts[:, a0 + r:a0 + r + W].T
                for c in range(0, dn, step):
                    g = dot(lt, dy[:, d0 + c:d0 + c + step]).astype(BF)
                    for b in range(step // 128):
                        o = at + (c // 128 + b) * rows + r
                        flat[o:o + W, :] = g[:, b * 128:b * 128 + 128]
            at += rows * blocks
        if part == 0:
            for c in copies[waited:]:
                c.wait()
            waited = len(copies)
        first, count = dec_share(part, W, FF, WD, WF)
        if part == 2:
            total = small[:16, :].astype(F32) + small[16:, :].astype(F32)
            for b in range(half // 128):
                flat[at:at + 8, :] = total[0:8, b * 128:b * 128 + 128].astype(BF)
                at += 8
            tail = flat.shape[0] - count - at
            bias = [total[8 + t:9 + t, b * 128:b * 128 + 128] for t in range(FF // 2 // W) for b in range(W // 128)]
            bias = jnp.concatenate(bias + [jnp.zeros((tail - len(bias), 128), F32)], axis=0)
            flat[at:at + tail, :] = bias.astype(BF)
        flat[flat.shape[0] - count:, :] = (pack[first:first + count, :].astype(F32) + pack_came[first:first + count, :].astype(F32)).astype(BF)
        size = flat.shape[0] // PIECES
        me = idx_ref[1 + part]
        for p in range(PIECES // 2):
            src = lambda q: flat.at[pl.ds(pl.multiple_of((q ^ me) * size, 16), size), :]
            to = pl.ds(p * size, size)
            pltpu.make_async_copy(src(p), keep.at[to, :], out_sem.at[part]).start()
            pltpu.make_async_copy(src(p + PIECES // 2), give.at[to, :], out_sem.at[part]).start()
    for part, flat in enumerate((flat0, flat1, flat2)):
        pltpu.make_async_copy(flat, flat, out_sem.at[part]).wait()


def weight_grad_call(idx, acts, came, mine, dcame, pack, pack_came, W, FF, WD, WF):
    n = acts.shape[0]
    rows = [part_rows(i, W, FF, WD, WF) for i in range(3)]
    hbm = pl.BlockSpec(memory_space=pl.ANY)
    return pl.pallas_call(
        functools.partial(weight_grad_kernel, W=W, FF=FF, WD=WD, WF=WF),
        in_specs=[pl.BlockSpec(memory_space=pltpu.SMEM)] + [hbm] * 6,
        out_specs=[hbm] * 6,
        out_shape=[jax.ShapeDtypeStruct((r // 2, 128), BF) for r in rows] * 2,
        scratch_shapes=[pltpu.VMEM((r, 128), BF) for r in rows] + [pltpu.VMEM((2 * n, acts.shape[1]), BF), pltpu.VMEM((2 * n, mine.shape[1]), BF),
                        pltpu.VMEM((WD, 2 * n), BF), pltpu.VMEM((32, W), BF), pltpu.VMEM(pack.shape, BF), pltpu.VMEM(pack.shape, BF),
                        pltpu.SemaphoreType.DMA((3,)), pltpu.SemaphoreType.DMA((24,))],
        compiler_params=pltpu.CompilerParams(vmem_limit_bytes=VMEM),
        cost_estimate=pl.CostEstimate(flops=1_700_000_000, bytes_accessed=20_000_000, transcendentals=0),
        name="encoder_weight_gradients",
    )(idx, acts, came, mine, dcame, pack, pack_came)


def unpack_kernel(idx_ref, own0, own1, own2, came0, came1, came2, *refs, W, FF, WD, WF, slots, patches):
    down, up, qkv, out, proj, vec_ref, bias_ref, sq_ref = refs[:8]
    dec_refs, refs = refs[8:16], refs[16:]
    flats, stages, pack, fetch_sem, store_sem = refs[:3], refs[3:8], refs[8], refs[9], refs[10]
    for i, (own, came) in enumerate(((own0, came0), (own1, came1), (own2, came2))):
        me = idx_ref[1 + i]
        size = flats[i].shape[0] // PIECES

        def fetch(p, k, own=own, came=came, me=me, flat=flats[i], size=size, i=i):
            to = lambda q: flat.at[pl.ds(pl.multiple_of((q ^ me) * size, 16), size), :]
            src = pl.ds(pl.multiple_of(p * size, 16), size)
            pltpu.make_async_copy(own.at[src, :], to(p), fetch_sem.at[i]).start()
            pltpu.make_async_copy(came.at[src, :], to(p + PIECES // 2), fetch_sem.at[i]).start()
            return k

        lax.fori_loop(0, PIECES // 2, fetch, 0)
    named = dict(zip(("down", "up", "qkv", "out", "proj"), zip((down, up, qkv, out, proj), stages)))
    enc = jnp.zeros((8, 128), F32)
    dec = jnp.zeros((8, 128), F32)
    fold = lambda v: jnp.sum((v * v).reshape(-1, 8, 128), axis=0)
    stores = []
    for part, flat in enumerate(flats):
        pltpu.make_async_copy(flat, flat, fetch_sem.at[part]).wait()
        first, count = dec_share(part, W, FF, WD, WF)
        pack[first:first + count, :] = flat[flat.shape[0] - count:, :]
        at = 0
        for name, rows, blocks in flat_blocks(W, FF, WD)[part]:
            ref, stage = named[name]
            for b in range(blocks):
                g = flat[at:at + rows, :].astype(F32)
                c = slice(b * 128, b * 128 + 128)
                stage[:, c] = g
                if name == "proj":
                    dec += fold(g)
                else:
                    enc += fold(g)
                at += rows
                if b % 3 == 2:
                    cols = pl.ds(b * 128 - 256, 384)
                    stores.append(pltpu.make_async_copy(stage.at[:, cols], ref.at[:, cols], store_sem.at[len(stores)]))
                    stores[-1].start()
    for b in range(W // 2 // 128):
        g = flat[at:at + 8, :].astype(F32)
        enc += g * g
        vec_ref[:, b * 128:b * 128 + 128] = g
        at += 8
    g = flat[at:at + 16, :].astype(F32)[:FF // 2 // 128]
    bias_ref[...] = g
    enc += jnp.concatenate([jnp.sum(g * g, axis=0, keepdims=True), jnp.zeros((7, 128), F32)], axis=0)
    dec += finish(lambda at, n: pack[at:at + n, :], *dec_refs, W=WD, FF=WF, slots=slots, patches=patches)
    sq_ref[:8, :] = enc
    sq_ref[8:, :] = dec
    for s in stores:
        s.wait()


def unpack_call(idx, own, came, slots, patches, W, FF, WD, WF):
    vm, hbm = pl.BlockSpec(memory_space=pltpu.VMEM), pl.BlockSpec(memory_space=pl.ANY)
    S = lambda *shape: jax.ShapeDtypeStruct(shape, F32)
    half = W // 2
    wh = WD // 2
    dec = [S(3 * wh, WD), S(wh, WD), S(WD, WF // 2), S(wh, WF), S(9, wh), S(8, WF // 2), S(slots, wh), S(patches, wh)]
    big = [S(FF, half), S(W, FF // 2), S(W, 3 * half), S(W, half), S(WD // 2, W)]
    return pl.pallas_call(
        functools.partial(unpack_kernel, W=W, FF=FF, WD=WD, WF=WF, slots=slots, patches=patches),
        in_specs=[pl.BlockSpec(memory_space=pltpu.SMEM)] + [hbm] * 6,
        out_specs=[hbm] * 5 + [vm] * 11,
        out_shape=big + [S(8, half), S(FF // 2 // 128, 128), S(16, 128)] + dec,
        scratch_shapes=[pltpu.VMEM((part_rows(i, W, FF, WD, WF), 128), BF) for i in range(3)] + [pltpu.VMEM(s.shape, F32) for s in big]
        + [pltpu.VMEM((dec_blocks(WD, WF)["all"], 128), BF)]
        + [pltpu.SemaphoreType.DMA((3,)), pltpu.SemaphoreType.DMA((sum(s.shape[1] // 384 for s in big),))],
        compiler_params=pltpu.CompilerParams(vmem_limit_bytes=VMEM),
        cost_estimate=pl.CostEstimate(flops=10_000_000, bytes_accessed=23_000_000, transcendentals=0),
        name="unpack",
    )(idx, *own, *came)


def pair_kernel(sec_ref, dec_mine, dec_came, tok_mine, tok_came, dec_ref, tok_ref):
    sec = sec_ref[0]
    for ref, mine, came in ((dec_ref, dec_mine, dec_came), (tok_ref, tok_mine, tok_came)):
        ref[sec] = mine[...]
        ref[1 - sec] = came[...]


def pair_call(sec, *arrays):
    vm = pl.BlockSpec(memory_space=pltpu.VMEM)
    return pl.pallas_call(
        pair_kernel,
        in_specs=[pl.BlockSpec(memory_space=pltpu.SMEM)] + [vm] * 4,
        out_specs=[vm] * 2,
        out_shape=[jax.ShapeDtypeStruct((2, *arrays[i].shape), BF) for i in (0, 2)],
        compiler_params=pltpu.CompilerParams(vmem_limit_bytes=VMEM),
        cost_estimate=pl.CostEstimate(flops=1000, bytes_accessed=1000, transcendentals=0),
        name="both_clips",
    )(sec, *arrays)


SIDE = 4


def coordinates(index):
    return (index // (SIDE * SIDE), index // SIDE % SIDE, index % SIDE)


def flip(place, axis, kind):
    place = list(place)
    place[axis] = place[axis] ^ 1 if kind == 0 else SIDE - 1 - place[axis]
    return tuple(place)


def swap(value, axes, far):
    pairs = []
    for core in range(2):
        for index in range(SIDE**3):
            place = coordinates(index)
            for axis in axes:
                place = flip(place, axis, core ^ far)
            target = (place[0] * SIDE + place[1]) * SIDE + place[2]
            pairs.append((core * SIDE**3 + index, core * SIDE**3 + target))
    return lax.ppermute(value, ("section", "dp"), pairs)


def add(left, right):
    return (left.astype(jnp.float32) + right.astype(jnp.float32)).astype(jnp.bfloat16)


def piece_numbers(place, core):
    near = [1 * ((p == 1) | (p == 2)) for p in place]
    far = [1 * (p >= 2) for p in place]
    first = [(1 - core) * a + core * b for a, b in zip(near, far)]
    return [first[i] * 4 + first[(i + 1) % 3] * 2 + first[(i + 2) % 3] for i in range(3)]


def halve(v, axis, far):
    half = v.shape[0] // 2
    return add(v[:half], swap(v[half:], (axis,), far))


def sum_over_chips(pairs):
    own, came = [], []
    for i, (give, keep) in enumerate(pairs):
        v = add(keep, swap(give, (i,), 0))
        for step in (1, 2):
            v = halve(v, (i + step) % 3, 0)
        for step in range(3):
            v = add(v, swap(v, ((i + step) % 3,), 1))
        for step in (2, 1):
            v = jnp.concatenate([v, swap(v, ((i + step) % 3,), 0)])
        own.append(v)
        came.append(swap(v, (i,), 0))
    return (own, came)


def from_partner(value):
    return lax.ppermute(value, "section", [(0, 1), (1, 0)])


def shards(
    tokens,
    frames,
    visible,
    out_grad,
    enc_vectors,
    enc_qkv,
    enc_out,
    enc_up,
    enc_up_bias,
    enc_down,
    proj_weight,
    dec_vectors,
    dec_qkv,
    dec_out,
    dec_up,
    dec_up_bias,
    dec_down,
    time_pos,
    space_pos,
):
    enc_width, enc_hidden = enc_up.shape
    dec_width, dec_hidden = dec_up.shape
    slot_count = time_pos.shape[0]
    patch_count = space_pos.shape[0]
    seen_count = visible.shape[1]
    section = lax.axis_index("section").astype(jnp.int32)
    core = section.reshape(1)
    sizes = (enc_width, enc_hidden, dec_width, dec_hidden)
    acts, qkv, mid, slopes, projected = enc_fwd_call(
        core, frames, seen_count, tokens, enc_vectors, enc_up_bias, enc_qkv, enc_out, enc_up, enc_down, proj_weight
    )
    acts_came = from_partner(acts)
    (decoded_mine, decoded_other), grad_projected, (dec_mine, dec_other) = dec_block_call(
        core,
        frames,
        visible,
        projected,
        time_pos,
        space_pos,
        dec_vectors,
        dec_qkv,
        dec_out,
        dec_up,
        dec_up_bias,
        dec_down,
        out_grad,
        TQ=384,
        TA=640,
    )
    dec_came = from_partner(dec_other)
    dy_mine, dy_other, token_mine, token_other = enc_bwd_call(
        core, frames, seen_count, grad_projected, tokens, enc_vectors, qkv, mid, slopes, proj_weight, enc_down, enc_up, enc_out, enc_qkv
    )
    dy_came = from_partner(dy_other)
    places = jnp.stack([section, *piece_numbers(coordinates(lax.axis_index("dp")), section)]).astype(jnp.int32)
    pieces = weight_grad_call(places, acts, acts_came, dy_mine, dy_came, dec_mine, dec_came, *sizes)
    own, came = sum_over_chips(list(zip(pieces[:3], pieces[3:])))
    decoded_came = from_partner(decoded_other)
    token_came = from_partner(token_other)
    decoded, token_grad = pair_call(core, decoded_mine, decoded_came, token_mine, token_came)
    (
        g_enc_down, g_enc_up, g_enc_qkv, g_enc_out, g_proj, g_vectors, g_enc_bias, squares,
        g_dec_qkv, g_dec_out, g_dec_up, g_dec_down, g_dec_vectors, g_dec_bias, g_time, g_space,
    ) = unpack_call(places, own, came, slot_count, patch_count, *sizes)
    enc_squares, dec_squares = squares[:8], squares[8:]
    give = jnp.where(section == 0, dec_squares, enc_squares)
    keep = jnp.where(section == 0, enc_squares, dec_squares)
    norms = jnp.sum(keep + from_partner(give)).reshape(1)
    return (
        decoded.transpose(0, 2, 1),
        token_grad,
        g_vectors,
        g_enc_qkv,
        g_enc_out,
        g_enc_up,
        g_enc_bias.reshape(-1),
        g_enc_down,
        g_proj.T,
        g_dec_vectors,
        g_dec_qkv.T,
        g_dec_out.T,
        g_dec_up,
        g_dec_bias[0],
        g_dec_down.T,
        g_time,
        g_space,
        norms,
    )


from jax.sharding import PartitionSpec as P


def solution(mesh):
    placed = (
        P("dp", None, None),
        P("dp"),
        P("dp", None),
        P("dp", None, None),
        P(),
        P(),
        P(),
        P(),
        P(),
        P(),
        P(),
        P(),
        P(),
        P(),
        P(),
        P(),
        P(),
        P(),
        P(),
    )
    return jax.shard_map(
        shards,
        mesh=mesh,
        in_specs=placed,
        out_specs=(
            P("dp", None, "section"),
            P("dp", None, "section"),
            P(None, "section"),
            P(None, "section"),
            P(None, "section"),
            P(None, "section"),
            P("section"),
            P(None, "section"),
            P(None, "section"),
            P(None, "section"),
            P(None, "section"),
            P(None, "section"),
            P(None, "section"),
            P("section"),
            P(None, "section"),
            P(None, "section"),
            P(None, "section"),
            P("section"),
        ),
        check_vma=False,
    )
```

```python
import functools
import jax, jax.numpy as jnp, numpy as np
from jax import lax
from jax.experimental import pallas as pl
from jax.experimental.pallas import tpu as pltpu

EPS = 1e-6
NEG = -1e9
LOG2E = 1.4426950408889634
LN2 = 0.6931471805599453
F32, BF = jnp.float32, jnp.bfloat16


def dot(a, b, ca=1, cb=0):
    return lax.dot_general(a, b, (((ca,), (cb,)), ((), ())), preferred_element_type=F32)


def tiles_of(total, size):
    return [(s, min(size, total - s)) for s in range(0, total, size)]


def over(total, size, body, carry):
    full = total // size
    if full:
        carry = lax.fori_loop(0, full, lambda i, k: body(pl.ds(pl.multiple_of(i * size, 128), size), size, k), carry)
    if total % size:
        carry = body(pl.ds(full * size, total % size), total % size, carry)
    return carry


def norm_c(x):
    mean = jnp.mean(x, axis=0, keepdims=True)
    c = x - mean
    r = lax.rsqrt(jnp.mean(c * c, axis=0, keepdims=True) + EPS)
    return c * r, r


def gelu_pair(u):
    a = jnp.abs(u)
    t = 1.0 / (1.0 + (0.3275911 * 0.7071067811865476) * a)
    e = jnp.exp2((-0.5 * LOG2E) * (u * u))
    poly = t * (0.5 * 0.254829592 + t * (0.5 * -0.284496736 + t * (0.5 * 1.421413741 + t * (0.5 * -1.453152027 + t * (0.5 * 1.061405429)))))
    tail = poly * e
    phi = jnp.where(u >= 0, 1.0 - tail, tail)
    return u * phi, phi + u * (e * 0.3989422804014327)


def dec_kernel(sec_ref, frames_ref, vis_ref, proj_ref, time_ref, space_ref, vecs_ref, wqkv_ref, wo_ref, w1_ref, bias_ref, w2_ref, dy_any,
               out_refs, dz_ref, pack_refs,
               x_s, a1_s, qkv_s, e_s, l_s, o_s, m_s, a2_s, g_s, gp_s, dy_s, db_s, sel_s, doa_s, do_s, o32_s, dy_ref, vec_ref, b1_ref, dec_s, dy_sem, *, W, L, H, FF, V, slots, patches, TQ, TA):
    dqkv_s, ds_s = g_s, gp_s
    sec = sec_ref[0]
    used = frames_ref[sec] // 2
    valid = used * patches
    dy_copy = pltpu.make_async_copy(dy_any.at[sec], dy_ref, dy_sem)
    dy_copy.start()
    seen_count = V // slots
    vecs = vecs_ref[...].astype(F32)
    vec_ref[...] = jnp.concatenate([vecs, jnp.zeros((16 - vecs.shape[0], W), F32)], axis=0).T
    b1_ref[...] = jnp.broadcast_to(bias_ref[...].reshape(1, FF).astype(F32), (8, FF)).T[:, 0:1]
    col = lambda i: vec_ref[:, i:i + 1]
    HS = 64
    lane = lax.broadcasted_iota(jnp.int32, (1, L), 1)
    vrow = lax.broadcasted_iota(jnp.int32, (V, 1), 0)
    vslot = jnp.zeros((V, 1), jnp.int32)
    for t in range(1, slots):
        vslot += (vrow >= t * seen_count).astype(jnp.int32)
    vrank = vrow - vslot * seen_count
    target = vslot * patches
    for j in range(seen_count):
        target += jnp.where(vrank == j, vis_ref[sec, j], 0)
    onehot = (target == lax.broadcasted_iota(jnp.int32, (V, L), 1)).astype(F32)
    slot = jnp.zeros((1, L), jnp.int32)
    for t in range(1, slots):
        slot += (lane >= t * patches).astype(jnp.int32)
    patch_oh = (lax.broadcasted_iota(jnp.int32, (patches, L), 0) == lane - slot * patches).astype(BF)
    seen = jnp.sum(onehot, axis=0, keepdims=True)
    srow = lax.broadcasted_iota(jnp.int32, (32, L), 0)
    slot_oh = jnp.where(srow < 16, ((srow & 7) == slot).astype(F32), jnp.where(srow == 16, 1.0 - seen, 0.0)).astype(BF)
    sel_s[:V, :] = onehot.astype(BF)
    sel_s[V:V + patches, :] = patch_oh
    sel_s[V + patches:, :] = slot_oh
    ti = lax.broadcasted_iota(jnp.int32, (slots, slots), 0)
    ii = lax.broadcasted_iota(jnp.int32, (slots, slots), 1)
    num = ti * (slots - 1)
    lower = jnp.zeros((slots, slots), jnp.int32)
    for q in range(1, (slots - 1) * (slots - 1) + 1):
        lower += (num >= q * (used - 1)).astype(jnp.int32)
    frac = (num - lower * (used - 1)).astype(F32) / jnp.full((slots, slots), used - 1, jnp.int32).astype(F32)
    upper = jnp.minimum(lower + 1, slots - 1)
    table = (1.0 - frac) * (ii == lower).astype(F32) + frac * (ii == upper).astype(F32)
    exact = lambda a, b, ca, cb: lax.dot_general(a, b, (((ca,), (cb,)), ((), ())), precision=lax.Precision.HIGHEST, preferred_element_type=F32)
    spos = exact(table, time_ref[...].astype(F32), 1, 0)
    shi = spos.astype(BF)
    slo = (spos - shi.astype(F32)).astype(BF)
    proj = proj_ref[...]
    hi = proj.astype(BF)
    lo = (proj - hi.astype(F32)).astype(BF)
    mask = vecs[8:9, :].astype(BF)
    src = jnp.concatenate([hi.astype(F32), space_ref[...].astype(F32), shi.astype(F32), slo.astype(F32), mask.astype(F32), jnp.zeros((15, W), F32)], axis=0).astype(BF)

    def first(c, n, k):
        x = dot(src, sel_s[:, c], 0, 0) + dot(lo, sel_s[:V, c], 0, 0)
        x_s[:, c] = x
        xh, _ = norm_c(x)
        a1 = (xh * col(0) + col(1)).astype(BF)
        a1_s[:, c] = a1
        j = dot(wqkv_ref[...], a1, 0, 0)
        qkv_s[:W, c] = ((j[:W] + col(2)) * (0.125 * LOG2E)).astype(BF)
        qkv_s[W:2 * W, c] = j[W:2 * W].astype(BF)
        qkv_s[2 * W:, c] = (j[2 * W:] + col(3)).astype(BF)
        return k

    over(L, TQ, first, 0)
    arow = lax.broadcasted_iota(jnp.int32, (16, L), 0)
    kbias = jnp.where((arow == 0) & (lane >= valid), NEG, 0.0).astype(BF)
    one0 = (arow == 0).astype(BF)
    one01 = (arow < 2).astype(BF)

    def fwd_head(h, carry):
        hs = pl.ds(pl.multiple_of(h * HS, HS), HS)
        ks = pl.ds(pl.multiple_of(W + h * HS, HS), HS)
        vs = pl.ds(pl.multiple_of(2 * W + h * HS, HS), HS)
        kr = jnp.concatenate([qkv_s[ks, :], kbias], axis=0).T
        vc = jnp.concatenate([qkv_s[vs, :], one0], axis=0)

        def tile(c, n, exact):
            qc = jnp.concatenate([qkv_s[hs, c], one0[:, :n]], axis=0)
            st = dot(kr, qc)
            if exact:
                st = st - jnp.max(st, axis=0, keepdims=True)
            e = jnp.exp2(st).astype(BF)
            e_s[h, :, c] = e
            oa = dot(vc, e)
            rl = 1.0 / oa[HS:HS + 1]
            l_s[h, :, c] = jnp.broadcast_to(rl, (8, n))
            o = oa[:HS] * rl
            o32_s[hs, c] = o
            o_s[hs, c] = o.astype(BF)

        square = lambda v: jnp.max(jnp.sum(v * v, axis=0))
        bound = square(qkv_s[hs, :].astype(F32)) * square(qkv_s[ks, :].astype(F32))

        @pl.when(bound <= 60.0 * 60.0)
        def _():
            over(L, TA, lambda c, n, k: (tile(c, n, False), k)[1], 0)

        @pl.when(jnp.logical_not(bound <= 60.0 * 60.0))
        def _():
            over(L, TA, lambda c, n, k: (tile(c, n, True), k)[1], 0)

        return carry

    lax.fori_loop(0, H, fwd_head, 0)

    def middle(c, n, sums):
        sum_b1, sum_dy, sum_g2, sum_s2, sum_db = sums
        live = (lax.broadcasted_iota(jnp.int32, (1, n), 1) + c.start < valid).astype(F32)
        mid = x_s[:, c] + (dot(wo_ref[...], o_s[:, c], 0, 0) + col(4))
        xh, r = norm_c(mid)
        a2 = (xh * col(5) + col(6)).astype(BF)
        a2_s[:, c] = a2
        u = dot(w1_ref[...], a2, 0, 0) + b1_ref[...]
        g, gp = gelu_pair(u)
        g = g.astype(BF)
        g_s[:, c] = g
        y = mid + (dot(w2_ref[...], g, 0, 0) + col(7))
        dec_s[:, c] = (y * live).astype(BF)
        dyf = dy_ref[c, :].astype(F32).T * live
        dy = dyf.astype(BF)
        dy_s[:, c] = dy
        duf = gp * dot(w2_ref[...], dy)
        du = duf.astype(BF)
        gp_s[:, c] = du
        da2 = dot(w1_ref[...], du)
        dg = da2 * col(5)
        dm = dyf + r * (dg - jnp.mean(dg, axis=0, keepdims=True) - xh * jnp.mean(dg * xh, axis=0, keepdims=True))
        db = dm.astype(BF)
        db_s[:, c] = db
        do_s[:, c] = dot(wo_ref[...], db).astype(BF)
        m_s[:, c] = dm
        rs = lambda v: jnp.sum(v, axis=1, keepdims=True)
        return (sum_b1 + rs(duf), sum_dy + rs(dyf), sum_g2 + rs(da2 * xh), sum_s2 + rs(da2), sum_db + rs(dm))

    dy_copy.wait()
    zero = jnp.zeros((W, 1), F32)
    sum_b1, sum_dy, sum_g2, sum_s2, sum_db = over(L, TQ, middle, (jnp.zeros((FF, 1), F32), zero, zero, zero, zero))
    blocks = dec_blocks(W, FF)
    for who, s in enumerate((sec, 1 - sec)):
        rows = lambda size, at=0: pl.ds(pl.multiple_of(s * (size // 2) + at, 16), W // 2)
        out_refs[who][...] = dec_s[rows(W), :]
        pack = pack_refs[who]
        for b in range(FF // W):
            put(pack, blocks["down"] + b * 3 * (W // 2), dot(dy_s[rows(W), :], g_s[b * W:b * W + W, :], 1, 1))
        for b in range(FF // 2 // W):
            put(pack, blocks["up"] + b * 3 * W, dot(a2_s[...], gp_s[pl.ds(pl.multiple_of(s * (FF // 2) + b * W, 16), W), :], 1, 1))
        put(pack, blocks["out"], dot(db_s[rows(W), :], o_s[...], 1, 1))

    def bwd_head(h, carry):
        hs = pl.ds(pl.multiple_of(h * HS, HS), HS)
        ks = pl.ds(pl.multiple_of(W + h * HS, HS), HS)
        vs = pl.ds(pl.multiple_of(2 * W + h * HS, HS), HS)
        vr = jnp.concatenate([qkv_s[vs, :], one01], axis=0).T
        kc = qkv_s[ks, :]
        dob = (do_s[hs, :].astype(F32) * l_s[h, 0:1, :]).astype(BF)
        dl = -jnp.sum(dob.astype(F32) * o32_s[hs, :], axis=0, keepdims=True)
        dlh = dl.astype(BF).astype(F32)
        doa_s[:HS, :] = dob
        doa_s[HS:, :] = jnp.where(arow == 0, dlh, jnp.where(arow == 1, dl - dlh, 0.0)).astype(BF)
        def tile(c, n, k):
            dp = dot(vr, doa_s[:, c])
            ds = (e_s[h, :, c].astype(F32) * dp).astype(BF)
            ds_s[:L, c] = ds
            dqkv_s[hs, c] = (dot(kc, ds) * 0.125).astype(BF)
            return k

        over(L, TA, tile, 0)
        dor = doa_s[:HS, :].T
        qr = qkv_s[hs, :].T

        def tile2(c, n, k):
            dqkv_s[vs, c] = dot(e_s[h, c, :], dor).T.astype(BF)
            dqkv_s[ks, c] = (dot(ds_s[c, :], qr) * LN2).T.astype(BF)
            return k

        return over(L, TA, tile2, carry)

    lax.fori_loop(0, H, bwd_head, 0)
    def last(c, n, sums):
        sum_g1, sum_s1, sum_q, sum_v, gsel = sums
        rs = lambda v: jnp.sum(v, axis=1, keepdims=True)
        da = dot(wqkv_ref[...], dqkv_s[:3 * W, c])
        xh, r = norm_c(x_s[:, c])
        dg = da * col(0)
        dx = m_s[:, c] + r * (dg - jnp.mean(dg, axis=0, keepdims=True) - xh * jnp.mean(dg * xh, axis=0, keepdims=True))
        return (sum_g1 + rs(da * xh), sum_s1 + rs(da), sum_q + rs(dqkv_s[:W, c].astype(F32)), sum_v + rs(dqkv_s[2 * W:3 * W, c].astype(F32)),
                gsel + dot(dx.astype(BF), sel_s[:, c], 1, 1))

    sum_g1, sum_s1, sum_q, sum_v, gsel = over(L, TQ, last, (zero, zero, zero, zero, jnp.zeros((W, sel_s.shape[0]), F32)))
    dz_ref[...] = gsel[:, :V].T.astype(BF)
    small = o32_s
    small[:, :8] = jnp.concatenate([sum_g1, sum_s1, sum_q, sum_v, sum_db, sum_g2, sum_s2, sum_dy], axis=1)
    small[:, 8:16] = gsel[:, V + patches + 16:V + patches + 24]
    small[:, 16:24] = exact(gsel[:, V + patches:V + patches + slots], table, 1, 0)
    small[:, 24:24 + patches] = gsel[:, V:V + patches]
    small[:, 24 + patches:256] = jnp.zeros((W, 256 - 24 - patches), F32)
    for who, s in enumerate((sec, 1 - sec)):
        pack = pack_refs[who]
        put(pack, blocks["qkv"], dot(dqkv_s[pl.ds(pl.multiple_of(s * (3 * W // 2), 16), 3 * W // 2), :], a1_s[...], 1, 1))
        half = small[pl.ds(pl.multiple_of(s * (W // 2), 8), W // 2), :256].T[:32 + patches]
        put(pack, blocks["small"], jnp.concatenate([half, jnp.zeros((32 + patches, 256 - W // 2), F32)], axis=1))
        b1_ref[...] = sum_b1
        put(pack, blocks["bias"], jnp.broadcast_to(b1_ref[pl.ds(pl.multiple_of(s * (FF // 2), 8), FF // 2), :], (FF // 2, 128)).T[:16])
        pack[blocks["end"]:, :] = jnp.zeros((pack.shape[0] - blocks["end"], 128), BF)


def put(pack, at, value):
    n = value.shape[0]
    for b in range(value.shape[1] // 128):
        pack[at + b * n:at + b * n + n, :] = value[:, b * 128:b * 128 + 128].astype(BF)


def dec_blocks(W, FF):
    at, rows = 0, {}
    for name, count in (("qkv", 3 * (3 * W // 2)), ("out", 3 * (W // 2)), ("up", 3 * (FF // 2)), ("down", 3 * (FF // 2)), ("small", 2 * 176), ("bias", 16 * (FF // 2 // 128))):
        rows[name] = at
        at += count
    rows["end"] = at
    unit = 3 * 8 * 16
    rows["all"] = -(-at // unit) * unit
    return rows


def finish(read, qkv_ref, out_ref, up_ref, down_ref, vec_ref, bias_ref, time_ref, space_ref, *, W, FF, slots, patches):
    blocks = dec_blocks(W, FF)
    total = jnp.zeros((8, 128), F32)
    fold = lambda v: jnp.sum((v * v).reshape(-1, 8, 128), axis=0)
    for name, ref, n, parts in (("qkv", qkv_ref, 3 * W // 2, 1), ("out", out_ref, W // 2, 1), ("up", up_ref, W, FF // 2 // W), ("down", down_ref, W // 2, FF // W)):
        for b in range(3 * parts):
            g = read(blocks[name] + b * n, n).astype(F32)
            ref[:, b * 128:b * 128 + 128] = g
            total += fold(g)
    low = read(blocks["small"], 176).astype(F32)
    high = read(blocks["small"] + 176, 176).astype(F32)
    total += fold(low) + fold(high)
    for ref, at, n in ((vec_ref, 0, 9), (time_ref, 16, slots), (space_ref, 16 + slots, patches)):
        ref[:, :128] = low[at:at + n]
        ref[:, 128:] = high[at:at + n, :W // 2 - 128]
    for b in range(FF // 2 // 128):
        g = read(blocks["bias"] + 16 * b, 16).astype(F32)
        bias_ref[:, b * 128:b * 128 + 128] = g[:8]
        total += 0.0625 * fold(g)
    return total


def dec_block_call(sec, frames, visible, proj, time_pos, space, vecs, wqkv, wo, w1, bias, w2, dy, TQ, TA):
    W, L, FF = wqkv.shape[0], dy.shape[1], w1.shape[1]
    H = W // 64
    patches, slots = space.shape[0], time_pos.shape[0]
    V = proj.shape[0]
    sm, vm = pl.BlockSpec(memory_space=pltpu.SMEM), pl.BlockSpec(memory_space=pltpu.VMEM)
    S = jax.ShapeDtypeStruct
    return pl.pallas_call(
        functools.partial(dec_kernel, W=W, L=L, H=H, FF=FF, V=V, slots=slots, patches=patches, TQ=TQ, TA=TA),
        in_specs=[sm, sm, sm] + [vm] * 9 + [pl.BlockSpec(memory_space=pl.ANY)],
        out_specs=[[vm] * 2, vm, [vm] * 2],
        out_shape=[[S((W // 2, L), BF)] * 2, S((V, W), BF), [S((dec_blocks(W, FF)["all"], 128), BF)] * 2],
        scratch_shapes=[
            pltpu.VMEM((W, L), F32),
            pltpu.VMEM((W, L), BF),
            pltpu.VMEM((3 * W, L), BF),
            pltpu.VMEM((H, L, L), BF),
            pltpu.VMEM((H, 8, L), F32),
            pltpu.VMEM((W, L), BF),
            pltpu.VMEM((W, L), F32),
            pltpu.VMEM((W, L), BF),
            pltpu.VMEM((FF, L), BF),
            pltpu.VMEM((FF, L), BF),
            pltpu.VMEM((W, L), BF),
            pltpu.VMEM((W, L), BF),
            pltpu.VMEM((V + patches + 32, L), BF),
            pltpu.VMEM((80, L), BF),
            pltpu.VMEM((W, L), BF),
            pltpu.VMEM((W, L), F32),
            pltpu.VMEM((L, W), BF),
            pltpu.VMEM((W, 16), F32),
            pltpu.VMEM((FF, 1), F32),
            pltpu.VMEM((W, L), BF),
            pltpu.SemaphoreType.DMA,
        ],
        compiler_params=pltpu.CompilerParams(vmem_limit_bytes=63 * 1024 * 1024),
        cost_estimate=pl.CostEstimate(flops=28_000_000_000, bytes_accessed=12_000_000, transcendentals=10_000_000),
        name="decoder",
    )(sec, frames, visible, proj, time_pos, space, vecs, wqkv, wo, w1, bias, w2, dy)


VMEM = 63 * 1024 * 1024


def aligned(start, size):
    return pl.ds(pl.multiple_of(start, size), size)


def norm_r(x):
    mean = jnp.mean(x, axis=1, keepdims=True)
    c = x - mean
    r = lax.rsqrt(jnp.mean(c * c, axis=1, keepdims=True) + EPS)
    return c * r, r


def enc_probs(qm, k, valid):
    s = dot(qm, k, 1, 1)
    live = lax.broadcasted_iota(jnp.int32, s.shape, 1) < valid
    s = jnp.where(live, s, NEG)
    e = jnp.exp2(s - jnp.max(s, axis=1, keepdims=True))
    return e / jnp.sum(e, axis=1, keepdims=True)


def two_heads(v):
    low = lax.broadcasted_iota(jnp.int32, v.shape, 1) < 64
    zero = jnp.zeros_like(v)
    return jnp.concatenate([jnp.where(low, v, zero), jnp.where(low, zero, v)], axis=0)


def enc_fwd_kernel(sec_ref, frames_ref, tok_ref, vec_ref, b1_ref, wqkv_any, wo_any, w1_any, w2_any, wp_any,
                   acts_ref, qkv_ref, mid_ref, gp_ref, proj_ref,
                   wqkv_ref, wo_ref, w1_ref, w2_ref, wp_ref, sem, *, W, FF, seen):
    pairs = ((wqkv_any, wqkv_ref), (wo_any, wo_ref), (w1_any, w1_ref), (w2_any, w2_ref), (wp_any, wp_ref))
    copies = [pltpu.make_async_copy(a, b, sem.at[i]) for i, (a, b) in enumerate(pairs)]
    for c in copies[:2]:
        c.start()

    def arrived(i):
        copies[i].wait()
        if i + 2 < len(copies):
            copies[i + 2].start()

    sec = sec_ref[0]
    valid = frames_ref[sec] // 2 * seen
    vec = vec_ref[...].astype(F32)
    row = lambda i: vec[i:i + 1, :]
    x = tok_ref[sec].astype(F32)
    n = x.shape[0]
    xh, _ = norm_r(x)
    a1 = (xh * row(0) + row(1)).astype(BF)
    acts_ref[:, :W] = a1
    arrived(0)
    j = dot(a1, wqkv_ref[...])
    qkv_ref[:, :W] = (j[:, :W] + row(2)).astype(BF)
    qkv_ref[:, W:2 * W] = j[:, W:2 * W].astype(BF)
    qkv_ref[:, 2 * W:] = (j[:, 2 * W:] + row(3)).astype(BF)
    for h in range(W // 128):
        s = slice(h * 128, h * 128 + 128)
        q = (qkv_ref[:, s].astype(F32) * (0.125 * LOG2E)).astype(BF)
        p = enc_probs(two_heads(q), qkv_ref[:, W + h * 128:W + h * 128 + 128], valid).astype(BF)
        v = two_heads(qkv_ref[:, 2 * W + h * 128:2 * W + h * 128 + 128])
        acts_ref[:, W + h * 128:W + h * 128 + 128] = (dot(p[:n], v[:n]) + dot(p[n:], v[n:])).astype(BF)
    arrived(1)
    mid = x + (dot(acts_ref[:, W:2 * W], wo_ref[...]) + row(4))
    mid_ref[...] = mid
    xh, _ = norm_r(mid)
    a2 = (xh * row(5) + row(6)).astype(BF)
    acts_ref[:, 2 * W:3 * W] = a2
    arrived(2)
    for f in range(0, FF, W):
        g, gp = gelu_pair(dot(a2, w1_ref[:, f:f + W]) + b1_ref[f:f + W].astype(F32).reshape(1, W))
        acts_ref[:, 3 * W + f:3 * W + f + W] = g.astype(BF)
        gp_ref[:, f:f + W] = gp.astype(BF)
    arrived(3)
    y = mid + (dot(acts_ref[:, 3 * W:3 * W + FF], w2_ref[...]) + row(7))
    enc = y.astype(BF)
    acts_ref[:, 3 * W + FF:] = enc
    arrived(4)
    proj_ref[...] = dot(enc, wp_ref[...])


def enc_fwd_call(sec, frames, seen, tokens, vec, b1, wqkv, wo, w1, w2, wp):
    n, W = tokens.shape[1], tokens.shape[2]
    FF = w1.shape[1]
    vm, hbm = pl.BlockSpec(memory_space=pltpu.VMEM), pl.BlockSpec(memory_space=pl.ANY)
    S = jax.ShapeDtypeStruct
    return pl.pallas_call(
        functools.partial(enc_fwd_kernel, W=W, FF=FF, seen=seen),
        in_specs=[pl.BlockSpec(memory_space=pltpu.SMEM)] * 2 + [vm] * 3 + [hbm] * 5,
        out_specs=[vm] * 5,
        out_shape=[S((n, 4 * W + FF), BF), S((n, 3 * W), BF), S((n, W), F32), S((n, FF), BF), S((n, wp.shape[1]), F32)],
        scratch_shapes=[pltpu.VMEM(w.shape, BF) for w in (wqkv, wo, w1, w2, wp)] + [pltpu.SemaphoreType.DMA((5,))],
        compiler_params=pltpu.CompilerParams(vmem_limit_bytes=VMEM),
        cost_estimate=pl.CostEstimate(flops=1_700_000_000, bytes_accessed=18_000_000, transcendentals=1_000_000),
        name="encoder_forward",
    )(sec, frames, tokens, vec, b1, wqkv, wo, w1, w2, wp)


def half_of(ref, start, size, s):
    return ref[:, pl.ds(pl.multiple_of(start + s * (size // 2), 128), size // 2)]


def enc_bwd_kernel(sec_ref, frames_ref, dz_ref, tok_ref, vec_ref, qkv_ref, mid_ref, gp_ref, wp_any, w2_any, w1_any, wo_any, wqkv_any,
                   mine_ref, other_ref, tok_mine_ref, tok_other_ref,
                   wp_ref, w2_ref, w1_ref, wo_ref, wqkv_ref, full, tokg, small, sem, *, W, FF, seen):
    pairs = ((wp_any, wp_ref), (w2_any, w2_ref), (w1_any, w1_ref), (wo_any, wo_ref), (wqkv_any, wqkv_ref))
    copies = [pltpu.make_async_copy(a, b, sem.at[i]) for i, (a, b) in enumerate(pairs)]
    for c in copies:
        c.start()
    sec = sec_ref[0]
    valid = frames_ref[sec] // 2 * seen
    vec = vec_ref[...].astype(F32)
    row = lambda i: vec[i:i + 1, :]
    rsum = lambda v: jnp.sum(v, axis=0, keepdims=True)
    n = dz_ref.shape[0]
    small[...] = jnp.zeros_like(small)
    U, B, Q = W, W + FF, 2 * W + FF
    copies[0].wait()
    de = dot(dz_ref[...], wp_ref[...], 1, 1).astype(BF)
    full[:, :W] = de
    def_ = de.astype(F32)
    small[7:8, :W] = rsum(def_)
    copies[1].wait()
    for f in range(0, FF, W):
        duf = gp_ref[:, f:f + W].astype(F32) * dot(de, w2_ref[f:f + W, :], 1, 1)
        full[:, U + f:U + f + W] = duf.astype(BF)
        small[8 + f // W:9 + f // W, :W] = rsum(duf)
    copies[2].wait()
    da2 = dot(full[:, U:U + FF], w1_ref[...], 1, 1)
    xh, r = norm_r(mid_ref[...])
    small[5:6, :W] = rsum(da2 * xh)
    small[6:7, :W] = rsum(da2)
    dg = da2 * row(5)
    dm = def_ + r * (dg - jnp.mean(dg, axis=1, keepdims=True) - xh * jnp.mean(dg * xh, axis=1, keepdims=True))
    small[4:5, :W] = rsum(dm)
    db = dm.astype(BF)
    full[:, B:B + W] = db
    copies[3].wait()
    do = dot(db, wo_ref[...], 1, 1).astype(BF)
    for h in range(W // 128):
        c = h * 128
        q = two_heads((qkv_ref[:, c:c + 128].astype(F32) * (0.125 * LOG2E)).astype(BF))
        k = qkv_ref[:, W + c:W + c + 128]
        v = qkv_ref[:, 2 * W + c:2 * W + c + 128]
        k2 = two_heads(k)
        do2 = two_heads(do[:, c:c + 128])
        p = enc_probs(q, k, valid)
        dp = dot(do2, v, 1, 1)
        ds = (p * (dp - jnp.sum(dp * p, axis=1, keepdims=True))).astype(BF)
        p16 = p.astype(BF)
        full[:, Q + c:Q + c + 128] = ((dot(ds[:n], k2[:n]) + dot(ds[n:], k2[n:])) * 0.125).astype(BF)
        full[:, Q + W + c:Q + W + c + 128] = (dot(ds, q, 0, 0) * LN2).astype(BF)
        full[:, Q + 2 * W + c:Q + 2 * W + c + 128] = dot(p16, do2, 0, 0).astype(BF)
    small[2:3, :W] = rsum(full[:, Q:Q + W].astype(F32))
    small[3:4, :W] = rsum(full[:, Q + 2 * W:Q + 3 * W].astype(F32))
    copies[4].wait()
    da = dot(full[:, Q:Q + 3 * W], wqkv_ref[...], 1, 1)
    xh, r = norm_r(tok_ref[sec].astype(F32))
    small[0:1, :W] = rsum(da * xh)
    small[1:2, :W] = rsum(da)
    dg = da * row(0)
    dx = dm + r * (dg - jnp.mean(dg, axis=1, keepdims=True) - xh * jnp.mean(dg * xh, axis=1, keepdims=True))
    tokg[...] = dx.astype(BF)
    half = W // 2
    for ref, tref, s in ((mine_ref, tok_mine_ref, sec), (other_ref, tok_other_ref, 1 - sec)):
        tref[...] = tokg[:, aligned(s * half, half)]
        at = 0
        for start, size in ((0, half), (U, FF // 2), (B, half), (Q, 3 * half)):
            ref[:n, at:at + size] = full[:, pl.ds(pl.multiple_of(start + s * size, 128), size)]
            at += size
        ref[:n, at:] = dz_ref[...]
        ref[n:, :half] = small[:, aligned(s * half, half)].astype(BF)
        ref[n:, half:] = jnp.zeros((16, ref.shape[1] - half), BF)
        for t in range(FF // 2 // W):
            b = jnp.where(s == 0, small[8 + t:9 + t, :], small[8 + FF // 2 // W + t:9 + FF // 2 // W + t, :])
            ref[n + 8 + t:n + 9 + t, :W] = b.astype(BF)


def enc_bwd_call(sec, frames, seen, dz, tokens, vec, qkv, mid, gp, wp, w2, w1, wo, wqkv):
    n, W = tokens.shape[1], tokens.shape[2]
    FF = w1.shape[1]
    vm, hbm = pl.BlockSpec(memory_space=pltpu.VMEM), pl.BlockSpec(memory_space=pl.ANY)
    S = jax.ShapeDtypeStruct
    width = (5 * W + FF) // 2 + wp.shape[1]
    return pl.pallas_call(
        functools.partial(enc_bwd_kernel, W=W, FF=FF, seen=seen),
        in_specs=[pl.BlockSpec(memory_space=pltpu.SMEM)] * 2 + [vm] * 6 + [hbm] * 5,
        out_specs=[vm] * 4,
        out_shape=[S((n + 16, width), BF), S((n + 16, width), BF), S((n, W // 2), BF), S((n, W // 2), BF)],
        scratch_shapes=[pltpu.VMEM(w.shape, BF) for w in (wp, w2, w1, wo, wqkv)]
        + [pltpu.VMEM((n, 5 * W + FF), BF), pltpu.VMEM((n, W), BF), pltpu.VMEM((16, W), F32), pltpu.SemaphoreType.DMA((5,))],
        compiler_params=pltpu.CompilerParams(vmem_limit_bytes=VMEM),
        cost_estimate=pl.CostEstimate(flops=2_000_000_000, bytes_accessed=18_000_000, transcendentals=1_000_000),
        name="encoder_backward",
    )(sec, frames, dz, tokens, vec, qkv, mid, gp, wp, w2, w1, wo, wqkv)


PIECES = 8


def part_layout(part, W, FF, WD):
    half = W // 2
    if part == 0:
        blocks = [("down", r, c, W) for r in range(0, FF, W) for c in range(0, half, 128)]
    elif part == 1:
        blocks = [("up", 0, c, W) for c in range(0, FF // 2, 128)]
    else:
        blocks = [("qkv", 0, c, W) for c in range(0, 3 * half, 128)] + [("out", 0, c, W) for c in range(0, half, 128)]
    halves = [blocks[:len(blocks) // 2], blocks[len(blocks) // 2:]]
    if part == 2:
        halves[0] = halves[0] + [("proj", 0, c, WD // 2) for c in range(0, W, 128)]
    return halves


def half_rows(part, W, FF, WD):
    rows = [sum(n for _, _, _, n in h) for h in part_layout(part, W, FF, WD)]
    if part == 2:
        rows[1] += 128
    return rows


def dec_share(part, W, FF, WD, WF):
    total = dec_blocks(WD, WF)["all"]
    flats = [sum(half_rows(i, W, FF, WD)) for i in range(3)]
    counts = [((sum(flats) + total) // 3 - f) // (PIECES * 16) * (PIECES * 16) for f in flats[:2]]
    counts.append(total - sum(counts))
    size = (flats[part] + counts[part]) // 2
    rows = half_rows(part, W, FF, WD)
    return (sum(counts[:part]), size - rows[0], size - rows[1])


def part_rows(part, W, FF, WD, WF):
    return sum(half_rows(part, W, FF, WD)) + sum(dec_share(part, W, FF, WD, WF)[1:])


def placed(part, W, FF, WD, WF):
    at = {}
    for h, blocks in enumerate(part_layout(part, W, FF, WD)):
        row = h * part_rows(part, W, FF, WD, WF) // 2
        for name, r, c, n in blocks:
            at[name, r, c] = row
            row += n
    return at


def weight_grad_kernel(idx_ref, acts_any, came_any, mine_any, dcame_any, pack_any, pack_came_any, give0, give1, give2, keep0, keep1, keep2,
                       flat0, flat1, flat2, acts, dy, dzt, small, pack, pack_came, out_sem, in_sem, *, W, FF, WD, WF):
    n = acts_any.shape[0]
    half = W // 2
    lhs = {"qkv": (0, W), "out": (W, W), "up": (2 * W, W), "down": (3 * W, FF), "proj": (3 * W + FF, W)}
    cols = {"down": (0, half), "up": (half, FF // 2), "out": (half + FF // 2, half), "qkv": (2 * half + FF // 2, 3 * half)}
    zc = 5 * half + FF // 2
    copies = []

    def fetch(src, dst):
        copies.append(pltpu.make_async_copy(src, dst, in_sem.at[len(copies)]))
        copies[-1].start()

    both = lambda rows, c, dst: [fetch(src.at[pl.ds(rows.start, rows.stop - rows.start), pl.ds(*c)], dst.at[pl.ds(k * (rows.stop - rows.start), rows.stop - rows.start), pl.ds(*c)])
                                 for k, src in enumerate((mine_any, dcame_any))]
    own = lambda c: [fetch(src.at[:, pl.ds(*c)], acts.at[pl.ds(k * n, n), pl.ds(*c)]) for k, src in enumerate((acts_any, came_any))]
    ready = {}
    for name, d in (("down", (0, half)), ("up", (half, FF // 2)), ("qkv", (half + FF // 2, mine_any.shape[1] - half - FF // 2))):
        both(slice(0, n), d, dy)
        own(lhs[name])
        ready[name] = len(copies)
    for name in ("out", "proj"):
        own(lhs[name])
        ready[name] = len(copies)
    both(slice(n, n + 16), (0, W), small)
    fetch(pack_any, pack)
    fetch(pack_came_any, pack_came)
    waited = 0
    step = 384
    for part, (flat, give, keep) in enumerate(((flat0, give0, keep0), (flat1, give1, keep1), (flat2, give2, keep2))):
        at = placed(part, W, FF, WD, WF)
        for name in (("down",), ("up",), ("qkv", "out", "proj"))[part]:
            while waited < ready[name]:
                copies[waited].wait()
                waited += 1
            a0, an = lhs[name]
            if name == "proj":
                dzt[...] = dy[:, zc:zc + WD].T
                g = dot(dzt[pl.ds(pl.multiple_of(idx_ref[0] * (WD // 2), 16), WD // 2), :], acts[:, a0:a0 + an]).astype(BF)
                for c in range(0, W, 128):
                    flat[at[name, 0, c]:at[name, 0, c] + WD // 2, :] = g[:, c:c + 128]
                continue
            d0, dn = cols[name]
            for r in range(0, an, W):
                lt = acts[:, a0 + r:a0 + r + W].T
                for c in range(0, dn, step):
                    g = dot(lt, dy[:, d0 + c:d0 + c + step]).astype(BF)
                    for b in range(0, step, 128):
                        o = at[name, r, c + b]
                        flat[o:o + W, :] = g[:, b:b + 128]
        if part == 0:
            for c in copies[waited:]:
                c.wait()
            waited = len(copies)
        first, low, high = dec_share(part, W, FF, WD, WF)
        middle = flat.shape[0] // 2
        if part == 2:
            total = small[:16, :].astype(F32) + small[16:, :].astype(F32)
            rows = [total[0:8, c:c + 128] for c in range(0, half, 128)]
            rows += [total[8 + t:9 + t, c:c + 128] for t in range(FF // 2 // W) for c in range(0, W, 128)]
            used = 8 * (half // 128) + FF // 2 // 128
            flat[flat.shape[0] - high - 128:flat.shape[0] - high, :] = jnp.concatenate(rows + [jnp.zeros((128 - used, 128), F32)], axis=0).astype(BF)
        for row, p0, n in ((middle - low, first, low), (flat.shape[0] - high, first + low, high)):
            flat[row:row + n, :] = (pack[p0:p0 + n, :].astype(F32) + pack_came[p0:p0 + n, :].astype(F32)).astype(BF)
        size = flat.shape[0] // PIECES
        me = idx_ref[1 + part]
        for p in range(PIECES // 2):
            src = lambda q: flat.at[pl.ds(pl.multiple_of((q ^ me) * size, 16), size), :]
            to = pl.ds(p * size, size)
            pltpu.make_async_copy(src(p), keep.at[to, :], out_sem.at[part]).start()
            pltpu.make_async_copy(src(p + PIECES // 2), give.at[to, :], out_sem.at[part]).start()
    for part, flat in enumerate((flat0, flat1, flat2)):
        pltpu.make_async_copy(flat, flat, out_sem.at[part]).wait()


def weight_grad_call(idx, acts, came, mine, dcame, pack, pack_came, W, FF, WD, WF):
    n = acts.shape[0]
    rows = [part_rows(i, W, FF, WD, WF) for i in range(3)]
    hbm = pl.BlockSpec(memory_space=pl.ANY)
    return pl.pallas_call(
        functools.partial(weight_grad_kernel, W=W, FF=FF, WD=WD, WF=WF),
        in_specs=[pl.BlockSpec(memory_space=pltpu.SMEM)] + [hbm] * 6,
        out_specs=[hbm] * 6,
        out_shape=[jax.ShapeDtypeStruct((r // 2, 128), BF) for r in rows] * 2,
        scratch_shapes=[pltpu.VMEM((r, 128), BF) for r in rows] + [pltpu.VMEM((2 * n, acts.shape[1]), BF), pltpu.VMEM((2 * n, mine.shape[1]), BF),
                        pltpu.VMEM((WD, 2 * n), BF), pltpu.VMEM((32, W), BF), pltpu.VMEM(pack.shape, BF), pltpu.VMEM(pack.shape, BF),
                        pltpu.SemaphoreType.DMA((3,)), pltpu.SemaphoreType.DMA((24,))],
        compiler_params=pltpu.CompilerParams(vmem_limit_bytes=VMEM),
        cost_estimate=pl.CostEstimate(flops=1_700_000_000, bytes_accessed=20_000_000, transcendentals=0),
        name="encoder_weight_gradients",
    )(idx, acts, came, mine, dcame, pack, pack_came)


def unpack_half(part, h, flat, named, stage, sem, started, sizes):
    W, FF, WD, WF = sizes
    enc = jnp.zeros((8, 128), F32)
    proj = jnp.zeros((8, 128), F32)
    row = 0
    for i, (name, r, c, n) in enumerate(part_layout(part, W, FF, WD)[h]):
        g = flat[row:row + n, :].astype(F32)
        stage[row:row + n, :] = g
        squares = jnp.sum((g * g).reshape(-1, 8, 128), axis=0)
        if name == "proj":
            proj += squares
        else:
            enc += squares
        copy = pltpu.make_async_copy(stage.at[pl.ds(row, n), :], named[name].at[pl.ds(r, n), pl.ds(c, 128)], sem.at[i])
        copy.start()
        started.append(copy)
        row += n
    return enc, proj


def unpack_own_kernel(idx_ref, own0, own1, own2, down, up, qkv, out, proj, sq_ref, flat0, flat1, flat2, stage0, stage1, stage2, fetch_sem, sem, *, sizes):
    unpack_halves(idx_ref, (own0, own1, own2), (down, up, qkv, out, proj), sq_ref, (flat0, flat1, flat2), (stage0, stage1, stage2), fetch_sem, sem, False, sizes)


def unpack_halves(idx_ref, arrays, outs, sq_ref, flats, stages, fetch_sem, sem, other, sizes, between=None):
    named = dict(zip(("down", "up", "qkv", "out", "proj"), outs))
    quarter = PIECES // 2
    for i, (array, flat) in enumerate(zip(arrays, flats)):
        size = flat.shape[0] // quarter
        low = idx_ref[1 + i] & (quarter - 1)
        for p in range(quarter):
            to = flat.at[pl.ds(pl.multiple_of((p ^ low) * size, 16), size), :]
            pltpu.make_async_copy(array.at[pl.ds(p * size, size), :], to, fetch_sem.at[i]).start()
    sq_ref[...] = jnp.zeros_like(sq_ref)
    for part, (flat, stage) in enumerate(zip(flats, stages)):
        pltpu.make_async_copy(flat, flat, fetch_sem.at[part]).wait()
        top = idx_ref[1 + part] // quarter
        if other:
            top = 1 - top
        for h in range(2):
            @pl.when(top == h)
            def _(part=part, h=h, flat=flat, stage=stage):
                started = []
                enc, proj = unpack_half(part, h, flat, named, stage, sem.at[part], started, sizes)
                sq_ref[:8, :] = sq_ref[:8, :] + enc
                sq_ref[8:, :] = sq_ref[8:, :] + proj
    if between is not None:
        between()
    for part, stage in enumerate(stages):
        top = idx_ref[1 + part] // quarter
        if other:
            top = 1 - top
        W, FF, WD, WF = sizes
        for h in range(2):
            @pl.when(top == h)
            def _(part=part, h=h, stage=stage):
                row = 0
                for i, (name, r, c, n) in enumerate(part_layout(part, W, FF, WD)[h]):
                    pltpu.make_async_copy(stage.at[pl.ds(row, n), :], named[name].at[pl.ds(r, n), pl.ds(c, 128)], sem.at[part, i]).wait()
                    row += n


def unpack_scratch(sizes):
    W, FF, WD, WF = sizes
    rows = [part_rows(i, *sizes) // 2 for i in range(3)]
    return ([pltpu.VMEM((r, 128), BF) for r in rows] + [pltpu.VMEM((max(sum(b[3] for b in h) for h in part_layout(i, W, FF, WD)), 128), F32) for i in range(3)]
            + [pltpu.SemaphoreType.DMA((3,)), pltpu.SemaphoreType.DMA((3, 16))])


def big_shapes(sizes):
    W, FF, WD, WF = sizes
    S = lambda *shape: jax.ShapeDtypeStruct(shape, F32)
    half = W // 2
    return [S(FF, half), S(W, FF // 2), S(W, 3 * half), S(W, half), S(WD // 2, W)]


def unpack_own_call(idx, own, *sizes):
    vm, hbm = pl.BlockSpec(memory_space=pltpu.VMEM), pl.BlockSpec(memory_space=pl.ANY)
    return pl.pallas_call(
        functools.partial(unpack_own_kernel, sizes=sizes),
        in_specs=[pl.BlockSpec(memory_space=pltpu.SMEM)] + [hbm] * 3,
        out_specs=[hbm] * 5 + [vm],
        out_shape=big_shapes(sizes) + [jax.ShapeDtypeStruct((16, 128), F32)],
        scratch_shapes=unpack_scratch(sizes),
        compiler_params=pltpu.CompilerParams(vmem_limit_bytes=VMEM),
        cost_estimate=pl.CostEstimate(flops=10_000_000, bytes_accessed=12_000_000, transcendentals=0),
        name="unpack_own_half",
    )(idx, *own)


def unpack_kernel(idx_ref, came0, came1, came2, own0, own1, own2, sq_in, b0, b1, b2, b3, b4, down, up, qkv, out, proj, vec_ref, bias_ref, sq_ref,
                  d0, d1, d2, d3, d4, d5, d6, d7, flat0, flat1, flat2, stage0, stage1, stage2, fetch_sem, sem, rest0, rest1, rest2, pack, rest_sem, *, sizes, slots, patches):
    W, FF, WD, WF = sizes
    quarter = PIECES // 2
    rests, flats = (rest0, rest1, rest2), (flat0, flat1, flat2)
    copies = []
    for i, (own, rest) in enumerate(zip((own0, own1, own2), rests)):
        size = rest.shape[0]
        p = (quarter - 1) ^ (idx_ref[1 + i] & (quarter - 1))
        copies.append(pltpu.make_async_copy(own.at[pl.ds(pl.multiple_of(p * size, 16), size), :], rest, rest_sem.at[i]))
        copies[-1].start()

    def between():
        for c in copies:
            c.wait()
        for part, (rest, flat) in enumerate(zip(rests, flats)):
            first, low, high = dec_share(part, *sizes)
            top = idx_ref[1 + part] // quarter
            for h in range(2):
                @pl.when(top == h)
                def _(part=part, h=h, rest=rest, flat=flat, first=first, low=low, high=high):
                    zero, one = (rest, flat) if h == 0 else (flat, rest)
                    pack[first:first + low, :] = zero[zero.shape[0] - low:, :]
                    pack[first + low:first + low + high, :] = one[one.shape[0] - high:, :]
                    if part == 2:
                        at = one.shape[0] - high - 128
                        enc = jnp.zeros((8, 128), F32)
                        for b in range(W // 2 // 128):
                            g = one[at + 8 * b:at + 8 * b + 8, :].astype(F32)
                            enc += g * g
                            vec_ref[:, b * 128:b * 128 + 128] = g
                        at += 8 * (W // 2 // 128)
                        g = one[at:at + 16, :].astype(F32)[:FF // 2 // 128]
                        bias_ref[...] = g
                        enc += jnp.concatenate([jnp.sum(g * g, axis=0, keepdims=True), jnp.zeros((7, 128), F32)], axis=0)
                        sq_ref[:8, :] = sq_ref[:8, :] + enc
        dec = finish(lambda at, n: pack[at:at + n, :], d0, d1, d2, d3, d4, d5, d6, d7, W=WD, FF=WF, slots=slots, patches=patches)
        sq_ref[8:, :] = sq_ref[8:, :] + dec
        sq_ref[...] = sq_ref[...] + sq_in[...]

    unpack_halves(idx_ref, (came0, came1, came2), (down, up, qkv, out, proj), sq_ref, flats, (stage0, stage1, stage2), fetch_sem, sem, True, sizes, between)


def unpack_call(idx, own, came, big, squares, slots, patches, *sizes):
    W, FF, WD, WF = sizes
    vm, hbm = pl.BlockSpec(memory_space=pltpu.VMEM), pl.BlockSpec(memory_space=pl.ANY)
    S = lambda *shape: jax.ShapeDtypeStruct(shape, F32)
    wh = WD // 2
    dec = [S(3 * wh, WD), S(wh, WD), S(WD, WF // 2), S(wh, WF), S(9, wh), S(8, WF // 2), S(slots, wh), S(patches, wh)]
    return pl.pallas_call(
        functools.partial(unpack_kernel, sizes=sizes, slots=slots, patches=patches),
        in_specs=[pl.BlockSpec(memory_space=pltpu.SMEM)] + [hbm] * 6 + [vm] + [hbm] * 5,
        out_specs=[hbm] * 5 + [vm] * 11,
        out_shape=big_shapes(sizes) + [S(8, W // 2), S(FF // 2 // 128, 128), S(16, 128)] + dec,
        input_output_aliases={8 + i: i for i in range(5)},
        scratch_shapes=unpack_scratch(sizes) + [pltpu.VMEM((part_rows(i, *sizes) // PIECES, 128), BF) for i in range(3)]
        + [pltpu.VMEM((dec_blocks(WD, WF)["all"], 128), BF), pltpu.SemaphoreType.DMA((3,))],
        compiler_params=pltpu.CompilerParams(vmem_limit_bytes=VMEM),
        cost_estimate=pl.CostEstimate(flops=10_000_000, bytes_accessed=15_000_000, transcendentals=0),
        name="unpack_other_half",
    )(idx, *came, *own, squares, *big)


def pair_kernel(sec_ref, dec_mine, dec_came, tok_mine, tok_came, dec_ref, tok_ref):
    sec = sec_ref[0]
    for ref, mine, came in ((dec_ref, dec_mine, dec_came), (tok_ref, tok_mine, tok_came)):
        ref[sec] = mine[...]
        ref[1 - sec] = came[...]


def pair_call(sec, *arrays):
    vm = pl.BlockSpec(memory_space=pltpu.VMEM)
    return pl.pallas_call(
        pair_kernel,
        in_specs=[pl.BlockSpec(memory_space=pltpu.SMEM)] + [vm] * 4,
        out_specs=[vm] * 2,
        out_shape=[jax.ShapeDtypeStruct((2, *arrays[i].shape), BF) for i in (0, 2)],
        compiler_params=pltpu.CompilerParams(vmem_limit_bytes=VMEM),
        cost_estimate=pl.CostEstimate(flops=1000, bytes_accessed=1000, transcendentals=0),
        name="both_clips",
    )(sec, *arrays)


SIDE = 4


def coordinates(index):
    return (index // (SIDE * SIDE), index // SIDE % SIDE, index % SIDE)


def flip(place, axis, kind):
    place = list(place)
    place[axis] = place[axis] ^ 1 if kind == 0 else SIDE - 1 - place[axis]
    return tuple(place)


def swap(value, axes, far):
    pairs = []
    for core in range(2):
        for index in range(SIDE**3):
            place = coordinates(index)
            for axis in axes:
                place = flip(place, axis, core ^ far)
            target = (place[0] * SIDE + place[1]) * SIDE + place[2]
            pairs.append((core * SIDE**3 + index, core * SIDE**3 + target))
    return lax.ppermute(value, ("section", "dp"), pairs)


def add(left, right):
    return (left.astype(jnp.float32) + right.astype(jnp.float32)).astype(jnp.bfloat16)


def piece_numbers(place, core):
    near = [1 * ((p == 1) | (p == 2)) for p in place]
    far = [1 * (p >= 2) for p in place]
    first = [(1 - core) * a + core * b for a, b in zip(near, far)]
    return [first[i] * 4 + first[(i + 1) % 3] * 2 + first[(i + 2) % 3] for i in range(3)]


def halve(v, axis, far):
    half = v.shape[0] // 2
    return add(v[:half], swap(v[half:], (axis,), far))


def sum_over_chips(pairs):
    own, came = [], []
    for i, (give, keep) in enumerate(pairs):
        v = add(keep, swap(give, (i,), 0))
        for step in (1, 2):
            v = halve(v, (i + step) % 3, 0)
        for step in range(3):
            v = add(v, swap(v, ((i + step) % 3,), 1))
        for step in (2, 1):
            v = jnp.concatenate([v, swap(v, ((i + step) % 3,), 0)])
        own.append(v)
        came.append(swap(v, (i,), 0))
    return (own, came)


def from_partner(value):
    return lax.ppermute(value, "section", [(0, 1), (1, 0)])


def shards(
    tokens,
    frames,
    visible,
    out_grad,
    enc_vectors,
    enc_qkv,
    enc_out,
    enc_up,
    enc_up_bias,
    enc_down,
    proj_weight,
    dec_vectors,
    dec_qkv,
    dec_out,
    dec_up,
    dec_up_bias,
    dec_down,
    time_pos,
    space_pos,
):
    enc_width, enc_hidden = enc_up.shape
    dec_width, dec_hidden = dec_up.shape
    slot_count = time_pos.shape[0]
    patch_count = space_pos.shape[0]
    seen_count = visible.shape[1]
    section = lax.axis_index("section").astype(jnp.int32)
    core = section.reshape(1)
    sizes = (enc_width, enc_hidden, dec_width, dec_hidden)
    acts, qkv, mid, slopes, projected = enc_fwd_call(
        core, frames, seen_count, tokens, enc_vectors, enc_up_bias, enc_qkv, enc_out, enc_up, enc_down, proj_weight
    )
    acts_came = from_partner(acts)
    (decoded_mine, decoded_other), grad_projected, (dec_mine, dec_other) = dec_block_call(
        core,
        frames,
        visible,
        projected,
        time_pos,
        space_pos,
        dec_vectors,
        dec_qkv,
        dec_out,
        dec_up,
        dec_up_bias,
        dec_down,
        out_grad,
        TQ=384,
        TA=640,
    )
    dec_came = from_partner(dec_other)
    dy_mine, dy_other, token_mine, token_other = enc_bwd_call(
        core, frames, seen_count, grad_projected, tokens, enc_vectors, qkv, mid, slopes, proj_weight, enc_down, enc_up, enc_out, enc_qkv
    )
    dy_came = from_partner(dy_other)
    places = jnp.stack([section, *piece_numbers(coordinates(lax.axis_index("dp")), section)]).astype(jnp.int32)
    pieces = weight_grad_call(places, acts, acts_came, dy_mine, dy_came, dec_mine, dec_came, *sizes)
    own, came = sum_over_chips(list(zip(pieces[:3], pieces[3:])))
    decoded_came = from_partner(decoded_other)
    token_came = from_partner(token_other)
    decoded, token_grad = pair_call(core, decoded_mine, decoded_came, token_mine, token_came)
    *big, squares = unpack_own_call(places, own, *sizes)
    (
        g_enc_down, g_enc_up, g_enc_qkv, g_enc_out, g_proj, g_vectors, g_enc_bias, squares,
        g_dec_qkv, g_dec_out, g_dec_up, g_dec_down, g_dec_vectors, g_dec_bias, g_time, g_space,
    ) = unpack_call(places, own, came, big, squares, slot_count, patch_count, *sizes)
    enc_squares, dec_squares = squares[:8], squares[8:]
    give = jnp.where(section == 0, dec_squares, enc_squares)
    keep = jnp.where(section == 0, enc_squares, dec_squares)
    norms = jnp.sum(keep + from_partner(give)).reshape(1)
    return (
        decoded.transpose(0, 2, 1),
        token_grad,
        g_vectors,
        g_enc_qkv,
        g_enc_out,
        g_enc_up,
        g_enc_bias.reshape(-1),
        g_enc_down,
        g_proj.T,
        g_dec_vectors,
        g_dec_qkv.T,
        g_dec_out.T,
        g_dec_up,
        g_dec_bias[0],
        g_dec_down.T,
        g_time,
        g_space,
        norms,
    )


from jax.sharding import PartitionSpec as P


def solution(mesh):
    placed = (
        P("dp", None, None),
        P("dp"),
        P("dp", None),
        P("dp", None, None),
        P(),
        P(),
        P(),
        P(),
        P(),
        P(),
        P(),
        P(),
        P(),
        P(),
        P(),
        P(),
        P(),
        P(),
        P(),
    )
    return jax.shard_map(
        shards,
        mesh=mesh,
        in_specs=placed,
        out_specs=(
            P("dp", None, "section"),
            P("dp", None, "section"),
            P(None, "section"),
            P(None, "section"),
            P(None, "section"),
            P(None, "section"),
            P("section"),
            P(None, "section"),
            P(None, "section"),
            P(None, "section"),
            P(None, "section"),
            P(None, "section"),
            P(None, "section"),
            P("section"),
            P(None, "section"),
            P(None, "section"),
            P(None, "section"),
            P("section"),
        ),
        check_vma=False,
    )
```

```python
import functools
import jax, jax.numpy as jnp, numpy as np
from jax import lax
from jax.experimental import pallas as pl
from jax.experimental.pallas import tpu as pltpu

EPS = 1e-6
NEG = -1e9
LOG2E = 1.4426950408889634
LN2 = 0.6931471805599453
F32, BF = jnp.float32, jnp.bfloat16


def dot(a, b, ca=1, cb=0):
    return lax.dot_general(a, b, (((ca,), (cb,)), ((), ())), preferred_element_type=F32)


def tiles_of(total, size):
    return [(s, min(size, total - s)) for s in range(0, total, size)]


def over(total, size, body, carry):
    full = total // size
    if full:
        carry = lax.fori_loop(0, full, lambda i, k: body(pl.ds(pl.multiple_of(i * size, 128), size), size, k), carry)
    if total % size:
        carry = body(pl.ds(full * size, total % size), total % size, carry)
    return carry


def norm_c(x):
    mean = jnp.mean(x, axis=0, keepdims=True)
    c = x - mean
    r = lax.rsqrt(jnp.mean(c * c, axis=0, keepdims=True) + EPS)
    return c * r, r


def gelu_pair(u):
    a = jnp.abs(u)
    t = 1.0 / (1.0 + (0.3275911 * 0.7071067811865476) * a)
    e = jnp.exp2((-0.5 * LOG2E) * (u * u))
    poly = t * (0.5 * 0.254829592 + t * (0.5 * -0.284496736 + t * (0.5 * 1.421413741 + t * (0.5 * -1.453152027 + t * (0.5 * 1.061405429)))))
    tail = poly * e
    phi = jnp.where(u >= 0, 1.0 - tail, tail)
    return u * phi, phi + u * (e * 0.3989422804014327)


def dec_kernel(sec_ref, frames_ref, vis_ref, proj_ref, time_ref, space_ref, vecs_ref, wqkv_ref, wo_ref, w1_ref, bias_ref, w2_ref, dy_any,
               out_refs, dz_ref, pack_refs,
               x_s, a1_s, qkv_s, e_s, l_s, o_s, m_s, a2_s, g_s, gp_s, dy_s, db_s, sel_s, doa_s, do_s, o32_s, dy_ref, vec_ref, b1_ref, dec_s, dy_sem, *, W, L, H, FF, V, slots, patches, TQ, TA):
    dqkv_s, ds_s = g_s, gp_s
    sec = sec_ref[0]
    used = frames_ref[sec] // 2
    valid = used * patches
    dy_copy = pltpu.make_async_copy(dy_any.at[sec], dy_ref, dy_sem)
    dy_copy.start()
    seen_count = V // slots
    vecs = vecs_ref[...].astype(F32)
    vec_ref[...] = jnp.concatenate([vecs, jnp.zeros((16 - vecs.shape[0], W), F32)], axis=0).T
    b1_ref[...] = jnp.broadcast_to(bias_ref[...].reshape(1, FF).astype(F32), (8, FF)).T[:, 0:1]
    col = lambda i: vec_ref[:, i:i + 1]
    HS = 64
    lane = lax.broadcasted_iota(jnp.int32, (1, L), 1)
    vrow = lax.broadcasted_iota(jnp.int32, (V, 1), 0)
    vslot = jnp.zeros((V, 1), jnp.int32)
    for t in range(1, slots):
        vslot += (vrow >= t * seen_count).astype(jnp.int32)
    vrank = vrow - vslot * seen_count
    target = vslot * patches
    for j in range(seen_count):
        target += jnp.where(vrank == j, vis_ref[sec, j], 0)
    onehot = (target == lax.broadcasted_iota(jnp.int32, (V, L), 1)).astype(F32)
    slot = jnp.zeros((1, L), jnp.int32)
    for t in range(1, slots):
        slot += (lane >= t * patches).astype(jnp.int32)
    patch_oh = (lax.broadcasted_iota(jnp.int32, (patches, L), 0) == lane - slot * patches).astype(BF)
    seen = jnp.sum(onehot, axis=0, keepdims=True)
    srow = lax.broadcasted_iota(jnp.int32, (32, L), 0)
    slot_oh = jnp.where(srow < 16, ((srow & 7) == slot).astype(F32), jnp.where(srow == 16, 1.0 - seen, 0.0)).astype(BF)
    sel_s[:V, :] = onehot.astype(BF)
    sel_s[V:V + patches, :] = patch_oh
    sel_s[V + patches:, :] = slot_oh
    ti = lax.broadcasted_iota(jnp.int32, (slots, slots), 0)
    ii = lax.broadcasted_iota(jnp.int32, (slots, slots), 1)
    num = ti * (slots - 1)
    lower = jnp.zeros((slots, slots), jnp.int32)
    for q in range(1, (slots - 1) * (slots - 1) + 1):
        lower += (num >= q * (used - 1)).astype(jnp.int32)
    frac = (num - lower * (used - 1)).astype(F32) / jnp.full((slots, slots), used - 1, jnp.int32).astype(F32)
    upper = jnp.minimum(lower + 1, slots - 1)
    table = (1.0 - frac) * (ii == lower).astype(F32) + frac * (ii == upper).astype(F32)
    exact = lambda a, b, ca, cb: lax.dot_general(a, b, (((ca,), (cb,)), ((), ())), precision=lax.Precision.HIGHEST, preferred_element_type=F32)
    spos = exact(table, time_ref[...].astype(F32), 1, 0)
    shi = spos.astype(BF)
    slo = (spos - shi.astype(F32)).astype(BF)
    proj = proj_ref[...]
    hi = proj.astype(BF)
    lo = (proj - hi.astype(F32)).astype(BF)
    mask = vecs[8:9, :].astype(BF)
    src = jnp.concatenate([hi.astype(F32), space_ref[...].astype(F32), shi.astype(F32), slo.astype(F32), mask.astype(F32), jnp.zeros((15, W), F32)], axis=0).astype(BF)

    def first(c, n, k):
        x = dot(src, sel_s[:, c], 0, 0) + dot(lo, sel_s[:V, c], 0, 0)
        x_s[:, c] = x
        xh, _ = norm_c(x)
        a1 = (xh * col(0) + col(1)).astype(BF)
        a1_s[:, c] = a1
        j = dot(wqkv_ref[...], a1, 0, 0)
        qkv_s[:W, c] = ((j[:W] + col(2)) * (0.125 * LOG2E)).astype(BF)
        qkv_s[W:2 * W, c] = j[W:2 * W].astype(BF)
        qkv_s[2 * W:, c] = (j[2 * W:] + col(3)).astype(BF)
        return k

    over(L, TQ, first, 0)
    arow = lax.broadcasted_iota(jnp.int32, (16, L), 0)
    kbias = jnp.where((arow == 0) & (lane >= valid), NEG, 0.0).astype(BF)
    one0 = (arow == 0).astype(BF)
    one01 = (arow < 2).astype(BF)

    def fwd_head(h, carry):
        hs = pl.ds(pl.multiple_of(h * HS, HS), HS)
        ks = pl.ds(pl.multiple_of(W + h * HS, HS), HS)
        vs = pl.ds(pl.multiple_of(2 * W + h * HS, HS), HS)
        kr = jnp.concatenate([qkv_s[ks, :], kbias], axis=0).T
        vc = jnp.concatenate([qkv_s[vs, :], one0], axis=0)

        def tile(c, n, exact):
            qc = jnp.concatenate([qkv_s[hs, c], one0[:, :n]], axis=0)
            st = dot(kr, qc)
            if exact:
                st = st - jnp.max(st, axis=0, keepdims=True)
            e = jnp.exp2(st).astype(BF)
            e_s[h, :, c] = e
            oa = dot(vc, e)
            rl = 1.0 / oa[HS:HS + 1]
            l_s[h, :, c] = jnp.broadcast_to(rl, (8, n))
            o = oa[:HS] * rl
            o32_s[hs, c] = o
            o_s[hs, c] = o.astype(BF)

        square = lambda v: jnp.max(jnp.sum(v * v, axis=0))
        bound = square(qkv_s[hs, :].astype(F32)) * square(qkv_s[ks, :].astype(F32))

        @pl.when(bound <= 60.0 * 60.0)
        def _():
            over(L, TA, lambda c, n, k: (tile(c, n, False), k)[1], 0)

        @pl.when(jnp.logical_not(bound <= 60.0 * 60.0))
        def _():
            over(L, TA, lambda c, n, k: (tile(c, n, True), k)[1], 0)

        return carry

    lax.fori_loop(0, H, fwd_head, 0)

    def middle(c, n, sums):
        sum_b1, sum_dy, sum_g2, sum_s2, sum_db = sums
        live = (lax.broadcasted_iota(jnp.int32, (1, n), 1) + c.start < valid).astype(F32)
        mid = x_s[:, c] + (dot(wo_ref[...], o_s[:, c], 0, 0) + col(4))
        xh, r = norm_c(mid)
        a2 = (xh * col(5) + col(6)).astype(BF)
        a2_s[:, c] = a2
        u = dot(w1_ref[...], a2, 0, 0) + b1_ref[...]
        g, gp = gelu_pair(u)
        g = g.astype(BF)
        g_s[:, c] = g
        y = mid + (dot(w2_ref[...], g, 0, 0) + col(7))
        dec_s[:, c] = (y * live).astype(BF)
        dyf = dy_ref[c, :].astype(F32).T * live
        dy = dyf.astype(BF)
        dy_s[:, c] = dy
        duf = gp * dot(w2_ref[...], dy)
        du = duf.astype(BF)
        gp_s[:, c] = du
        da2 = dot(w1_ref[...], du)
        dg = da2 * col(5)
        dm = dyf + r * (dg - jnp.mean(dg, axis=0, keepdims=True) - xh * jnp.mean(dg * xh, axis=0, keepdims=True))
        db = dm.astype(BF)
        db_s[:, c] = db
        do_s[:, c] = dot(wo_ref[...], db).astype(BF)
        m_s[:, c] = dm
        rs = lambda v: jnp.sum(v, axis=1, keepdims=True)
        return (sum_b1 + rs(duf), sum_dy + rs(dyf), sum_g2 + rs(da2 * xh), sum_s2 + rs(da2), sum_db + rs(dm))

    dy_copy.wait()
    zero = jnp.zeros((W, 1), F32)
    sum_b1, sum_dy, sum_g2, sum_s2, sum_db = over(L, TQ, middle, (jnp.zeros((FF, 1), F32), zero, zero, zero, zero))
    blocks = dec_blocks(W, FF)
    for who, s in enumerate((sec, 1 - sec)):
        rows = lambda size, at=0: pl.ds(pl.multiple_of(s * (size // 2) + at, 16), W // 2)
        out_refs[who][...] = dec_s[rows(W), :]
        pack = pack_refs[who]
        for b in range(FF // W):
            put(pack, blocks["down"] + b * 3 * (W // 2), dot(dy_s[rows(W), :], g_s[b * W:b * W + W, :], 1, 1))
        for b in range(FF // 2 // W):
            put(pack, blocks["up"] + b * 3 * W, dot(a2_s[...], gp_s[pl.ds(pl.multiple_of(s * (FF // 2) + b * W, 16), W), :], 1, 1))
        put(pack, blocks["out"], dot(db_s[rows(W), :], o_s[...], 1, 1))

    def bwd_head(h, carry):
        hs = pl.ds(pl.multiple_of(h * HS, HS), HS)
        ks = pl.ds(pl.multiple_of(W + h * HS, HS), HS)
        vs = pl.ds(pl.multiple_of(2 * W + h * HS, HS), HS)
        vr = jnp.concatenate([qkv_s[vs, :], one01], axis=0).T
        kc = qkv_s[ks, :]
        dob = (do_s[hs, :].astype(F32) * l_s[h, 0:1, :]).astype(BF)
        dl = -jnp.sum(dob.astype(F32) * o32_s[hs, :], axis=0, keepdims=True)
        dlh = dl.astype(BF).astype(F32)
        doa_s[:HS, :] = dob
        doa_s[HS:, :] = jnp.where(arow == 0, dlh, jnp.where(arow == 1, dl - dlh, 0.0)).astype(BF)
        def tile(c, n, k):
            dp = dot(vr, doa_s[:, c])
            ds = (e_s[h, :, c].astype(F32) * dp).astype(BF)
            ds_s[:L, c] = ds
            dqkv_s[hs, c] = (dot(kc, ds) * 0.125).astype(BF)
            return k

        over(L, TA, tile, 0)
        dor = doa_s[:HS, :].T
        qr = qkv_s[hs, :].T

        def tile2(c, n, k):
            dqkv_s[vs, c] = dot(e_s[h, c, :], dor).T.astype(BF)
            dqkv_s[ks, c] = (dot(ds_s[c, :], qr) * LN2).T.astype(BF)
            return k

        return over(L, TA, tile2, carry)

    lax.fori_loop(0, H, bwd_head, 0)
    def last(c, n, sums):
        sum_g1, sum_s1, sum_q, sum_v, gsel = sums
        rs = lambda v: jnp.sum(v, axis=1, keepdims=True)
        da = dot(wqkv_ref[...], dqkv_s[:3 * W, c])
        xh, r = norm_c(x_s[:, c])
        dg = da * col(0)
        dx = m_s[:, c] + r * (dg - jnp.mean(dg, axis=0, keepdims=True) - xh * jnp.mean(dg * xh, axis=0, keepdims=True))
        return (sum_g1 + rs(da * xh), sum_s1 + rs(da), sum_q + rs(dqkv_s[:W, c].astype(F32)), sum_v + rs(dqkv_s[2 * W:3 * W, c].astype(F32)),
                gsel + dot(dx.astype(BF), sel_s[:, c], 1, 1))

    sum_g1, sum_s1, sum_q, sum_v, gsel = over(L, TQ, last, (zero, zero, zero, zero, jnp.zeros((W, sel_s.shape[0]), F32)))
    dz_ref[...] = gsel[:, :V].T.astype(BF)
    small = o32_s
    small[:, :8] = jnp.concatenate([sum_g1, sum_s1, sum_q, sum_v, sum_db, sum_g2, sum_s2, sum_dy], axis=1)
    small[:, 8:16] = gsel[:, V + patches + 16:V + patches + 24]
    small[:, 16:24] = exact(gsel[:, V + patches:V + patches + slots], table, 1, 0)
    small[:, 24:24 + patches] = gsel[:, V:V + patches]
    small[:, 24 + patches:256] = jnp.zeros((W, 256 - 24 - patches), F32)
    for who, s in enumerate((sec, 1 - sec)):
        pack = pack_refs[who]
        put(pack, blocks["qkv"], dot(dqkv_s[pl.ds(pl.multiple_of(s * (3 * W // 2), 16), 3 * W // 2), :], a1_s[...], 1, 1))
        half = small[pl.ds(pl.multiple_of(s * (W // 2), 8), W // 2), :256].T[:32 + patches]
        put(pack, blocks["small"], jnp.concatenate([half, jnp.zeros((32 + patches, 256 - W // 2), F32)], axis=1))
        b1_ref[...] = sum_b1
        put(pack, blocks["bias"], jnp.broadcast_to(b1_ref[pl.ds(pl.multiple_of(s * (FF // 2), 8), FF // 2), :], (FF // 2, 128)).T[:16])
        pack[blocks["end"]:, :] = jnp.zeros((pack.shape[0] - blocks["end"], 128), BF)


def put(pack, at, value):
    n = value.shape[0]
    for b in range(value.shape[1] // 128):
        pack[at + b * n:at + b * n + n, :] = value[:, b * 128:b * 128 + 128].astype(BF)


def dec_blocks(W, FF):
    at, rows = 0, {}
    for name, count in (("qkv", 3 * (3 * W // 2)), ("out", 3 * (W // 2)), ("up", 3 * (FF // 2)), ("down", 3 * (FF // 2)), ("small", 2 * 176), ("bias", 16 * (FF // 2 // 128))):
        rows[name] = at
        at += count
    rows["end"] = at
    unit = 3 * 8 * 16
    rows["all"] = -(-at // unit) * unit
    return rows


def finish(read, qkv_ref, out_ref, up_ref, down_ref, vec_ref, bias_ref, time_ref, space_ref, *, W, FF, slots, patches):
    blocks = dec_blocks(W, FF)
    total = jnp.zeros((8, 128), F32)
    fold = lambda v: jnp.sum((v * v).reshape(-1, 8, 128), axis=0)
    for name, ref, n, parts in (("qkv", qkv_ref, 3 * W // 2, 1), ("out", out_ref, W // 2, 1), ("up", up_ref, W, FF // 2 // W), ("down", down_ref, W // 2, FF // W)):
        for b in range(3 * parts):
            g = read(blocks[name] + b * n, n).astype(F32)
            ref[:, b * 128:b * 128 + 128] = g
            total += fold(g)
    low = read(blocks["small"], 176).astype(F32)
    high = read(blocks["small"] + 176, 176).astype(F32)
    total += fold(low) + fold(high)
    for ref, at, n in ((vec_ref, 0, 9), (time_ref, 16, slots), (space_ref, 16 + slots, patches)):
        ref[:, :128] = low[at:at + n]
        ref[:, 128:] = high[at:at + n, :W // 2 - 128]
    for b in range(FF // 2 // 128):
        g = read(blocks["bias"] + 16 * b, 16).astype(F32)
        bias_ref[:, b * 128:b * 128 + 128] = g[:8]
        total += 0.0625 * fold(g)
    return total


def dec_block_call(sec, frames, visible, proj, time_pos, space, vecs, wqkv, wo, w1, bias, w2, dy, TQ, TA):
    W, L, FF = wqkv.shape[0], dy.shape[1], w1.shape[1]
    H = W // 64
    patches, slots = space.shape[0], time_pos.shape[0]
    V = proj.shape[0]
    sm, vm = pl.BlockSpec(memory_space=pltpu.SMEM), pl.BlockSpec(memory_space=pltpu.VMEM)
    S = jax.ShapeDtypeStruct
    return pl.pallas_call(
        functools.partial(dec_kernel, W=W, L=L, H=H, FF=FF, V=V, slots=slots, patches=patches, TQ=TQ, TA=TA),
        in_specs=[sm, sm, sm] + [vm] * 9 + [pl.BlockSpec(memory_space=pl.ANY)],
        out_specs=[[vm] * 2, vm, [vm] * 2],
        out_shape=[[S((W // 2, L), BF)] * 2, S((V, W), BF), [S((dec_blocks(W, FF)["all"], 128), BF)] * 2],
        scratch_shapes=[
            pltpu.VMEM((W, L), F32),
            pltpu.VMEM((W, L), BF),
            pltpu.VMEM((3 * W, L), BF),
            pltpu.VMEM((H, L, L), BF),
            pltpu.VMEM((H, 8, L), F32),
            pltpu.VMEM((W, L), BF),
            pltpu.VMEM((W, L), F32),
            pltpu.VMEM((W, L), BF),
            pltpu.VMEM((FF, L), BF),
            pltpu.VMEM((FF, L), BF),
            pltpu.VMEM((W, L), BF),
            pltpu.VMEM((W, L), BF),
            pltpu.VMEM((V + patches + 32, L), BF),
            pltpu.VMEM((80, L), BF),
            pltpu.VMEM((W, L), BF),
            pltpu.VMEM((W, L), F32),
            pltpu.VMEM((L, W), BF),
            pltpu.VMEM((W, 16), F32),
            pltpu.VMEM((FF, 1), F32),
            pltpu.VMEM((W, L), BF),
            pltpu.SemaphoreType.DMA,
        ],
        compiler_params=pltpu.CompilerParams(vmem_limit_bytes=63 * 1024 * 1024),
        cost_estimate=pl.CostEstimate(flops=28_000_000_000, bytes_accessed=12_000_000, transcendentals=10_000_000),
        name="decoder",
    )(sec, frames, visible, proj, time_pos, space, vecs, wqkv, wo, w1, bias, w2, dy)


VMEM = 63 * 1024 * 1024


def aligned(start, size):
    return pl.ds(pl.multiple_of(start, size), size)


def norm_r(x):
    mean = jnp.mean(x, axis=1, keepdims=True)
    c = x - mean
    r = lax.rsqrt(jnp.mean(c * c, axis=1, keepdims=True) + EPS)
    return c * r, r


def enc_probs(qm, k, valid):
    s = dot(qm, k, 1, 1)
    live = lax.broadcasted_iota(jnp.int32, s.shape, 1) < valid
    s = jnp.where(live, s, NEG)
    e = jnp.exp2(s - jnp.max(s, axis=1, keepdims=True))
    return e / jnp.sum(e, axis=1, keepdims=True)


def two_heads(v):
    low = lax.broadcasted_iota(jnp.int32, v.shape, 1) < 64
    zero = jnp.zeros_like(v)
    return jnp.concatenate([jnp.where(low, v, zero), jnp.where(low, zero, v)], axis=0)


def enc_fwd_kernel(sec_ref, frames_ref, tok_ref, vec_ref, b1_ref, wqkv_any, wo_any, w1_any, w2_any, wp_any,
                   acts_ref, qkv_ref, mid_ref, gp_ref, proj_ref,
                   wqkv_ref, wo_ref, w1_ref, w2_ref, wp_ref, sem, *, W, FF, seen):
    pairs = ((wqkv_any, wqkv_ref), (wo_any, wo_ref), (w1_any, w1_ref), (w2_any, w2_ref), (wp_any, wp_ref))
    copies = [pltpu.make_async_copy(a, b, sem.at[i]) for i, (a, b) in enumerate(pairs)]
    for c in copies[:2]:
        c.start()

    def arrived(i):
        copies[i].wait()
        if i + 2 < len(copies):
            copies[i + 2].start()

    sec = sec_ref[0]
    valid = frames_ref[sec] // 2 * seen
    vec = vec_ref[...].astype(F32)
    row = lambda i: vec[i:i + 1, :]
    x = tok_ref[sec].astype(F32)
    n = x.shape[0]
    xh, _ = norm_r(x)
    a1 = (xh * row(0) + row(1)).astype(BF)
    acts_ref[:, :W] = a1
    arrived(0)
    j = dot(a1, wqkv_ref[...])
    qkv_ref[:, :W] = (j[:, :W] + row(2)).astype(BF)
    qkv_ref[:, W:2 * W] = j[:, W:2 * W].astype(BF)
    qkv_ref[:, 2 * W:] = (j[:, 2 * W:] + row(3)).astype(BF)
    for h in range(W // 128):
        s = slice(h * 128, h * 128 + 128)
        q = (qkv_ref[:, s].astype(F32) * (0.125 * LOG2E)).astype(BF)
        p = enc_probs(two_heads(q), qkv_ref[:, W + h * 128:W + h * 128 + 128], valid).astype(BF)
        v = two_heads(qkv_ref[:, 2 * W + h * 128:2 * W + h * 128 + 128])
        acts_ref[:, W + h * 128:W + h * 128 + 128] = (dot(p[:n], v[:n]) + dot(p[n:], v[n:])).astype(BF)
    arrived(1)
    mid = x + (dot(acts_ref[:, W:2 * W], wo_ref[...]) + row(4))
    mid_ref[...] = mid
    xh, _ = norm_r(mid)
    a2 = (xh * row(5) + row(6)).astype(BF)
    acts_ref[:, 2 * W:3 * W] = a2
    arrived(2)
    for f in range(0, FF, W):
        g, gp = gelu_pair(dot(a2, w1_ref[:, f:f + W]) + b1_ref[f:f + W].astype(F32).reshape(1, W))
        acts_ref[:, 3 * W + f:3 * W + f + W] = g.astype(BF)
        gp_ref[:, f:f + W] = gp.astype(BF)
    arrived(3)
    y = mid + (dot(acts_ref[:, 3 * W:3 * W + FF], w2_ref[...]) + row(7))
    enc = y.astype(BF)
    acts_ref[:, 3 * W + FF:] = enc
    arrived(4)
    proj_ref[...] = dot(enc, wp_ref[...])


def enc_fwd_call(sec, frames, seen, tokens, vec, b1, wqkv, wo, w1, w2, wp):
    n, W = tokens.shape[1], tokens.shape[2]
    FF = w1.shape[1]
    vm, hbm = pl.BlockSpec(memory_space=pltpu.VMEM), pl.BlockSpec(memory_space=pl.ANY)
    S = jax.ShapeDtypeStruct
    return pl.pallas_call(
        functools.partial(enc_fwd_kernel, W=W, FF=FF, seen=seen),
        in_specs=[pl.BlockSpec(memory_space=pltpu.SMEM)] * 2 + [vm] * 3 + [hbm] * 5,
        out_specs=[vm] * 5,
        out_shape=[S((n, 4 * W + FF), BF), S((n, 3 * W), BF), S((n, W), F32), S((n, FF), BF), S((n, wp.shape[1]), F32)],
        scratch_shapes=[pltpu.VMEM(w.shape, BF) for w in (wqkv, wo, w1, w2, wp)] + [pltpu.SemaphoreType.DMA((5,))],
        compiler_params=pltpu.CompilerParams(vmem_limit_bytes=VMEM),
        cost_estimate=pl.CostEstimate(flops=1_700_000_000, bytes_accessed=18_000_000, transcendentals=1_000_000),
        name="encoder_forward",
    )(sec, frames, tokens, vec, b1, wqkv, wo, w1, w2, wp)


def half_of(ref, start, size, s):
    return ref[:, pl.ds(pl.multiple_of(start + s * (size // 2), 128), size // 2)]


def enc_bwd_kernel(sec_ref, frames_ref, dz_ref, tok_ref, vec_ref, qkv_ref, mid_ref, gp_ref, wp_any, w2_any, w1_any, wo_any, wqkv_any,
                   mine_ref, other_ref, tok_mine_ref, tok_other_ref,
                   wp_ref, w2_ref, w1_ref, wo_ref, wqkv_ref, full, tokg, small, sem, *, W, FF, seen):
    pairs = ((wp_any, wp_ref), (w2_any, w2_ref), (w1_any, w1_ref), (wo_any, wo_ref), (wqkv_any, wqkv_ref))
    copies = [pltpu.make_async_copy(a, b, sem.at[i]) for i, (a, b) in enumerate(pairs)]
    for c in copies:
        c.start()
    sec = sec_ref[0]
    valid = frames_ref[sec] // 2 * seen
    vec = vec_ref[...].astype(F32)
    row = lambda i: vec[i:i + 1, :]
    rsum = lambda v: jnp.sum(v, axis=0, keepdims=True)
    n = dz_ref.shape[0]
    small[...] = jnp.zeros_like(small)
    U, B, Q = W, W + FF, 2 * W + FF
    copies[0].wait()
    de = dot(dz_ref[...], wp_ref[...], 1, 1).astype(BF)
    full[:, :W] = de
    def_ = de.astype(F32)
    small[7:8, :W] = rsum(def_)
    copies[1].wait()
    for f in range(0, FF, W):
        duf = gp_ref[:, f:f + W].astype(F32) * dot(de, w2_ref[f:f + W, :], 1, 1)
        full[:, U + f:U + f + W] = duf.astype(BF)
        small[8 + f // W:9 + f // W, :W] = rsum(duf)
    copies[2].wait()
    da2 = dot(full[:, U:U + FF], w1_ref[...], 1, 1)
    xh, r = norm_r(mid_ref[...])
    small[5:6, :W] = rsum(da2 * xh)
    small[6:7, :W] = rsum(da2)
    dg = da2 * row(5)
    dm = def_ + r * (dg - jnp.mean(dg, axis=1, keepdims=True) - xh * jnp.mean(dg * xh, axis=1, keepdims=True))
    small[4:5, :W] = rsum(dm)
    db = dm.astype(BF)
    full[:, B:B + W] = db
    copies[3].wait()
    do = dot(db, wo_ref[...], 1, 1).astype(BF)
    for h in range(W // 128):
        c = h * 128
        q = two_heads((qkv_ref[:, c:c + 128].astype(F32) * (0.125 * LOG2E)).astype(BF))
        k = qkv_ref[:, W + c:W + c + 128]
        v = qkv_ref[:, 2 * W + c:2 * W + c + 128]
        k2 = two_heads(k)
        do2 = two_heads(do[:, c:c + 128])
        p = enc_probs(q, k, valid)
        dp = dot(do2, v, 1, 1)
        ds = (p * (dp - jnp.sum(dp * p, axis=1, keepdims=True))).astype(BF)
        p16 = p.astype(BF)
        full[:, Q + c:Q + c + 128] = ((dot(ds[:n], k2[:n]) + dot(ds[n:], k2[n:])) * 0.125).astype(BF)
        full[:, Q + W + c:Q + W + c + 128] = (dot(ds, q, 0, 0) * LN2).astype(BF)
        full[:, Q + 2 * W + c:Q + 2 * W + c + 128] = dot(p16, do2, 0, 0).astype(BF)
    small[2:3, :W] = rsum(full[:, Q:Q + W].astype(F32))
    small[3:4, :W] = rsum(full[:, Q + 2 * W:Q + 3 * W].astype(F32))
    copies[4].wait()
    da = dot(full[:, Q:Q + 3 * W], wqkv_ref[...], 1, 1)
    xh, r = norm_r(tok_ref[sec].astype(F32))
    small[0:1, :W] = rsum(da * xh)
    small[1:2, :W] = rsum(da)
    dg = da * row(0)
    dx = dm + r * (dg - jnp.mean(dg, axis=1, keepdims=True) - xh * jnp.mean(dg * xh, axis=1, keepdims=True))
    tokg[...] = dx.astype(BF)
    half = W // 2
    for ref, tref, s in ((mine_ref, tok_mine_ref, sec), (other_ref, tok_other_ref, 1 - sec)):
        tref[...] = tokg[:, aligned(s * half, half)]
        at = 0
        for start, size in ((0, half), (U, FF // 2), (B, half), (Q, 3 * half)):
            ref[:n, at:at + size] = full[:, pl.ds(pl.multiple_of(start + s * size, 128), size)]
            at += size
        ref[:n, at:] = dz_ref[...]
        ref[n:, :half] = small[:, aligned(s * half, half)].astype(BF)
        ref[n:, half:] = jnp.zeros((16, ref.shape[1] - half), BF)
        for t in range(FF // 2 // W):
            b = jnp.where(s == 0, small[8 + t:9 + t, :], small[8 + FF // 2 // W + t:9 + FF // 2 // W + t, :])
            ref[n + 8 + t:n + 9 + t, :W] = b.astype(BF)


def enc_bwd_call(sec, frames, seen, dz, tokens, vec, qkv, mid, gp, wp, w2, w1, wo, wqkv):
    n, W = tokens.shape[1], tokens.shape[2]
    FF = w1.shape[1]
    vm, hbm = pl.BlockSpec(memory_space=pltpu.VMEM), pl.BlockSpec(memory_space=pl.ANY)
    S = jax.ShapeDtypeStruct
    width = (5 * W + FF) // 2 + wp.shape[1]
    return pl.pallas_call(
        functools.partial(enc_bwd_kernel, W=W, FF=FF, seen=seen),
        in_specs=[pl.BlockSpec(memory_space=pltpu.SMEM)] * 2 + [vm] * 6 + [hbm] * 5,
        out_specs=[vm] * 4,
        out_shape=[S((n + 16, width), BF), S((n + 16, width), BF), S((n, W // 2), BF), S((n, W // 2), BF)],
        scratch_shapes=[pltpu.VMEM(w.shape, BF) for w in (wp, w2, w1, wo, wqkv)]
        + [pltpu.VMEM((n, 5 * W + FF), BF), pltpu.VMEM((n, W), BF), pltpu.VMEM((16, W), F32), pltpu.SemaphoreType.DMA((5,))],
        compiler_params=pltpu.CompilerParams(vmem_limit_bytes=VMEM),
        cost_estimate=pl.CostEstimate(flops=2_000_000_000, bytes_accessed=18_000_000, transcendentals=1_000_000),
        name="encoder_backward",
    )(sec, frames, dz, tokens, vec, qkv, mid, gp, wp, w2, w1, wo, wqkv)


PIECES = 8


def part_layout(part, W, FF, WD):
    half = W // 2
    if part == 0:
        blocks = [("down", r, c, W) for r in range(0, FF, W) for c in range(0, half, 128)]
    elif part == 1:
        blocks = [("up", 0, c, W) for c in range(0, FF // 2, 128)]
    else:
        blocks = [("qkv", 0, c, W) for c in range(0, 3 * half, 128)] + [("out", 0, c, W) for c in range(0, half, 128)]
    halves = [blocks[:len(blocks) // 2], blocks[len(blocks) // 2:]]
    if part == 2:
        halves[0] = halves[0] + [("proj", 0, c, WD // 2) for c in range(0, W, 128)]
    return halves


def half_rows(part, W, FF, WD):
    rows = [sum(n for _, _, _, n in h) for h in part_layout(part, W, FF, WD)]
    if part == 2:
        rows[1] += 128
    return rows


def dec_share(part, W, FF, WD, WF):
    total = dec_blocks(WD, WF)["all"]
    flats = [sum(half_rows(i, W, FF, WD)) for i in range(3)]
    counts = [((sum(flats) + total) // 3 - f) // (PIECES * 16) * (PIECES * 16) for f in flats[:2]]
    counts.append(total - sum(counts))
    size = (flats[part] + counts[part]) // 2
    rows = half_rows(part, W, FF, WD)
    return (sum(counts[:part]), size - rows[0], size - rows[1])


def part_rows(part, W, FF, WD, WF):
    return sum(half_rows(part, W, FF, WD)) + sum(dec_share(part, W, FF, WD, WF)[1:])


def placed(part, W, FF, WD, WF):
    at = {}
    for h, blocks in enumerate(part_layout(part, W, FF, WD)):
        row = h * part_rows(part, W, FF, WD, WF) // 2
        for name, r, c, n in blocks:
            at[name, r, c] = row
            row += n
    return at


def weight_grad_kernel(idx_ref, acts_any, came_any, mine_any, dcame_any, pack_any, pack_came_any, give0, give1, give2, keep0, keep1, keep2,
                       flat0, flat1, flat2, acts, dy, dzt, small, pack, pack_came, out_sem, in_sem, *, W, FF, WD, WF):
    n = acts_any.shape[0]
    half = W // 2
    lhs = {"qkv": (0, W), "out": (W, W), "up": (2 * W, W), "down": (3 * W, FF), "proj": (3 * W + FF, W)}
    cols = {"down": (0, half), "up": (half, FF // 2), "out": (half + FF // 2, half), "qkv": (2 * half + FF // 2, 3 * half)}
    zc = 5 * half + FF // 2
    copies = []

    def fetch(src, dst):
        copies.append(pltpu.make_async_copy(src, dst, in_sem.at[len(copies)]))
        copies[-1].start()

    both = lambda rows, c, dst: [fetch(src.at[pl.ds(rows.start, rows.stop - rows.start), pl.ds(*c)], dst.at[pl.ds(k * (rows.stop - rows.start), rows.stop - rows.start), pl.ds(*c)])
                                 for k, src in enumerate((mine_any, dcame_any))]
    own = lambda c: [fetch(src.at[:, pl.ds(*c)], acts.at[pl.ds(k * n, n), pl.ds(*c)]) for k, src in enumerate((acts_any, came_any))]
    ready = {}
    for name, d in (("down", (0, half)), ("up", (half, FF // 2)), ("qkv", (half + FF // 2, mine_any.shape[1] - half - FF // 2))):
        both(slice(0, n), d, dy)
        own(lhs[name])
        ready[name] = len(copies)
    for name in ("out", "proj"):
        own(lhs[name])
        ready[name] = len(copies)
    both(slice(n, n + 16), (0, W), small)
    fetch(pack_any, pack)
    fetch(pack_came_any, pack_came)
    waited = 0
    step = 384
    for part, (flat, give, keep) in enumerate(((flat0, give0, keep0), (flat1, give1, keep1), (flat2, give2, keep2))):
        at = placed(part, W, FF, WD, WF)
        for name in (("down",), ("up",), ("qkv", "out", "proj"))[part]:
            while waited < ready[name]:
                copies[waited].wait()
                waited += 1
            a0, an = lhs[name]
            if name == "proj":
                dzt[...] = dy[:, zc:zc + WD].T
                g = dot(dzt[pl.ds(pl.multiple_of(idx_ref[0] * (WD // 2), 16), WD // 2), :], acts[:, a0:a0 + an]).astype(BF)
                for c in range(0, W, 128):
                    flat[at[name, 0, c]:at[name, 0, c] + WD // 2, :] = g[:, c:c + 128]
                continue
            d0, dn = cols[name]
            for r in range(0, an, W):
                lt = acts[:, a0 + r:a0 + r + W].T
                for c in range(0, dn, step):
                    g = dot(lt, dy[:, d0 + c:d0 + c + step]).astype(BF)
                    for b in range(0, step, 128):
                        o = at[name, r, c + b]
                        flat[o:o + W, :] = g[:, b:b + 128]
        if part == 0:
            for c in copies[waited:]:
                c.wait()
            waited = len(copies)
        first, low, high = dec_share(part, W, FF, WD, WF)
        middle = flat.shape[0] // 2
        if part == 2:
            total = small[:16, :].astype(F32) + small[16:, :].astype(F32)
            rows = [total[0:8, c:c + 128] for c in range(0, half, 128)]
            rows += [total[8 + t:9 + t, c:c + 128] for t in range(FF // 2 // W) for c in range(0, W, 128)]
            used = 8 * (half // 128) + FF // 2 // 128
            flat[flat.shape[0] - high - 128:flat.shape[0] - high, :] = jnp.concatenate(rows + [jnp.zeros((128 - used, 128), F32)], axis=0).astype(BF)
        for row, p0, n in ((middle - low, first, low), (flat.shape[0] - high, first + low, high)):
            flat[row:row + n, :] = (pack[p0:p0 + n, :].astype(F32) + pack_came[p0:p0 + n, :].astype(F32)).astype(BF)
        size = flat.shape[0] // PIECES
        me = idx_ref[1 + part]
        for p in range(PIECES // 2):
            src = lambda q: flat.at[pl.ds(pl.multiple_of((q ^ me) * size, 16), size), :]
            to = pl.ds(p * size, size)
            pltpu.make_async_copy(src(p), keep.at[to, :], out_sem.at[part]).start()
            pltpu.make_async_copy(src(p + PIECES // 2), give.at[to, :], out_sem.at[part]).start()
    for part, flat in enumerate((flat0, flat1, flat2)):
        pltpu.make_async_copy(flat, flat, out_sem.at[part]).wait()


def weight_grad_call(idx, acts, came, mine, dcame, pack, pack_came, W, FF, WD, WF):
    n = acts.shape[0]
    rows = [part_rows(i, W, FF, WD, WF) for i in range(3)]
    hbm = pl.BlockSpec(memory_space=pl.ANY)
    return pl.pallas_call(
        functools.partial(weight_grad_kernel, W=W, FF=FF, WD=WD, WF=WF),
        in_specs=[pl.BlockSpec(memory_space=pltpu.SMEM)] + [hbm] * 6,
        out_specs=[hbm] * 6,
        out_shape=[jax.ShapeDtypeStruct((r // 2, 128), BF) for r in rows] * 2,
        scratch_shapes=[pltpu.VMEM((r, 128), BF) for r in rows] + [pltpu.VMEM((2 * n, acts.shape[1]), BF), pltpu.VMEM((2 * n, mine.shape[1]), BF),
                        pltpu.VMEM((WD, 2 * n), BF), pltpu.VMEM((32, W), BF), pltpu.VMEM(pack.shape, BF), pltpu.VMEM(pack.shape, BF),
                        pltpu.SemaphoreType.DMA((3,)), pltpu.SemaphoreType.DMA((24,))],
        compiler_params=pltpu.CompilerParams(vmem_limit_bytes=VMEM),
        cost_estimate=pl.CostEstimate(flops=1_700_000_000, bytes_accessed=20_000_000, transcendentals=0),
        name="encoder_weight_gradients",
    )(idx, acts, came, mine, dcame, pack, pack_came)


def unpack_half(part, h, flat, named, stage, sem, started, sizes):
    W, FF, WD, WF = sizes
    enc = jnp.zeros((8, 128), F32)
    proj = jnp.zeros((8, 128), F32)
    row = 0
    for i, (name, r, c, n) in enumerate(part_layout(part, W, FF, WD)[h]):
        g = flat[row:row + n, :].astype(F32)
        stage[row:row + n, :] = g
        squares = jnp.sum((g * g).reshape(-1, 8, 128), axis=0)
        if name == "proj":
            proj += squares
        else:
            enc += squares
        copy = pltpu.make_async_copy(stage.at[pl.ds(row, n), :], named[name].at[pl.ds(r, n), pl.ds(c, 128)], sem.at[i])
        copy.start()
        started.append(copy)
        row += n
    return enc, proj


def unpack_own_kernel(idx_ref, own0, own1, own2, down, up, qkv, out, proj, sq_ref, flat0, flat1, flat2, stage0, stage1, stage2, fetch_sem, sem, *, sizes):
    unpack_halves(idx_ref, (own0, own1, own2), (down, up, qkv, out, proj), sq_ref, (flat0, flat1, flat2), (stage0, stage1, stage2), fetch_sem, sem, False, sizes)


def unpack_halves(idx_ref, arrays, outs, sq_ref, flats, stages, fetch_sem, sem, other, sizes, between=None):
    named = dict(zip(("down", "up", "qkv", "out", "proj"), outs))
    quarter = PIECES // 2
    for i, (array, flat) in enumerate(zip(arrays, flats)):
        size = flat.shape[0] // quarter
        low = idx_ref[1 + i] & (quarter - 1)
        for p in range(quarter):
            to = flat.at[pl.ds(pl.multiple_of((p ^ low) * size, 16), size), :]
            pltpu.make_async_copy(array.at[pl.ds(p * size, size), :], to, fetch_sem.at[i]).start()
    sq_ref[...] = jnp.zeros_like(sq_ref)
    for part, (flat, stage) in enumerate(zip(flats, stages)):
        pltpu.make_async_copy(flat, flat, fetch_sem.at[part]).wait()
        top = idx_ref[1 + part] // quarter
        if other:
            top = 1 - top
        for h in range(2):
            @pl.when(top == h)
            def _(part=part, h=h, flat=flat, stage=stage):
                started = []
                enc, proj = unpack_half(part, h, flat, named, stage, sem.at[part], started, sizes)
                sq_ref[:8, :] = sq_ref[:8, :] + enc
                sq_ref[8:, :] = sq_ref[8:, :] + proj
    if between is not None:
        between()
    for part, stage in enumerate(stages):
        top = idx_ref[1 + part] // quarter
        if other:
            top = 1 - top
        W, FF, WD, WF = sizes
        for h in range(2):
            @pl.when(top == h)
            def _(part=part, h=h, stage=stage):
                row = 0
                for i, (name, r, c, n) in enumerate(part_layout(part, W, FF, WD)[h]):
                    pltpu.make_async_copy(stage.at[pl.ds(row, n), :], named[name].at[pl.ds(r, n), pl.ds(c, 128)], sem.at[part, i]).wait()
                    row += n


def unpack_scratch(sizes):
    W, FF, WD, WF = sizes
    rows = [part_rows(i, *sizes) // 2 for i in range(3)]
    return ([pltpu.VMEM((r, 128), BF) for r in rows] + [pltpu.VMEM((max(sum(b[3] for b in h) for h in part_layout(i, W, FF, WD)), 128), F32) for i in range(3)]
            + [pltpu.SemaphoreType.DMA((3,)), pltpu.SemaphoreType.DMA((3, 16))])


def big_shapes(sizes):
    W, FF, WD, WF = sizes
    S = lambda *shape: jax.ShapeDtypeStruct(shape, F32)
    half = W // 2
    return [S(FF, half), S(W, FF // 2), S(W, 3 * half), S(W, half), S(WD // 2, W)]


def unpack_own_call(idx, own, *sizes):
    vm, hbm = pl.BlockSpec(memory_space=pltpu.VMEM), pl.BlockSpec(memory_space=pl.ANY)
    return pl.pallas_call(
        functools.partial(unpack_own_kernel, sizes=sizes),
        in_specs=[pl.BlockSpec(memory_space=pltpu.SMEM)] + [hbm] * 3,
        out_specs=[hbm] * 5 + [vm],
        out_shape=big_shapes(sizes) + [jax.ShapeDtypeStruct((16, 128), F32)],
        scratch_shapes=unpack_scratch(sizes),
        compiler_params=pltpu.CompilerParams(vmem_limit_bytes=18 * 1024 * 1024),
        cost_estimate=pl.CostEstimate(flops=10_000_000, bytes_accessed=12_000_000, transcendentals=0),
        name="unpack_own_half",
    )(idx, *own)


def unpack_kernel(idx_ref, came0, came1, came2, own0, own1, own2, sq_in, b0, b1, b2, b3, b4, down, up, qkv, out, proj, vec_ref, bias_ref, sq_ref,
                  d0, d1, d2, d3, d4, d5, d6, d7, flat0, flat1, flat2, stage0, stage1, stage2, fetch_sem, sem, rest0, rest1, rest2, pack, rest_sem, *, sizes, slots, patches):
    W, FF, WD, WF = sizes
    quarter = PIECES // 2
    rests, flats = (rest0, rest1, rest2), (flat0, flat1, flat2)
    copies = []
    for i, (own, rest) in enumerate(zip((own0, own1, own2), rests)):
        size = rest.shape[0]
        p = (quarter - 1) ^ (idx_ref[1 + i] & (quarter - 1))
        copies.append(pltpu.make_async_copy(own.at[pl.ds(pl.multiple_of(p * size, 16), size), :], rest, rest_sem.at[i]))
        copies[-1].start()

    def between():
        for c in copies:
            c.wait()
        for part, (rest, flat) in enumerate(zip(rests, flats)):
            first, low, high = dec_share(part, *sizes)
            top = idx_ref[1 + part] // quarter
            for h in range(2):
                @pl.when(top == h)
                def _(part=part, h=h, rest=rest, flat=flat, first=first, low=low, high=high):
                    zero, one = (rest, flat) if h == 0 else (flat, rest)
                    pack[first:first + low, :] = zero[zero.shape[0] - low:, :]
                    pack[first + low:first + low + high, :] = one[one.shape[0] - high:, :]
                    if part == 2:
                        at = one.shape[0] - high - 128
                        enc = jnp.zeros((8, 128), F32)
                        for b in range(W // 2 // 128):
                            g = one[at + 8 * b:at + 8 * b + 8, :].astype(F32)
                            enc += g * g
                            vec_ref[:, b * 128:b * 128 + 128] = g
                        at += 8 * (W // 2 // 128)
                        g = one[at:at + 16, :].astype(F32)[:FF // 2 // 128]
                        bias_ref[...] = g
                        enc += jnp.concatenate([jnp.sum(g * g, axis=0, keepdims=True), jnp.zeros((7, 128), F32)], axis=0)
                        sq_ref[:8, :] = sq_ref[:8, :] + enc
        dec = finish(lambda at, n: pack[at:at + n, :], d0, d1, d2, d3, d4, d5, d6, d7, W=WD, FF=WF, slots=slots, patches=patches)
        sq_ref[8:, :] = sq_ref[8:, :] + dec
        sq_ref[...] = sq_ref[...] + sq_in[...]

    unpack_halves(idx_ref, (came0, came1, came2), (down, up, qkv, out, proj), sq_ref, flats, (stage0, stage1, stage2), fetch_sem, sem, True, sizes, between)


def unpack_call(idx, own, came, big, squares, slots, patches, *sizes):
    W, FF, WD, WF = sizes
    vm, hbm = pl.BlockSpec(memory_space=pltpu.VMEM), pl.BlockSpec(memory_space=pl.ANY)
    S = lambda *shape: jax.ShapeDtypeStruct(shape, F32)
    wh = WD // 2
    dec = [S(3 * wh, WD), S(wh, WD), S(WD, WF // 2), S(wh, WF), S(9, wh), S(8, WF // 2), S(slots, wh), S(patches, wh)]
    return pl.pallas_call(
        functools.partial(unpack_kernel, sizes=sizes, slots=slots, patches=patches),
        in_specs=[pl.BlockSpec(memory_space=pltpu.SMEM)] + [hbm] * 6 + [vm] + [hbm] * 5,
        out_specs=[hbm] * 5 + [vm] * 11,
        out_shape=big_shapes(sizes) + [S(8, W // 2), S(FF // 2 // 128, 128), S(16, 128)] + dec,
        input_output_aliases={8 + i: i for i in range(5)},
        scratch_shapes=unpack_scratch(sizes) + [pltpu.VMEM((part_rows(i, *sizes) // PIECES, 128), BF) for i in range(3)]
        + [pltpu.VMEM((dec_blocks(WD, WF)["all"], 128), BF), pltpu.SemaphoreType.DMA((3,))],
        compiler_params=pltpu.CompilerParams(vmem_limit_bytes=28 * 1024 * 1024),
        cost_estimate=pl.CostEstimate(flops=10_000_000, bytes_accessed=15_000_000, transcendentals=0),
        name="unpack_other_half",
    )(idx, *came, *own, squares, *big)


def pair_kernel(sec_ref, dec_mine, dec_came, tok_mine, tok_came, dec_ref, tok_ref):
    sec = sec_ref[0]
    for ref, mine, came in ((dec_ref, dec_mine, dec_came), (tok_ref, tok_mine, tok_came)):
        ref[sec] = mine[...]
        ref[1 - sec] = came[...]


def pair_call(sec, *arrays):
    vm = pl.BlockSpec(memory_space=pltpu.VMEM)
    return pl.pallas_call(
        pair_kernel,
        in_specs=[pl.BlockSpec(memory_space=pltpu.SMEM)] + [vm] * 4,
        out_specs=[vm] * 2,
        out_shape=[jax.ShapeDtypeStruct((2, *arrays[i].shape), BF) for i in (0, 2)],
        compiler_params=pltpu.CompilerParams(vmem_limit_bytes=8 * 1024 * 1024),
        cost_estimate=pl.CostEstimate(flops=1000, bytes_accessed=1000, transcendentals=0),
        name="both_clips",
    )(sec, *arrays)


SIDE = 4


def coordinates(index):
    return (index // (SIDE * SIDE), index // SIDE % SIDE, index % SIDE)


def flip(place, axis, kind):
    place = list(place)
    place[axis] = place[axis] ^ 1 if kind == 0 else SIDE - 1 - place[axis]
    return tuple(place)


def swap(value, axes, far):
    pairs = []
    for core in range(2):
        for index in range(SIDE**3):
            place = coordinates(index)
            for axis in axes:
                place = flip(place, axis, core ^ far)
            target = (place[0] * SIDE + place[1]) * SIDE + place[2]
            pairs.append((core * SIDE**3 + index, core * SIDE**3 + target))
    return lax.ppermute(value, ("section", "dp"), pairs)


def add(left, right):
    return (left.astype(jnp.float32) + right.astype(jnp.float32)).astype(jnp.bfloat16)


def piece_numbers(place, core):
    near = [1 * ((p == 1) | (p == 2)) for p in place]
    far = [1 * (p >= 2) for p in place]
    first = [(1 - core) * a + core * b for a, b in zip(near, far)]
    return [first[i] * 4 + first[(i + 1) % 3] * 2 + first[(i + 2) % 3] for i in range(3)]


def halve(v, axis, far):
    half = v.shape[0] // 2
    return add(v[:half], swap(v[half:], (axis,), far))


def sum_over_chips(pairs):
    own, came = [], []
    for i, (give, keep) in enumerate(pairs):
        v = add(keep, swap(give, (i,), 0))
        for step in (1, 2):
            v = halve(v, (i + step) % 3, 0)
        for step in range(3):
            v = add(v, swap(v, ((i + step) % 3,), 1))
        for step in (2, 1):
            v = jnp.concatenate([v, swap(v, ((i + step) % 3,), 0)])
        own.append(v)
        came.append(swap(v, (i,), 0))
    return (own, came)


def from_partner(value):
    return lax.ppermute(value, "section", [(0, 1), (1, 0)])


def shards(
    tokens,
    frames,
    visible,
    out_grad,
    enc_vectors,
    enc_qkv,
    enc_out,
    enc_up,
    enc_up_bias,
    enc_down,
    proj_weight,
    dec_vectors,
    dec_qkv,
    dec_out,
    dec_up,
    dec_up_bias,
    dec_down,
    time_pos,
    space_pos,
):
    enc_width, enc_hidden = enc_up.shape
    dec_width, dec_hidden = dec_up.shape
    slot_count = time_pos.shape[0]
    patch_count = space_pos.shape[0]
    seen_count = visible.shape[1]
    section = lax.axis_index("section").astype(jnp.int32)
    core = section.reshape(1)
    sizes = (enc_width, enc_hidden, dec_width, dec_hidden)
    acts, qkv, mid, slopes, projected = enc_fwd_call(
        core, frames, seen_count, tokens, enc_vectors, enc_up_bias, enc_qkv, enc_out, enc_up, enc_down, proj_weight
    )
    acts_came = from_partner(acts)
    (decoded_mine, decoded_other), grad_projected, (dec_mine, dec_other) = dec_block_call(
        core,
        frames,
        visible,
        projected,
        time_pos,
        space_pos,
        dec_vectors,
        dec_qkv,
        dec_out,
        dec_up,
        dec_up_bias,
        dec_down,
        out_grad,
        TQ=384,
        TA=640,
    )
    dec_came = from_partner(dec_other)
    dy_mine, dy_other, token_mine, token_other = enc_bwd_call(
        core, frames, seen_count, grad_projected, tokens, enc_vectors, qkv, mid, slopes, proj_weight, enc_down, enc_up, enc_out, enc_qkv
    )
    dy_came = from_partner(dy_other)
    places = jnp.stack([section, *piece_numbers(coordinates(lax.axis_index("dp")), section)]).astype(jnp.int32)
    pieces = weight_grad_call(places, acts, acts_came, dy_mine, dy_came, dec_mine, dec_came, *sizes)
    own, came = sum_over_chips(list(zip(pieces[:3], pieces[3:])))
    decoded_came = from_partner(decoded_other)
    token_came = from_partner(token_other)
    decoded, token_grad = pair_call(core, decoded_mine, decoded_came, token_mine, token_came)
    *big, squares = unpack_own_call(places, own, *sizes)
    (
        g_enc_down, g_enc_up, g_enc_qkv, g_enc_out, g_proj, g_vectors, g_enc_bias, squares,
        g_dec_qkv, g_dec_out, g_dec_up, g_dec_down, g_dec_vectors, g_dec_bias, g_time, g_space,
    ) = unpack_call(places, own, came, big, squares, slot_count, patch_count, *sizes)
    enc_squares, dec_squares = squares[:8], squares[8:]
    give = jnp.where(section == 0, dec_squares, enc_squares)
    keep = jnp.where(section == 0, enc_squares, dec_squares)
    norms = jnp.sum(keep + from_partner(give)).reshape(1)
    return (
        decoded.transpose(0, 2, 1),
        token_grad,
        g_vectors,
        g_enc_qkv,
        g_enc_out,
        g_enc_up,
        g_enc_bias.reshape(-1),
        g_enc_down,
        g_proj.T,
        g_dec_vectors,
        g_dec_qkv.T,
        g_dec_out.T,
        g_dec_up,
        g_dec_bias[0],
        g_dec_down.T,
        g_time,
        g_space,
        norms,
    )


from jax.sharding import PartitionSpec as P


def solution(mesh):
    placed = (
        P("dp", None, None),
        P("dp"),
        P("dp", None),
        P("dp", None, None),
        P(),
        P(),
        P(),
        P(),
        P(),
        P(),
        P(),
        P(),
        P(),
        P(),
        P(),
        P(),
        P(),
        P(),
        P(),
    )
    return jax.shard_map(
        shards,
        mesh=mesh,
        in_specs=placed,
        out_specs=(
            P("dp", None, "section"),
            P("dp", None, "section"),
            P(None, "section"),
            P(None, "section"),
            P(None, "section"),
            P(None, "section"),
            P("section"),
            P(None, "section"),
            P(None, "section"),
            P(None, "section"),
            P(None, "section"),
            P(None, "section"),
            P(None, "section"),
            P("section"),
            P(None, "section"),
            P(None, "section"),
            P(None, "section"),
            P("section"),
        ),
        check_vma=False,
    )
```
